32 devices in a mesh: ctx: 8 (over z, y), fsdp: 4 (over x, core).
Axes of the slice: x: 2, y: 2, z: 4, core: 2. Of those that a mesh axis runs over, the one named last changes fastest.
Arguments:
- tokens: bfloat16 [4, 2048, 1024], P('fsdp', 'ctx'), may hold values from -6 to 6
- encoded: bfloat16 [4, 512, 1024], P('fsdp', 'ctx'), may hold values from -6 to 6
- grad_out: bfloat16 [4, 2048, 1024], P('fsdp', 'ctx'), may hold values from -6 to 6
- doc_lengths: int32 [4, 8], P('fsdp'), may hold values from 1 to 1024, 2048 in all within a row
- src_lengths: int32 [4, 8], P('fsdp'), may hold values from 1 to 256, 512 in all within a row
- norm_gain: float32 [3, 1024], replicated, may hold values from 0.5 to 1.5
- norm_bias: float32 [3, 1024], replicated, may hold values from -0.6 to 0.6
- w_qkv: bfloat16 [1024, 3072], P('fsdp'), may hold values from -0.1875 to 0.1875
- self_bias: float32 [3, 1024], replicated, may hold values from -0.6 to 0.6
- w_self_out: bfloat16 [1024, 1024], P('fsdp'), may hold values from -0.75 to 0.75
- w_cross_q: bfloat16 [1024, 1024], P('fsdp'), may hold values from -0.1875 to 0.1875
- w_cross_kv: bfloat16 [1024, 2048], P('fsdp'), may hold values from -0.1875 to 0.1875
- cross_bias: float32 [3, 1024], replicated, may hold values from -0.6 to 0.6
- w_cross_out: bfloat16 [1024, 1024], P('fsdp'), may hold values from -0.75 to 0.75
- w_up: bfloat16 [1024, 8192], P('fsdp'), may hold values from -0.1875 to 0.1875
- up_bias: float32 [8192], replicated, may hold values from -0.6 to 0.6
- w_down: bfloat16 [8192, 1024], P('fsdp'), may hold values from -0.0625 to 0.0625
- down_bias: float32 [1024], replicated, may hold values from -1.2 to 1.2
Outputs:
- layer_out: bfloat16 [4, 2048, 1024], P('fsdp', 'ctx')
- grad_tokens: float32 [4, 2048, 1024], P('fsdp', 'ctx')
- grad_encoded: float32 [4, 512, 1024], P('fsdp', 'ctx')
- grad_norm_gain: float32 [3, 1024], replicated
- grad_norm_bias: float32 [3, 1024], replicated
- grad_w_qkv: float32 [1024, 3072], P('fsdp', 'ctx')
- grad_self_bias: float32 [3, 1024], replicated
- grad_w_self_out: float32 [1024, 1024], P('fsdp', 'ctx')
- grad_w_cross_q: float32 [1024, 1024], P('fsdp', 'ctx')
- grad_w_cross_kv: float32 [1024, 2048], P('fsdp', 'ctx')
- grad_cross_bias: float32 [3, 1024], replicated
- grad_w_cross_out: float32 [1024, 1024], P('fsdp', 'ctx')
- grad_w_up: float32 [1024, 8192], P('fsdp', 'ctx')
- grad_up_bias: float32 [8192], replicated
- grad_w_down: float32 [8192, 1024], P('fsdp', 'ctx')
- grad_down_bias: float32 [1024], replicated
The draws below stay inside these ranges and needn't reach their ends.
Inputs may be any that keep to these rules, and one draw needn't show every extreme that they name: `doc_lengths`: each row of target document lengths sums to 2048, and its longest is exactly 1024. `src_lengths`: each row of source span lengths sums to 512, and its longest is exactly 256.
All inputs are finite; a program needn't handle non-finite values.
Results may differ from the reference program's by a relative error of at most 0.024.
Values may be sent and summed in bfloat16 or wider, within the bound.
No kernel may reach another device: no remote copies, remote signals or barrier semaphores. Data moves between devices by JAX's collectives and lax.ppermute only.
A program may use at most 512 MiB of HBM per device.

```python
import math
import jax
import jax.numpy as jnp
import numpy as np
from jax import lax

D = 1024
HEADS = 16
HEAD_DIM = 64
FF = 8192
TOK_DEV = 256
DOCS = 8
KBLOCK = 512
MB = 4
STREAM = 2048
SRC_STREAM = 512
MAX_DOC = 1024
SRC_MAX = 256
N_CTX = 8


def block_scale(stream_key, extent, cuts, low, high):
    factor_of, own = 1.0, jax.random.fold_in(stream_key, 6)
    for position, blocks in cuts:
        draws = jnp.exp(jax.random.uniform(jax.random.fold_in(own, position), (blocks,), jnp.float32, low / len(cuts), high / len(cuts)))
        factor_of = factor_of * jnp.repeat(draws, extent[position] // blocks).reshape([-1 if axis == position else 1 for axis in range(len(extent))])
    return factor_of


def profile(amount, total, bound, slope):
    weights = [(1 << 20) // math.isqrt(standing ** slope) + 1 for standing in range(2, amount + 1)]
    rest, given = total - bound - (amount - 1), [1] * (amount - 1)
    while rest > 0:
        free = [i for i in range(amount - 1) if given[i] < bound]
        whole, budget = sum([weights[i] for i in free]), rest
        for i in free:
            more = min(bound - given[i], max(1, budget * weights[i] // whole), rest)
            given[i] = given[i] + more
            rest = rest - more
    return np.array([bound] + given)


def uneven_parts(rng, number_of, total, bound, slope):
    if number_of == 2:
        one = jax.random.randint(rng, (), max(1, total - bound), min(bound, total - 1) + 1)
        return jnp.stack([one, total - one])
    sizes = jnp.asarray(profile(number_of, total, bound, slope), jnp.int32)
    twos = (number_of - 1) // 2
    donor, sink = sizes[1:1 + 2 * twos:2], sizes[2:2 + 2 * twos:2]
    margin = jnp.minimum(donor - 1, bound - sink)
    moved = jax.random.randint(jax.random.fold_in(rng, 1), (twos,), 0, 1 << 20) % (margin + 1)
    sizes = sizes.at[1:1 + 2 * twos:2].set(donor - moved).at[2:2 + 2 * twos:2].set(sink + moved)
    return sizes[jax.random.permutation(jax.random.fold_in(rng, 2), number_of)]


def scatter_about(stream_key, dims, scale, bound, cuts=(), kind=jnp.bfloat16):
    loudness = block_scale(stream_key, dims, cuts, -0.22, 0.18) if cuts else 1.0
    values = jax.random.normal(stream_key, dims, jnp.float32) * scale * loudness
    return jnp.minimum(jnp.maximum(values, -bound), bound).astype(kind)


def setup_inputs(seed: int = 0) -> dict:
    arg_keys = jax.random.split(jax.random.key(seed), 19)
    tokens = scatter_about(arg_keys[0], (MB, STREAM, D), 1.0, 6.0, ((0, 4), (1, 8)))
    encoded = scatter_about(arg_keys[1], (MB, SRC_STREAM, D), 1.0, 6.0, ((0, 4), (1, 8)))
    grad_out = scatter_about(arg_keys[2], (MB, STREAM, D), 1.0, 6.0, ((0, 4), (1, 8)))
    doc_lengths = jax.vmap(lambda own: uneven_parts(own, DOCS, STREAM, MAX_DOC, 2))(jax.random.split(arg_keys[3], MB)).reshape((MB, DOCS)).astype(jnp.int32)
    src_lengths = jax.vmap(lambda own: uneven_parts(own, DOCS, SRC_STREAM, SRC_MAX, 2))(jax.random.split(arg_keys[4], MB)).reshape((MB, DOCS)).astype(jnp.int32)
    norm_gain = jnp.clip(1.0 + 0.1 * jax.random.normal(arg_keys[5], (3, D), jnp.float32), 0.5, 1.5)
    norm_bias = scatter_about(arg_keys[6], (3, D), 0.1, 0.6, (), jnp.float32)
    w_qkv = scatter_about(arg_keys[7], (D, 3 * D), D ** -0.5, 0.1875, ((0, 4),))
    self_bias = scatter_about(arg_keys[8], (3, D), 0.1, 0.6, (), jnp.float32)
    w_self_out = scatter_about(arg_keys[9], (D, D), HEAD_DIM ** -0.5, 0.75, ((0, 4),))
    w_cross_q = scatter_about(arg_keys[10], (D, D), D ** -0.5, 0.1875, ((0, 4),))
    w_cross_kv = scatter_about(arg_keys[11], (D, 2 * D), D ** -0.5, 0.1875, ((0, 4),))
    cross_bias = scatter_about(arg_keys[12], (3, D), 0.1, 0.6, (), jnp.float32)
    w_cross_out = scatter_about(arg_keys[13], (D, D), HEAD_DIM ** -0.5, 0.75, ((0, 4),))
    w_up = scatter_about(arg_keys[14], (D, FF), D ** -0.5, 0.1875, ((0, 4),))
    up_bias = scatter_about(arg_keys[15], (FF,), 0.1, 0.6, (), jnp.float32)
    w_down = scatter_about(arg_keys[16], (FF, D), FF ** -0.5, 0.0625, ((0, 4),))
    down_bias = scatter_about(arg_keys[17], (D,), 0.2, 1.2, (), jnp.float32)
    return {"tokens": tokens, "encoded": encoded, "grad_out": grad_out, "doc_lengths": doc_lengths, "src_lengths": src_lengths, "norm_gain": norm_gain, "norm_bias": norm_bias, "w_qkv": w_qkv, "self_bias": self_bias, "w_self_out": w_self_out, "w_cross_q": w_cross_q, "w_cross_kv": w_cross_kv, "cross_bias": cross_bias, "w_cross_out": w_cross_out, "w_up": w_up, "up_bias": up_bias, "w_down": w_down, "down_bias": down_bias}


@jax.custom_vjp
def low(v):
    return lax.optimization_barrier(v.astype(jnp.bfloat16)).astype(jnp.float32)

@jax.custom_vjp
def low_back(v):
    return v

def low_keep(v):
    return (low(v), None)

def low_pass(kept, grad):
    return (grad,)

def back_keep(v):
    return (v, None)

def back_low(kept, grad):
    return (low(grad),)
low.defvjp(low_keep, low_pass)
low_back.defvjp(back_keep, back_low)
EPS = 1e-05
NEG = -1e+30

def stream_position(rows, tok_dev, ctx_count):
    half = tok_dev // 2
    device = (rows // tok_dev).astype(jnp.int32)
    within = (rows % tok_dev).astype(jnp.int32)
    early = device * half + within
    late = (2 * ctx_count - 1 - device) * half + (within - half)
    return jnp.where(within < half, early, late).astype(jnp.int32)

def layer_norm(inputs, gain_row, shift_row):
    center = inputs - lax.optimization_barrier(jnp.mean(inputs, axis=1, keepdims=True))
    inverse = lax.rsqrt(lax.optimization_barrier(jnp.mean(center * center, axis=1, keepdims=True)) + EPS)
    return center * inverse * gain_row + shift_row

def matmul(left, right):
    return jnp.dot(left, right, precision=lax.Precision.HIGHEST, preferred_element_type=jnp.float32)

def doc_index(doc_starts, positions):
    flags = (doc_starts[None, :] <= positions[:, None]).astype(jnp.int32)
    counted = lax.optimization_barrier(jnp.sum(flags, axis=1, dtype=jnp.int32))
    return (counted - 1).astype(jnp.int32)

def pick_doc(lookup, doc_ids):
    onehot = doc_ids[:, None] == jnp.arange(lookup.shape[0], dtype=jnp.int32)[None, :]
    picked = jnp.where(onehot, lookup[None, :].astype(jnp.int32), jnp.zeros((), jnp.int32))
    return lax.optimization_barrier(jnp.sum(picked, axis=1, dtype=jnp.int32)).astype(jnp.int32)

def split_heads(matrix):
    return matrix.reshape(matrix.shape[0], HEADS, matrix.shape[1] // HEADS)

def attention(queries, key_heads, value_heads, allowed_fn):

    def one_block(block_start):
        query_block = lax.dynamic_slice_in_dim(queries, block_start, KBLOCK, 0)
        raw_scores = jnp.einsum('qhd,khd->hqk', query_block, key_heads, precision=lax.Precision.HIGHEST)
        raw_scores = low_back(raw_scores)
        allowed = allowed_fn(block_start)[None]
        row_peak = lax.optimization_barrier(jnp.max(jnp.where(allowed, raw_scores, NEG), axis=2, keepdims=True))
        shifted = jnp.where(allowed, raw_scores - row_peak, 0.0)
        exp_terms = jnp.where(allowed, jnp.exp(shifted), 0.0)
        prob_low = low(exp_terms / lax.optimization_barrier(jnp.sum(exp_terms, axis=2, keepdims=True)))
        return jnp.einsum('hqk,khd->qhd', prob_low, value_heads, precision=lax.Precision.HIGHEST)
    starts = jnp.arange(queries.shape[0] // KBLOCK, dtype=jnp.int32) * KBLOCK
    blocks = lax.map(jax.checkpoint(one_block), starts)
    return blocks.reshape(queries.shape[0], queries.shape[1] * queries.shape[2])

def decoder_layer(params, self_allowed, cross_allowed, tok_f32, enc_f32):
    gain_all, shift_all, w_qkv, self_bias, w_self_out, w_cross_q, w_cross_kv, cross_bias, w_cross_out, w_up, up_bias, w_down, down_bias = params
    width = tok_f32.shape[1]
    q_scale = 1.0 / math.sqrt(HEAD_DIM)
    act_one = low(layer_norm(tok_f32, gain_all[0], shift_all[0]))
    projected = matmul(act_one, w_qkv)
    q_self = low(low_back((projected[:, :width] + self_bias[0]) * q_scale))
    k_self = low(low_back(projected[:, width:2 * width]))
    v_self = low(low_back(projected[:, 2 * width:] + self_bias[1]))
    att_self = attention(split_heads(q_self), split_heads(k_self), split_heads(v_self), self_allowed)
    att_self = low(low_back(att_self))
    hidden_one = tok_f32 + low_back(matmul(att_self, w_self_out) + self_bias[2])
    act_two = low(layer_norm(hidden_one, gain_all[1], shift_all[1]))
    q_cross = low(low_back((matmul(act_two, w_cross_q) + cross_bias[0]) * q_scale))
    src_proj = matmul(enc_f32, w_cross_kv)
    k_cross = low(low_back(src_proj[:, :width]))
    v_cross = low(low_back(src_proj[:, width:] + cross_bias[1]))
    att_cross = attention(split_heads(q_cross), split_heads(k_cross), split_heads(v_cross), cross_allowed)
    att_cross = low(low_back(att_cross))
    hidden_two = hidden_one + low_back(matmul(att_cross, w_cross_out) + cross_bias[2])
    act_three = low(layer_norm(hidden_two, gain_all[2], shift_all[2]))
    pre_act = low_back(matmul(act_three, w_up) + up_bias)
    gelu_low = low(jax.nn.gelu(pre_act, approximate=True))
    return hidden_two + low_back(matmul(gelu_low, w_down) + down_bias)

def reference(tokens, encoded, grad_out, doc_lengths, src_lengths, norm_gain, norm_bias, w_qkv, self_bias, w_self_out, w_cross_q, w_cross_kv, cross_bias, w_cross_out, w_up, up_bias, w_down, down_bias):
    params = (norm_gain, norm_bias, w_qkv.astype(jnp.float32), self_bias, w_self_out.astype(jnp.float32), w_cross_q.astype(jnp.float32), w_cross_kv.astype(jnp.float32), cross_bias, w_cross_out.astype(jnp.float32), w_up.astype(jnp.float32), up_bias, w_down.astype(jnp.float32), down_bias)
    totals = jax.tree.map(jnp.zeros_like, params)
    layer_list, grad_tok_list, grad_enc_list = ([], [], [])
    tok_pos = stream_position(jnp.arange(STREAM, dtype=jnp.int32), TOK_DEV, N_CTX)
    src_pos = jnp.arange(SRC_STREAM, dtype=jnp.int32)
    for micro_batch in range(MB):
        lengths_row = doc_lengths[micro_batch].astype(jnp.int32)
        doc_starts = (jnp.cumsum(lengths_row, dtype=jnp.int32) - lengths_row).astype(jnp.int32)
        tok_doc = doc_index(doc_starts, tok_pos)
        src_row = src_lengths[micro_batch].astype(jnp.int32)
        src_ends = jnp.cumsum(src_row, dtype=jnp.int32).astype(jnp.int32)
        src_starts = (src_ends - src_row).astype(jnp.int32)
        span_low = pick_doc(src_starts, tok_doc)
        span_high = pick_doc(src_ends, tok_doc)

        def self_allowed(block_start, tok_doc=tok_doc):
            query_pos = lax.dynamic_slice_in_dim(tok_pos, block_start, KBLOCK, 0)
            query_doc = lax.dynamic_slice_in_dim(tok_doc, block_start, KBLOCK, 0)
            return (tok_pos[None, :] <= query_pos[:, None]) & (tok_doc[None, :] == query_doc[:, None])

        def cross_allowed(block_start, span_low=span_low, span_high=span_high):
            low_edge = lax.dynamic_slice_in_dim(span_low, block_start, KBLOCK, 0)
            high_edge = lax.dynamic_slice_in_dim(span_high, block_start, KBLOCK, 0)
            return (src_pos[None, :] >= low_edge[:, None]) & (src_pos[None, :] < high_edge[:, None])

        def forward(tok_f32, enc_f32, param_set, self_allowed=self_allowed, cross_allowed=cross_allowed):
            return decoder_layer(param_set, self_allowed, cross_allowed, tok_f32, enc_f32)
        layer_value, pull_back = jax.vjp(forward, tokens[micro_batch].astype(jnp.float32), encoded[micro_batch].astype(jnp.float32), params)
        grad_tok, grad_enc, grad_params = pull_back(grad_out[micro_batch].astype(jnp.float32))
        totals = jax.tree.map(lambda left, right: left + right, totals, grad_params)
        layer_list.append(layer_value.astype(jnp.bfloat16))
        grad_tok_list.append(grad_tok)
        grad_enc_list.append(grad_enc)
    return (jnp.stack(layer_list), jnp.stack(grad_tok_list), jnp.stack(grad_enc_list), totals[0], totals[1], totals[2], totals[3], totals[4], totals[5], totals[6], totals[7], totals[8], totals[9], totals[10], totals[11], totals[12])
```

```python
import functools
import math

import jax
import jax.numpy as jnp
from jax import lax
from jax.experimental import pallas as pl
from jax.experimental.pallas import tpu as pltpu
from jax.sharding import Mesh
from jax.sharding import PartitionSpec as P

HEADS = 16
HEAD_DIM = 64
KBLOCK = 512


EPS = 1e-05
NEG = -1e30
GELU_C = 0.7978845608028654
GELU_A = 0.044715
CONTRACT_ROWS = (((0,), (0,)), ((), ()))
CONTRACT_COLS = (((1,), (1,)), ((), ()))


def shortened(shard):
    return jax.tree.map(lambda a: a.astype(jnp.bfloat16) if a.dtype == jnp.float32 else a, shard)


def gelu_value(pre):
    return 0.5 * pre * (1.0 + jnp.tanh(GELU_C * (pre + GELU_A * pre * pre * pre)))


def gelu_slope(pre):
    tangent = jnp.tanh(GELU_C * (pre + GELU_A * pre * pre * pre))
    return 0.5 * (1.0 + tangent) + 0.5 * pre * (1.0 - tangent * tangent) * GELU_C * (
        1.0 + 3.0 * GELU_A * pre * pre
    )


def stream_position(rows, tok_dev, ctx_count):
    half = tok_dev // 2
    device = rows // tok_dev
    within = rows % tok_dev
    early = device * half + within
    late = (2 * ctx_count - 1 - device) * half + (within - half)
    return jnp.where(within < half, early, late)


def layer_norm(inputs, gain_row, shift_row):
    center = inputs - jnp.mean(inputs, axis=1, keepdims=True)
    inverse = lax.rsqrt(jnp.mean(center * center, axis=1, keepdims=True) + EPS)
    normed = center * inverse
    return (normed * gain_row + shift_row, normed, inverse)


def norm_back(upstream, normed, inverse, gain_row):
    scaled = upstream * gain_row
    mean_plain = jnp.mean(scaled, axis=1, keepdims=True)
    mean_normed = jnp.mean(scaled * normed, axis=1, keepdims=True)
    return (
        inverse * (scaled - mean_plain - normed * mean_normed),
        jnp.sum(upstream * normed, axis=0),
        jnp.sum(upstream, axis=0),
    )


def outer_rows(left, right):
    return lax.dot_general(left, right, CONTRACT_ROWS, preferred_element_type=jnp.float32)


def times_transpose(left, right):
    return lax.dot_general(left, right, CONTRACT_COLS, preferred_element_type=jnp.float32)


def plain_dot(left, right):
    return jnp.dot(left, right, preferred_element_type=jnp.float32)


def doc_index(doc_starts, positions):
    counted = jnp.sum((doc_starts[None, :] <= positions[:, None]).astype(jnp.int32), axis=1)
    return counted - 1


def pick_doc(lookup, doc_ids):
    onehot = doc_ids[:, None] == jnp.arange(lookup.shape[0], dtype=jnp.int32)[None, :]
    return jnp.sum(jnp.where(onehot, lookup[None, :], 0), axis=1)


def split_heads(matrix):
    return matrix.reshape(matrix.shape[0], HEADS, matrix.shape[1] // HEADS)


def split_pair(kv_piece):
    half_width = kv_piece.shape[1] // 2
    return (split_heads(kv_piece[:, :half_width]), split_heads(kv_piece[:, half_width:]))


def key_block(kv_whole, block_start):
    return split_pair(lax.dynamic_slice_in_dim(kv_whole, block_start, KBLOCK, 0))


def block_starts(kv_whole):
    return jnp.arange(kv_whole.shape[0] // KBLOCK, dtype=jnp.int32) * KBLOCK


def score_block(queries, key_heads):
    return jnp.einsum("qhd,khd->hqk", queries, key_heads, preferred_element_type=jnp.float32)


def attend(queries, kv_whole, allowed_fn):
    shape_stat = (queries.shape[1], queries.shape[0])

    def stat_step(state_pair, block_start):
        allowed = allowed_fn(block_start)

        def stat_compute_block(running):
            running_top, running_sum = running
            key_heads, value_heads = key_block(kv_whole, block_start)
            masked = jnp.where(allowed[None], score_block(queries, key_heads), NEG)
            new_top = jnp.maximum(running_top, jnp.max(masked, axis=2))
            exp_terms = jnp.where(allowed[None], jnp.exp(masked - new_top[:, :, None]), 0.0)
            return (
                new_top,
                running_sum * jnp.exp(running_top - new_top) + jnp.sum(exp_terms, axis=2),
            )

        return (
            lax.cond(jnp.any(allowed), stat_compute_block, lambda running: running, state_pair),
            None,
        )

    initial = (jnp.full(shape_stat, NEG, jnp.float32), jnp.zeros(shape_stat, jnp.float32))
    (final_top, final_sum), _ = lax.scan(stat_step, initial, block_starts(kv_whole))
    logsum = final_top + jnp.log(final_sum)

    def value_step(running, block_start):
        allowed = allowed_fn(block_start)

        def value_compute_block(partial_value):
            key_heads, value_heads = key_block(kv_whole, block_start)
            raw_scores = score_block(queries, key_heads)
            prob_low = jnp.where(
                allowed[None], jnp.exp(raw_scores - logsum[:, :, None]), 0.0
            ).astype(jnp.bfloat16)
            return partial_value + jnp.einsum(
                "hqk,khd->qhd", prob_low, value_heads, preferred_element_type=jnp.float32
            )

        return (
            lax.cond(
                jnp.any(allowed), value_compute_block, lambda partial_value: partial_value, running
            ),
            None,
        )

    attended, _ = lax.scan(
        value_step, jnp.zeros(queries.shape, jnp.float32), block_starts(kv_whole)
    )
    return (attended, logsum)


def score_grads(queries, key_heads, value_heads, grad_heads, logsum, row_delta, allowed):
    raw_scores = score_block(queries, key_heads)
    probs_full = jnp.where(allowed[None], jnp.exp(raw_scores - logsum[:, :, None]), 0.0)
    grad_probs = jnp.einsum(
        "qhd,khd->hqk", grad_heads, value_heads, preferred_element_type=jnp.float32
    )
    grad_scores = (probs_full * (grad_probs - row_delta[:, :, None])).astype(jnp.bfloat16)
    return (probs_full, grad_scores)


def key_terms(queries, key_heads, value_heads, grad_heads, logsum, row_delta, allowed):
    probs_full, grad_scores = score_grads(
        queries, key_heads, value_heads, grad_heads, logsum, row_delta, allowed
    )
    grad_keys = jnp.einsum("hqk,qhd->khd", grad_scores, queries, preferred_element_type=jnp.float32)
    grad_values = jnp.einsum(
        "hqk,qhd->khd",
        probs_full.astype(jnp.bfloat16),
        grad_heads,
        preferred_element_type=jnp.float32,
    )
    key_count = key_heads.shape[0]
    return jnp.concatenate(
        [grad_keys.reshape(key_count, -1), grad_values.reshape(key_count, -1)], axis=1
    )


def row_deltas(grad_heads, attended):
    return jnp.einsum("qhd,qhd->hq", grad_heads.astype(jnp.float32), attended)


def query_back(queries, kv_whole, allowed_fn, logsum, row_delta, grad_heads):

    def query_grad_step(partial_value, block_start):
        allowed = allowed_fn(block_start)

        def query_compute_block(running):
            key_heads, value_heads = key_block(kv_whole, block_start)
            probs_full, grad_scores = score_grads(
                queries, key_heads, value_heads, grad_heads, logsum, row_delta, allowed
            )
            return running + jnp.einsum(
                "hqk,khd->qhd", grad_scores, key_heads, preferred_element_type=jnp.float32
            )

        return (
            lax.cond(jnp.any(allowed), query_compute_block, lambda running: running, partial_value),
            None,
        )

    grad_query, _ = lax.scan(
        query_grad_step, jnp.zeros(queries.shape, jnp.float32), block_starts(kv_whole)
    )
    return grad_query


def attend_back(queries, kv_whole, allowed_fn, attended, logsum, grad_heads):
    row_delta = row_deltas(grad_heads, attended)

    def attend_grad_step(grad_query, block_start):
        allowed = allowed_fn(block_start)

        def attend_compute_block(partial_value):
            key_heads, value_heads = key_block(kv_whole, block_start)
            probs_full, grad_scores = score_grads(
                queries, key_heads, value_heads, grad_heads, logsum, row_delta, allowed
            )
            partial_value = partial_value + jnp.einsum(
                "hqk,khd->qhd", grad_scores, key_heads, preferred_element_type=jnp.float32
            )
            grad_keys = jnp.einsum(
                "hqk,qhd->khd", grad_scores, queries, preferred_element_type=jnp.float32
            )
            grad_values = jnp.einsum(
                "hqk,qhd->khd",
                probs_full.astype(jnp.bfloat16),
                grad_heads,
                preferred_element_type=jnp.float32,
            )
            return (
                partial_value,
                jnp.concatenate(
                    [grad_keys.reshape(KBLOCK, -1), grad_values.reshape(KBLOCK, -1)], axis=1
                ),
            )

        def attend_skip_block(partial_value):
            return (partial_value, jnp.zeros((KBLOCK, kv_whole.shape[1]), jnp.float32))

        return lax.cond(jnp.any(allowed), attend_compute_block, attend_skip_block, grad_query)

    grad_query, kv_terms = lax.scan(
        attend_grad_step, jnp.zeros(queries.shape, jnp.float32), block_starts(kv_whole)
    )
    return (grad_query, kv_terms.reshape(kv_whole.shape[0], kv_whole.shape[1]))


def owners_end(grads):
    columns = jax.tree.map(
        lambda part: part.astype(jnp.float32),
        lax.psum_scatter(shortened(grads), "ctx", scatter_dimension=1, tiled=True),
    )
    return jax.tree.map(
        lambda part: part.astype(jnp.float32),
        lax.psum_scatter(shortened(columns), "fsdp", scatter_dimension=0, tiled=True),
    )


def per_device(
    tokens,
    encoded,
    grad_out,
    doc_lengths,
    src_lengths,
    norm_gain,
    norm_bias,
    w_qkv,
    self_bias,
    w_self_out,
    w_cross_q,
    w_cross_kv,
    cross_bias,
    w_cross_out,
    w_up,
    up_bias,
    w_down,
    down_bias,
):
    q_scale = 1.0 / math.sqrt(HEAD_DIM)
    tok_rows = tokens.shape[1]
    features = tokens.shape[2]
    ctx_count = lax.axis_size("ctx")
    ctx_index = lax.axis_index("ctx")
    own_rows = ctx_index * tok_rows + jnp.arange(tok_rows, dtype=jnp.int32)
    tok_pos = stream_position(own_rows, tok_rows, ctx_count)
    lengths_row = doc_lengths[0]
    doc_starts = jnp.cumsum(lengths_row) - lengths_row
    tok_doc = doc_index(doc_starts, tok_pos)
    src_row = src_lengths[0]
    src_ends = jnp.cumsum(src_row)
    src_starts = src_ends - src_row
    span_low = pick_doc(src_starts, tok_doc)
    span_high = pick_doc(src_ends, tok_doc)

    def self_mask(key_rows):
        key_pos = stream_position(key_rows, tok_rows, ctx_count)
        key_doc = doc_index(doc_starts, key_pos)
        return (key_pos[None, :] <= tok_pos[:, None]) & (key_doc[None, :] == tok_doc[:, None])

    def self_allowed(block_start):
        return self_mask(block_start + jnp.arange(KBLOCK, dtype=jnp.int32))

    def cross_allowed(block_start):
        key_pos = block_start + jnp.arange(KBLOCK, dtype=jnp.int32)
        return (key_pos[None, :] >= span_low[:, None]) & (key_pos[None, :] < span_high[:, None])

    def gather_self():
        return (
            lax.all_gather(w_qkv, "fsdp", axis=0, tiled=True),
            lax.all_gather(w_self_out, "fsdp", axis=0, tiled=True),
        )

    def gather_cross():
        return (
            lax.all_gather(w_cross_q, "fsdp", axis=0, tiled=True),
            lax.all_gather(w_cross_kv, "fsdp", axis=0, tiled=True),
            lax.all_gather(w_cross_out, "fsdp", axis=0, tiled=True),
        )

    def gather_mlp():
        return (
            lax.all_gather(w_up, "fsdp", axis=0, tiled=True),
            lax.all_gather(w_down, "fsdp", axis=0, tiled=True),
        )

    tok_f32 = tokens[0].astype(jnp.float32)
    enc_low = encoded[0]
    ln_one, normed_one, inverse_one = layer_norm(tok_f32, norm_gain[0], norm_bias[0])
    act_one = ln_one.astype(jnp.bfloat16)
    full_qkv, full_self_out = gather_self()
    projected = plain_dot(act_one, full_qkv)
    q_self = ((projected[:, :features] + self_bias[0]) * q_scale).astype(jnp.bfloat16)
    kv_self = jnp.concatenate(
        [projected[:, features : 2 * features], projected[:, 2 * features :] + self_bias[1]], axis=1
    ).astype(jnp.bfloat16)
    kv_self_all = lax.all_gather(kv_self, "ctx", axis=0, tiled=True)
    self_heads = split_heads(q_self)
    att_self, lse_self = attend(self_heads, kv_self_all, self_allowed)
    att_self_low = att_self.reshape(tok_rows, features).astype(jnp.bfloat16)
    hidden_one = tok_f32 + plain_dot(att_self_low, full_self_out) + self_bias[2]
    ln_two, normed_two, inverse_two = layer_norm(hidden_one, norm_gain[1], norm_bias[1])
    act_two = ln_two.astype(jnp.bfloat16)
    full_cross_q, full_cross_kv, full_cross_out = gather_cross()
    q_cross = ((plain_dot(act_two, full_cross_q) + cross_bias[0]) * q_scale).astype(jnp.bfloat16)
    src_proj = plain_dot(enc_low, full_cross_kv)
    kv_cross = jnp.concatenate(
        [src_proj[:, :features], src_proj[:, features:] + cross_bias[1]], axis=1
    ).astype(jnp.bfloat16)
    kv_cross_all = lax.all_gather(kv_cross, "ctx", axis=0, tiled=True)
    cross_heads = split_heads(q_cross)
    att_cross, lse_cross = attend(cross_heads, kv_cross_all, cross_allowed)
    att_cross_low = att_cross.reshape(tok_rows, features).astype(jnp.bfloat16)
    hidden_two = hidden_one + plain_dot(att_cross_low, full_cross_out) + cross_bias[2]
    ln_three, normed_three, inverse_three = layer_norm(hidden_two, norm_gain[2], norm_bias[2])
    act_three = ln_three.astype(jnp.bfloat16)
    full_up, full_down = gather_mlp()
    pre_act = plain_dot(act_three, full_up) + up_bias
    gelu_low = gelu_value(pre_act).astype(jnp.bfloat16)
    layer_out = (hidden_two + plain_dot(gelu_low, full_down) + down_bias).astype(jnp.bfloat16)
    upstream = grad_out[0].astype(jnp.float32)
    down_grad_low = grad_out[0]
    full_up, full_down = gather_mlp()
    grad_w_down = outer_rows(gelu_low, down_grad_low)
    grad_down_bias = jnp.sum(upstream, axis=0)
    gelu_grad = times_transpose(down_grad_low, full_down)
    pre_grad_low = (gelu_grad * gelu_slope(pre_act)).astype(jnp.bfloat16)
    grad_w_up = outer_rows(act_three, pre_grad_low)
    grad_up_bias = jnp.sum(pre_grad_low.astype(jnp.float32), axis=0)
    norm_in_three, gain_grad_three, shift_grad_three = norm_back(
        times_transpose(pre_grad_low, full_up), normed_three, inverse_three, norm_gain[2]
    )
    grad_two = upstream + norm_in_three
    full_cross_q, full_cross_kv, full_cross_out = gather_cross()
    cross_grad_low = grad_two.astype(jnp.bfloat16)
    grad_w_cross_out = outer_rows(att_cross_low, cross_grad_low)
    cross_out_bias_grad = jnp.sum(cross_grad_low.astype(jnp.float32), axis=0)
    cross_att_grad = split_heads(
        times_transpose(cross_grad_low, full_cross_out).astype(jnp.bfloat16)
    )
    cross_q_grad, cross_kv_terms = attend_back(
        cross_heads, kv_cross_all, cross_allowed, att_cross, lse_cross, cross_att_grad
    )
    cross_kv_grad = lax.psum_scatter(
        cross_kv_terms.astype(jnp.bfloat16), "ctx", scatter_dimension=0, tiled=True
    )
    cross_q_low = (cross_q_grad.reshape(tok_rows, features) * q_scale).astype(jnp.bfloat16)
    grad_w_cross_q = outer_rows(act_two, cross_q_low)
    cross_q_bias_grad = jnp.sum(cross_q_low.astype(jnp.float32), axis=0)
    grad_w_cross_kv = outer_rows(enc_low, cross_kv_grad)
    cross_v_bias_grad = jnp.sum(cross_kv_grad[:, features:].astype(jnp.float32), axis=0)
    grad_encoded = times_transpose(cross_kv_grad, full_cross_kv)
    norm_in_two, gain_grad_two, shift_grad_two = norm_back(
        times_transpose(cross_q_low, full_cross_q), normed_two, inverse_two, norm_gain[1]
    )
    grad_one = grad_two + norm_in_two
    full_qkv, full_self_out = gather_self()
    self_grad_low = grad_one.astype(jnp.bfloat16)
    grad_w_self_out = outer_rows(att_self_low, self_grad_low)
    self_out_bias_grad = jnp.sum(self_grad_low.astype(jnp.float32), axis=0)
    self_att_flat = times_transpose(self_grad_low, full_self_out).astype(jnp.bfloat16)
    self_att_grad = split_heads(self_att_flat)
    self_delta = row_deltas(self_att_grad, att_self)
    self_q_grad = query_back(
        self_heads, kv_self_all, self_allowed, lse_self, self_delta, self_att_grad
    )

    def one_piece(sub_start):
        key_rows = sub_start + jnp.arange(tok_rows, dtype=jnp.int32)
        allowed = self_mask(key_rows)

        def one_compute_block(piece_start):
            key_heads, value_heads = split_pair(
                lax.dynamic_slice_in_dim(kv_self_all, piece_start, tok_rows, 0)
            )
            return key_terms(
                self_heads, key_heads, value_heads, self_att_grad, lse_self, self_delta, allowed
            )

        def one_skip_block(piece_start):
            return jnp.zeros((tok_rows, 2 * features), jnp.float32)

        return lax.cond(jnp.any(allowed), one_compute_block, one_skip_block, sub_start)

    piece_starts = (
        jnp.arange(tok_rows * lax.axis_size("ctx") // tok_rows, dtype=jnp.int32) * tok_rows
    )
    self_kv_grad = lax.psum_scatter(
        lax.map(one_piece, piece_starts)
        .reshape(tok_rows * lax.axis_size("ctx"), 2 * features)
        .astype(jnp.bfloat16),
        "ctx",
        scatter_dimension=0,
        tiled=True,
    )
    self_q_low = (self_q_grad.reshape(tok_rows, features) * q_scale).astype(jnp.bfloat16)
    proj_grad_low = jnp.concatenate([self_q_low, self_kv_grad], axis=1)
    grad_w_qkv = outer_rows(act_one, proj_grad_low)
    self_q_bias_grad = jnp.sum(self_q_low.astype(jnp.float32), axis=0)
    self_v_bias_grad = jnp.sum(self_kv_grad[:, features:].astype(jnp.float32), axis=0)
    norm_in_one, gain_grad_one, shift_grad_one = norm_back(
        times_transpose(proj_grad_low, full_qkv), normed_one, inverse_one, norm_gain[0]
    )
    grad_tokens = grad_one + norm_in_one
    owned = owners_end(
        (
            grad_w_qkv,
            grad_w_self_out,
            grad_w_cross_q,
            grad_w_cross_kv,
            grad_w_cross_out,
            grad_w_up,
            grad_w_down,
        )
    )
    gain_grads = jnp.stack([gain_grad_one, gain_grad_two, gain_grad_three])
    shift_grads = jnp.stack([shift_grad_one, shift_grad_two, shift_grad_three])
    self_bias_grads = jnp.stack([self_q_bias_grad, self_v_bias_grad, self_out_bias_grad])
    cross_bias_grads = jnp.stack([cross_q_bias_grad, cross_v_bias_grad, cross_out_bias_grad])
    summed = lax.psum(
        (gain_grads, shift_grads, self_bias_grads, cross_bias_grads, grad_up_bias, grad_down_bias),
        ("ctx", "fsdp"),
    )
    return (
        layer_out[None],
        grad_tokens[None],
        grad_encoded[None],
        summed[0],
        summed[1],
        owned[0],
        summed[2],
        owned[1],
        owned[2],
        owned[3],
        summed[3],
        owned[4],
        owned[5],
        summed[4],
        owned[6],
        summed[5],
    )


def general_solution(mesh):
    placed = (
        P("fsdp", "ctx", None),
        P("fsdp", "ctx", None),
        P("fsdp", "ctx", None),
        P("fsdp", None),
        P("fsdp", None),
        P(),
        P(),
        P("fsdp", None),
        P(),
        P("fsdp", None),
        P("fsdp", None),
        P("fsdp", None),
        P(),
        P("fsdp", None),
        P("fsdp", None),
        P(),
        P("fsdp", None),
        P(),
    )
    return jax.shard_map(
        per_device,
        mesh=mesh,
        in_specs=placed,
        out_specs=(
            P("fsdp", "ctx", None),
            P("fsdp", "ctx", None),
            P("fsdp", "ctx", None),
            P(),
            P(),
            P("fsdp", "ctx"),
            P(),
            P("fsdp", "ctx"),
            P("fsdp", "ctx"),
            P("fsdp", "ctx"),
            P(),
            P("fsdp", "ctx"),
            P("fsdp", "ctx"),
            P(),
            P("fsdp", "ctx"),
            P(),
        ),
        check_vma=False,
    )


CTX = ("cz", "cy")
GRID = ("cy", "fsdp")
QBLOCK = 256
HALF = 128
PAIR = 2 * HEAD_DIM
MAX_KEY_BLOCKS = 5


def doc_start_of(starts_ref, positions):
    first = jnp.zeros_like(positions)
    for doc in range(starts_ref.shape[0]):
        begin = starts_ref[doc]
        first = jnp.where(positions >= begin, begin, first)
    return first


def doc_start_scalar(starts_ref, position):
    first = jnp.int32(0)
    for doc in range(starts_ref.shape[0]):
        begin = starts_ref[doc]
        first = jnp.where(position >= begin, begin, first)
    return first


def half_row(pos_block, pos_blocks):
    early = pos_block * (2 * HALF)
    late = (pos_blocks - 1 - pos_block) * (2 * HALF) + HALF
    return pl.multiple_of(jnp.where(2 * pos_block < pos_blocks, early, late), HALF)


def lane_mask(rows, head):
    lanes = lax.broadcasted_iota(jnp.int32, (rows, PAIR), 1)
    return (lanes >= head * HEAD_DIM) & (lanes < (head + 1) * HEAD_DIM)


def to_positions(src_ref, column, dst_ref):
    pos_blocks = src_ref.shape[0] // HALF

    def move(block, carry):
        row = half_row(block, pos_blocks)
        dst_ref[pl.ds(pl.multiple_of(block * HALF, HALF), HALF), :] = src_ref[
            pl.ds(row, HALF), pl.ds(column, PAIR)
        ]
        return carry

    lax.fori_loop(0, pos_blocks, move, 0)


def self_forward_kernel(starts_ref, qkv_ref, out_ref, key_ref, value_ref):
    step = pl.program_id(0)
    pos_blocks = qkv_ref.shape[0] // HALF

    @pl.when(step == 0)
    def _():
        to_positions(qkv_ref, PAIR, key_ref)
        to_positions(qkv_ref, 2 * PAIR, value_ref)

    row_a = half_row(2 * step, pos_blocks)
    row_b = half_row(2 * step + 1, pos_blocks)
    queries = jnp.concatenate(
        [qkv_ref[pl.ds(row_a, HALF), pl.ds(0, PAIR)], qkv_ref[pl.ds(row_b, HALF), pl.ds(0, PAIR)]],
        axis=0,
    )
    q_start = step * QBLOCK
    first_block = doc_start_scalar(starts_ref, q_start) // QBLOCK
    count = step - first_block + 1
    q_pos = q_start + lax.broadcasted_iota(jnp.int32, (QBLOCK, 1), 0)
    q_first = doc_start_of(starts_ref, q_pos)

    def compute(blocks):
        width = blocks * QBLOCK
        k_start = pl.multiple_of(first_block * QBLOCK, QBLOCK)
        keys = key_ref[pl.ds(k_start, width), :]
        values = value_ref[pl.ds(k_start, width), :]
        k_pos = k_start + lax.broadcasted_iota(jnp.int32, (QBLOCK, width), 1)
        allowed = (k_pos >= q_first) & (k_pos <= q_pos)
        parts = []
        for head in range(2):
            picked = jnp.where(lane_mask(QBLOCK, head), queries, jnp.zeros_like(queries))
            scores = lax.dot_general(picked, keys, CONTRACT_COLS, preferred_element_type=jnp.float32)
            scores = jnp.where(allowed, scores, NEG)
            terms = jnp.exp(scores - jnp.max(scores, axis=1, keepdims=True))
            inverse = 1.0 / jnp.sum(terms, axis=1, keepdims=True)
            mixed = jnp.dot(
                (terms * inverse).astype(jnp.bfloat16), values, preferred_element_type=jnp.float32
            )
            parts.append(mixed)
        result = jnp.where(lane_mask(QBLOCK, 0), parts[0], parts[1]).astype(jnp.bfloat16)
        out_ref[pl.ds(row_a, HALF), :] = result[:HALF]
        out_ref[pl.ds(row_b, HALF), :] = result[HALF:]

    for blocks in range(1, MAX_KEY_BLOCKS + 1):
        pl.when(count == blocks)(functools.partial(compute, blocks))


def self_backward_kernel(
    starts_ref, qkv_ref, grad_ref, out_ref, key_ref, value_ref, dkey_ref, dvalue_ref
):
    step = pl.program_id(0)
    pos_blocks = qkv_ref.shape[0] // HALF

    @pl.when(step == 0)
    def _():
        to_positions(qkv_ref, PAIR, key_ref)
        to_positions(qkv_ref, 2 * PAIR, value_ref)
        dkey_ref[...] = jnp.zeros_like(dkey_ref)
        dvalue_ref[...] = jnp.zeros_like(dvalue_ref)

    row_a = half_row(2 * step, pos_blocks)
    row_b = half_row(2 * step + 1, pos_blocks)
    queries = jnp.concatenate(
        [qkv_ref[pl.ds(row_a, HALF), pl.ds(0, PAIR)], qkv_ref[pl.ds(row_b, HALF), pl.ds(0, PAIR)]],
        axis=0,
    )
    grads = jnp.concatenate([grad_ref[pl.ds(row_a, HALF), :], grad_ref[pl.ds(row_b, HALF), :]], axis=0)
    q_start = step * QBLOCK
    first_block = doc_start_scalar(starts_ref, q_start) // QBLOCK
    count = step - first_block + 1
    q_pos = q_start + lax.broadcasted_iota(jnp.int32, (1, QBLOCK), 1)
    q_first = doc_start_of(starts_ref, q_pos)

    def compute(blocks):
        width = blocks * QBLOCK
        k_start = pl.multiple_of(first_block * QBLOCK, QBLOCK)
        keys = key_ref[pl.ds(k_start, width), :]
        values = value_ref[pl.ds(k_start, width), :]
        k_pos = k_start + lax.broadcasted_iota(jnp.int32, (width, QBLOCK), 0)
        allowed = (k_pos >= q_first) & (k_pos <= q_pos)
        dq_parts = []
        dkey = jnp.zeros((width, PAIR), jnp.float32)
        dvalue = jnp.zeros((width, PAIR), jnp.float32)
        for head in range(2):
            inside = lane_mask(QBLOCK, head)
            picked = jnp.where(inside, queries, jnp.zeros_like(queries))
            grad = jnp.where(inside, grads, jnp.zeros_like(grads))
            scores = lax.dot_general(keys, picked, CONTRACT_COLS, preferred_element_type=jnp.float32)
            scores = jnp.where(allowed, scores, NEG)
            terms = jnp.exp(scores - jnp.max(scores, axis=0, keepdims=True))
            probs = terms * (1.0 / jnp.sum(terms, axis=0, keepdims=True))
            dprobs = lax.dot_general(
                values, grad, CONTRACT_COLS, preferred_element_type=jnp.float32
            )
            delta = jnp.sum(probs * dprobs, axis=0, keepdims=True)
            dscores = (probs * (dprobs - delta)).astype(jnp.bfloat16)
            dq_parts.append(
                lax.dot_general(dscores, keys, CONTRACT_ROWS, preferred_element_type=jnp.float32)
            )
            dkey = dkey + jnp.dot(dscores, picked, preferred_element_type=jnp.float32)
            dvalue = dvalue + jnp.dot(
                probs.astype(jnp.bfloat16), grad, preferred_element_type=jnp.float32
            )
        dkey_ref[pl.ds(k_start, width), :] += dkey
        dvalue_ref[pl.ds(k_start, width), :] += dvalue
        dq = jnp.where(lane_mask(QBLOCK, 0), dq_parts[0], dq_parts[1])
        dq = (dq * (1.0 / math.sqrt(HEAD_DIM))).astype(jnp.bfloat16)
        out_ref[pl.ds(row_a, HALF), pl.ds(0, PAIR)] = dq[:HALF]
        out_ref[pl.ds(row_b, HALF), pl.ds(0, PAIR)] = dq[HALF:]

    for blocks in range(1, MAX_KEY_BLOCKS + 1):
        pl.when(count == blocks)(functools.partial(compute, blocks))

    @pl.when(step == pl.num_programs(0) - 1)
    def _():
        def move(block, carry):
            row = half_row(block, pos_blocks)
            place = pl.ds(pl.multiple_of(block * HALF, HALF), HALF)
            out_ref[pl.ds(row, HALF), pl.ds(PAIR, PAIR)] = dkey_ref[place, :].astype(jnp.bfloat16)
            out_ref[pl.ds(row, HALF), pl.ds(2 * PAIR, PAIR)] = dvalue_ref[place, :].astype(
                jnp.bfloat16
            )
            return carry

        lax.fori_loop(0, pos_blocks, move, 0)


def cross_forward_kernel(q_ref, key_ref, value_ref, low_ref, high_ref, out_ref):
    rows, width = q_ref.shape[0], key_ref.shape[0]
    queries, keys, values = q_ref[...], key_ref[...], value_ref[...]
    k_pos = lax.broadcasted_iota(jnp.int32, (rows, width), 1)
    allowed = (k_pos >= low_ref[...]) & (k_pos < high_ref[...])
    parts = []
    for head in range(2):
        picked = jnp.where(lane_mask(rows, head), queries, jnp.zeros_like(queries))
        scores = lax.dot_general(picked, keys, CONTRACT_COLS, preferred_element_type=jnp.float32)
        scores = jnp.where(allowed, scores, NEG)
        terms = jnp.exp(scores - jnp.max(scores, axis=1, keepdims=True))
        inverse = 1.0 / jnp.sum(terms, axis=1, keepdims=True)
        parts.append(
            jnp.dot((terms * inverse).astype(jnp.bfloat16), values, preferred_element_type=jnp.float32)
        )
    out_ref[...] = jnp.where(lane_mask(rows, 0), parts[0], parts[1]).astype(jnp.bfloat16)


def cross_backward_kernel(q_ref, key_ref, value_ref, grad_ref, low_ref, high_ref, dq_ref, dkv_ref):
    rows, width = q_ref.shape[0], key_ref.shape[0]
    queries, keys, values, grads = q_ref[...], key_ref[...], value_ref[...], grad_ref[...]
    k_pos = lax.broadcasted_iota(jnp.int32, (width, rows), 0)
    allowed = (k_pos >= low_ref[...]) & (k_pos < high_ref[...])
    dq_parts = []
    dkey = jnp.zeros((width, PAIR), jnp.float32)
    dvalue = jnp.zeros((width, PAIR), jnp.float32)
    for head in range(2):
        inside = lane_mask(rows, head)
        picked = jnp.where(inside, queries, jnp.zeros_like(queries))
        grad = jnp.where(inside, grads, jnp.zeros_like(grads))
        scores = lax.dot_general(keys, picked, CONTRACT_COLS, preferred_element_type=jnp.float32)
        scores = jnp.where(allowed, scores, NEG)
        terms = jnp.exp(scores - jnp.max(scores, axis=0, keepdims=True))
        probs = terms * (1.0 / jnp.sum(terms, axis=0, keepdims=True))
        dprobs = lax.dot_general(values, grad, CONTRACT_COLS, preferred_element_type=jnp.float32)
        delta = jnp.sum(probs * dprobs, axis=0, keepdims=True)
        dscores = (probs * (dprobs - delta)).astype(jnp.bfloat16)
        dq_parts.append(
            lax.dot_general(dscores, keys, CONTRACT_ROWS, preferred_element_type=jnp.float32)
        )
        dkey = dkey + jnp.dot(dscores, picked, preferred_element_type=jnp.float32)
        dvalue = dvalue + jnp.dot(
            probs.astype(jnp.bfloat16), grad, preferred_element_type=jnp.float32
        )
    dq = jnp.where(lane_mask(rows, 0), dq_parts[0], dq_parts[1])
    dq_ref[...] = (dq * (1.0 / math.sqrt(HEAD_DIM))).astype(jnp.bfloat16)
    dkv_ref[0, 0] = dkey.astype(jnp.bfloat16)
    dkv_ref[1, 0] = dvalue.astype(jnp.bfloat16)


def kernel_params():
    return pltpu.CompilerParams(vmem_limit_bytes=48 * 1024 * 1024)


def self_forward(doc_starts, qkv):
    rows = qkv.shape[0]
    return pl.pallas_call(
        self_forward_kernel,
        grid=(rows // QBLOCK,),
        in_specs=[
            pl.BlockSpec(memory_space=pltpu.SMEM),
            pl.BlockSpec((rows, 3 * PAIR), lambda step: (0, 0)),
        ],
        out_specs=pl.BlockSpec((rows, PAIR), lambda step: (0, 0)),
        out_shape=jax.ShapeDtypeStruct((rows, PAIR), jnp.bfloat16),
        scratch_shapes=[pltpu.VMEM((rows, PAIR), jnp.bfloat16)] * 2,
        compiler_params=kernel_params(),
        cost_estimate=pl.CostEstimate(
            flops=2 * rows * 1024 * 256 * 2, bytes_accessed=rows * PAIR * 8, transcendentals=0
        ),
    )(doc_starts, qkv)


def self_backward(doc_starts, qkv, grads):
    rows = qkv.shape[0]
    return pl.pallas_call(
        self_backward_kernel,
        grid=(rows // QBLOCK,),
        in_specs=[
            pl.BlockSpec(memory_space=pltpu.SMEM),
            pl.BlockSpec((rows, 3 * PAIR), lambda step: (0, 0)),
            pl.BlockSpec((rows, PAIR), lambda step: (0, 0)),
        ],
        out_specs=pl.BlockSpec((rows, 3 * PAIR), lambda step: (0, 0)),
        out_shape=jax.ShapeDtypeStruct((rows, 3 * PAIR), jnp.bfloat16),
        scratch_shapes=[pltpu.VMEM((rows, PAIR), jnp.bfloat16)] * 2
        + [pltpu.VMEM((rows, PAIR), jnp.float32)] * 2,
        compiler_params=kernel_params(),
        cost_estimate=pl.CostEstimate(
            flops=5 * rows * 1024 * 256 * 2, bytes_accessed=rows * PAIR * 14, transcendentals=0
        ),
    )(doc_starts, qkv, grads)


def cross_forward(queries, kv_cross, low, high):
    rows, features = queries.shape
    pairs = features // PAIR
    src = kv_cross.shape[0]
    return pl.pallas_call(
        cross_forward_kernel,
        grid=(pairs,),
        in_specs=[
            pl.BlockSpec((rows, PAIR), lambda p: (0, p)),
            pl.BlockSpec((src, PAIR), lambda p: (0, p)),
            pl.BlockSpec((src, PAIR), lambda p: (0, p + pairs)),
            pl.BlockSpec((rows, 1), lambda p: (0, 0)),
            pl.BlockSpec((rows, 1), lambda p: (0, 0)),
        ],
        out_specs=pl.BlockSpec((rows, PAIR), lambda p: (0, p)),
        out_shape=jax.ShapeDtypeStruct((rows, features), jnp.bfloat16),
        compiler_params=kernel_params(),
        cost_estimate=pl.CostEstimate(
            flops=4 * rows * src * features, bytes_accessed=3 << 20, transcendentals=0
        ),
    )(queries, kv_cross, kv_cross, low[:, None], high[:, None])


def cross_backward(queries, kv_cross, grads, low, high):
    rows, features = queries.shape
    pairs = features // PAIR
    src = kv_cross.shape[0]
    return pl.pallas_call(
        cross_backward_kernel,
        grid=(pairs,),
        in_specs=[
            pl.BlockSpec((rows, PAIR), lambda p: (0, p)),
            pl.BlockSpec((src, PAIR), lambda p: (0, p)),
            pl.BlockSpec((src, PAIR), lambda p: (0, p + pairs)),
            pl.BlockSpec((rows, PAIR), lambda p: (0, p)),
            pl.BlockSpec((1, rows), lambda p: (0, 0)),
            pl.BlockSpec((1, rows), lambda p: (0, 0)),
        ],
        out_specs=[
            pl.BlockSpec((rows, PAIR), lambda p: (0, p)),
            pl.BlockSpec((2, 1, src, PAIR), lambda p: (0, p, 0, 0)),
        ],
        out_shape=[
            jax.ShapeDtypeStruct((rows, features), jnp.bfloat16),
            jax.ShapeDtypeStruct((2, pairs, src, PAIR), jnp.bfloat16),
        ],
        compiler_params=kernel_params(),
        cost_estimate=pl.CostEstimate(
            flops=10 * rows * src * features, bytes_accessed=6 << 20, transcendentals=0
        ),
    )(queries, kv_cross, kv_cross, grads, low[None, :], high[None, :])


def swap_fsdp(pieces):
    own = lax.axis_index("fsdp")
    count = pieces.shape[0]
    whole = pieces
    for distance in range(1, count):
        moved = lax.ppermute(
            lax.dynamic_index_in_dim(pieces, own ^ distance, 0, keepdims=False),
            "fsdp",
            [(i, i ^ distance) for i in range(count)],
        )
        whole = lax.dynamic_update_index_in_dim(whole, moved, own ^ distance, 0)
    return whole


def low(value):
    return value.astype(jnp.bfloat16)


def wide(value):
    return value.astype(jnp.float32)


def planned_device(
    tokens,
    encoded,
    grad_out,
    doc_lengths,
    src_lengths,
    norm_gain,
    norm_bias,
    w_qkv,
    self_bias,
    w_self_out,
    w_cross_q,
    w_cross_kv,
    cross_bias,
    w_cross_out,
    w_up,
    up_bias,
    w_down,
    down_bias,
):
    q_scale = 1.0 / math.sqrt(HEAD_DIM)
    rows, features = tokens.shape[1:]
    n_z, n_y, n_f = lax.axis_size("cz"), lax.axis_size("cy"), lax.axis_size("fsdp")
    n_ctx = n_z * n_y
    me_y, me_f = lax.axis_index("cy"), lax.axis_index("fsdp")
    me_c = lax.axis_index(CTX)
    shard = w_up.shape[0]
    hidden = w_up.shape[1]
    slab = hidden // (n_z * n_y * n_f)

    own_rows = me_c * rows + jnp.arange(rows, dtype=jnp.int32)
    tok_pos = stream_position(own_rows, rows, n_ctx)
    lengths_row = doc_lengths[0]
    doc_starts = jnp.cumsum(lengths_row) - lengths_row
    tok_doc = doc_index(doc_starts, tok_pos)
    src_row = src_lengths[0]
    src_ends = jnp.cumsum(src_row)
    span_low = pick_doc(src_ends - src_row, tok_doc)
    span_high = pick_doc(src_ends, tok_doc)

    qkv_cols = lax.dynamic_index_in_dim(
        w_qkv.reshape(shard, 3, n_ctx, PAIR), me_c, 2, keepdims=False
    ).reshape(shard, 3 * PAIR)
    qkv_own = lax.all_gather(qkv_cols, "fsdp", axis=0, tiled=True)

    tok_f32 = wide(tokens[0])
    ln_one, normed_one, inverse_one = layer_norm(tok_f32, norm_gain[0], norm_bias[0])
    act_one = low(ln_one)
    act_one_all = lax.all_gather(act_one, CTX, axis=0, tiled=True)
    full_self_out, full_cross_q, full_cross_out = (
        lax.all_gather(w, "fsdp", axis=0, tiled=True) for w in (w_self_out, w_cross_q, w_cross_out)
    )
    enc_all = lax.all_gather(encoded[0], CTX, axis=0, tiled=True)
    full_cross_kv = lax.all_gather(w_cross_kv, "fsdp", axis=0, tiled=True)

    up_pieces = jnp.moveaxis(
        lax.dynamic_index_in_dim(
            w_up.reshape(shard, n_z, n_y, n_f, slab), me_y, 2, keepdims=False
        ),
        2,
        0,
    ).reshape(n_f, shard, n_z * slab)
    down_pieces = lax.dynamic_index_in_dim(
        w_down.reshape(n_y, n_f, slab, features), me_y, 0, keepdims=False
    )
    mlp_w = swap_fsdp(jnp.concatenate([up_pieces, down_pieces], axis=1))
    up_own = mlp_w[:, :shard].reshape(n_f * shard, n_z * slab)
    down_own = mlp_w[:, shard:].reshape(n_f * slab, features)

    head_bias = lax.dynamic_slice_in_dim(self_bias, me_c * PAIR, PAIR, 1)
    projected = plain_dot(act_one_all, qkv_own)
    qkv_heads = low(
        jnp.concatenate(
            [
                (projected[:, :PAIR] + head_bias[0]) * q_scale,
                projected[:, PAIR : 2 * PAIR],
                projected[:, 2 * PAIR :] + head_bias[1],
            ],
            axis=1,
        )
    )
    att_heads = self_forward(doc_starts, qkv_heads)
    att_self = lax.all_to_all(att_heads, CTX, 0, 1, tiled=True)
    hidden_one = tok_f32 + plain_dot(att_self, full_self_out) + self_bias[2]

    ln_two, normed_two, inverse_two = layer_norm(hidden_one, norm_gain[1], norm_bias[1])
    act_two = low(ln_two)
    q_cross = low((plain_dot(act_two, full_cross_q) + cross_bias[0]) * q_scale)
    kv_bias = jnp.concatenate([jnp.zeros((features,), jnp.float32), cross_bias[1]])
    kv_cross = low(plain_dot(enc_all, full_cross_kv) + kv_bias)
    att_cross = cross_forward(q_cross, kv_cross, span_low, span_high)
    hidden_two = hidden_one + plain_dot(att_cross, full_cross_out) + cross_bias[2]

    ln_three, normed_three, inverse_three = layer_norm(hidden_two, norm_gain[2], norm_bias[2])
    act_three = lax.all_gather(low(ln_three), GRID, axis=0, tiled=True)
    grad_all = lax.all_gather(grad_out[0], GRID, axis=0, tiled=True)
    up_bias_own = lax.dynamic_index_in_dim(
        lax.dynamic_index_in_dim(up_bias.reshape(n_z, n_y, n_f, slab), me_f, 2, keepdims=False),
        me_y,
        1,
        keepdims=False,
    ).reshape(-1)
    pre_act = plain_dot(act_three, up_own) + up_bias_own
    gelu_low = low(gelu_value(pre_act))
    slope = gelu_slope(pre_act)
    pre_grad = low(times_transpose(grad_all, down_own) * slope)
    act_grad = lax.psum_scatter(
        low(times_transpose(pre_grad, up_own)), GRID, scatter_dimension=0, tiled=True
    )
    down_part = low(plain_dot(gelu_low, down_own))

    upstream = wide(grad_out[0])
    norm_in_three, gain_grad_three, shift_grad_three = norm_back(
        wide(act_grad), normed_three, inverse_three, norm_gain[2]
    )
    grad_two = upstream + norm_in_three
    down_part, grad_two = lax.optimization_barrier((down_part, grad_two))
    mlp_out = lax.psum_scatter(down_part, GRID, scatter_dimension=0, tiled=True)
    layer_out = low(hidden_two + wide(mlp_out) + down_bias)

    up_grad = low(outer_rows(pre_grad, act_three))
    down_grad = low(outer_rows(grad_all, gelu_low))
    up_grad = lax.psum_scatter(up_grad, "cz", scatter_dimension=0, tiled=True)
    down_grad = lax.psum_scatter(down_grad, "cz", scatter_dimension=0, tiled=True)
    up_bias_grad = jnp.sum(wide(pre_grad), axis=0)
    grad_down_bias = jnp.sum(upstream, axis=0)

    cross_grad_low = low(grad_two)
    grad_w_cross_out = low(outer_rows(att_cross, cross_grad_low))
    cross_out_bias_grad = jnp.sum(wide(cross_grad_low), axis=0)
    cross_att_grad = low(times_transpose(cross_grad_low, full_cross_out))
    cross_v_bias_grad = jnp.sum(wide(cross_att_grad), axis=0)
    cross_q_low, cross_kv_part = cross_backward(
        q_cross, kv_cross, cross_att_grad, span_low, span_high
    )
    grad_w_cross_q = low(outer_rows(act_two, cross_q_low))
    cross_q_bias_grad = jnp.sum(wide(cross_q_low), axis=0)
    norm_in_two, gain_grad_two, shift_grad_two = norm_back(
        times_transpose(cross_q_low, full_cross_q), normed_two, inverse_two, norm_gain[1]
    )
    grad_one = grad_two + norm_in_two
    self_grad_low = low(grad_one)
    self_att_grad = low(times_transpose(self_grad_low, full_self_out))
    self_v_bias_grad = jnp.sum(wide(self_att_grad), axis=0)
    att_grad_heads = lax.all_to_all(self_att_grad, CTX, 1, 0, tiled=True)
    proj_grad_heads = self_backward(doc_starts, qkv_heads, att_grad_heads)

    grad_w_self_out = low(outer_rows(att_self, self_grad_low))
    self_out_bias_grad = jnp.sum(wide(self_grad_low), axis=0)

    blocks = 2 * features // PAIR
    src_rows = enc_all.shape[0]
    cross_kv_grad = lax.psum_scatter(
        cross_kv_part.reshape(blocks, src_rows, PAIR), CTX, scatter_dimension=0, tiled=True
    )
    per = blocks // n_ctx
    cross_kv_grad = jnp.concatenate([cross_kv_grad[i] for i in range(per)], axis=1)
    kv_w_own = lax.dynamic_slice_in_dim(full_cross_kv, me_c * per * PAIR, per * PAIR, 1)
    grad_encoded = wide(
        lax.psum_scatter(
            low(times_transpose(cross_kv_grad, kv_w_own)), CTX, scatter_dimension=0, tiled=True
        )
    )
    grad_w_cross_kv = wide(
        lax.psum_scatter(
            low(outer_rows(enc_all, cross_kv_grad)), "fsdp", scatter_dimension=0, tiled=True
        )
    )

    proj_grad = lax.all_to_all(
        proj_grad_heads.reshape(n_ctx, rows, 3 * PAIR), CTX, 0, 0, tiled=False
    )
    full_qkv = lax.all_gather(w_qkv, "fsdp", axis=0, tiled=True)
    proj_grad = jnp.transpose(proj_grad.reshape(n_ctx, rows, 3, PAIR), (1, 2, 0, 3)).reshape(
        rows, 3 * features
    )
    self_q_bias_grad = jnp.sum(wide(proj_grad[:, :features]), axis=0)
    norm_in_one, gain_grad_one, shift_grad_one = norm_back(
        times_transpose(proj_grad, full_qkv), normed_one, inverse_one, norm_gain[0]
    )
    grad_tokens = grad_one + norm_in_one

    qkv_grad = lax.psum_scatter(
        low(outer_rows(act_one_all, proj_grad_heads)), "fsdp", scatter_dimension=0, tiled=True
    ).reshape(shard, 3, PAIR)
    qkv_blocks = []
    inverse_of_three = pow(3, -1, n_ctx)
    for slot in range(3):
        pairs = [((3 * dest + slot) % n_ctx, dest) for dest in range(n_ctx)]
        dest = (inverse_of_three * (me_c - slot)) % n_ctx
        part = (3 * dest + slot) // n_ctx
        qkv_blocks.append(
            lax.ppermute(
                lax.dynamic_index_in_dim(qkv_grad, part, 1, keepdims=False), CTX, pairs
            )
        )
    grad_w_qkv = wide(jnp.concatenate(qkv_blocks, axis=1))

    three = jnp.concatenate([grad_w_self_out, grad_w_cross_q, grad_w_cross_out], axis=1)
    three = lax.psum_scatter(three, "fsdp", scatter_dimension=0, tiled=True)
    width = features // n_ctx
    three = jnp.transpose(three.reshape(shard, 3, n_ctx, width), (2, 1, 0, 3)).reshape(
        n_ctx * 3 * shard, width
    )
    three = wide(lax.psum_scatter(three, CTX, scatter_dimension=0, tiled=True)).reshape(
        3, shard, width
    )

    mlp_pieces = jnp.concatenate(
        [
            jnp.moveaxis(up_grad.reshape(slab, n_f, shard), 1, 0),
            jnp.moveaxis(down_grad.reshape(features // n_z, n_f, slab), 1, 0),
        ],
        axis=1,
    )
    mlp_pieces = swap_fsdp(mlp_pieces)
    grad_w_up = wide(jnp.transpose(mlp_pieces[:, :slab].reshape(n_f * slab, shard)))
    down_cols = mlp_pieces[:, slab:].reshape(n_f, n_y, width, slab)
    other = lax.ppermute(
        lax.dynamic_index_in_dim(down_cols, 1 - me_y, 1, keepdims=False), "cy", [(0, 1), (1, 0)]
    )
    mine = lax.dynamic_index_in_dim(down_cols, me_y, 1, keepdims=False)
    down_halves = jnp.stack([jnp.where(me_y == 0, mine, other), jnp.where(me_y == 0, other, mine)])
    grad_w_down = wide(jnp.transpose(down_halves, (0, 1, 3, 2)).reshape(n_y * n_f * slab, width))

    vectors = jnp.stack(
        [
            gain_grad_one,
            gain_grad_two,
            gain_grad_three,
            shift_grad_one,
            shift_grad_two,
            shift_grad_three,
            self_q_bias_grad,
            self_v_bias_grad,
            self_out_bias_grad,
            cross_q_bias_grad,
            cross_v_bias_grad,
            cross_out_bias_grad,
            grad_down_bias,
            up_bias_grad,
        ]
    )
    gathered = lax.all_gather(vectors, GRID, axis=0, tiled=False)
    up_rows = gathered[:, -1]
    level = jnp.concatenate([jnp.sum(gathered[:, :-1], axis=0), up_rows], axis=0)
    level = jnp.sum(lax.all_gather(level, "cz", axis=0, tiled=False), axis=0)
    grad_up_bias = jnp.transpose(
        level[13:].reshape(n_y, n_f, n_z, slab), (2, 0, 1, 3)
    ).reshape(hidden)

    return (
        layer_out[None],
        grad_tokens[None],
        grad_encoded[None],
        level[0:3],
        level[3:6],
        grad_w_qkv,
        level[6:9],
        three[0],
        three[1],
        grad_w_cross_kv,
        level[9:12],
        three[2],
        grad_w_up,
        grad_up_bias,
        grad_w_down,
        level[12],
    )


def planned_solution(mesh):
    n_ctx, n_f = mesh.shape["ctx"], mesh.shape["fsdp"]
    split = Mesh(mesh.devices.reshape(n_ctx // 2, 2, n_f), ("cz", "cy", "fsdp"))
    token = P("fsdp", CTX, None)
    row = P("fsdp", None)
    owned = P("fsdp", CTX)
    return jax.shard_map(
        planned_device,
        mesh=split,
        in_specs=(token, token, token, row, row, P(), P(), row, P(), row, row, row, P(), row)
        + (row, P(), row, P()),
        out_specs=(token, token, token, P(), P(), owned, P(), owned, owned, owned, P(), owned)
        + (owned, P(), owned, P()),
        check_vma=False,
    )


def solution(mesh):
    if mesh.shape["ctx"] * 2 == HEADS and mesh.shape["fsdp"] * 2 == mesh.shape["ctx"]:
        return planned_solution(mesh)
    return general_solution(mesh)
```

```python
import functools
import math

import jax
import jax.numpy as jnp
from jax import lax
from jax.experimental import pallas as pl
from jax.experimental.layout import Layout, with_layout_constraint
from jax.experimental.pallas import tpu as pltpu
from jax.sharding import Mesh
from jax.sharding import PartitionSpec as P

HEADS = 16
HEAD_DIM = 64
KBLOCK = 512


EPS = 1e-05
NEG = -1e30
GELU_C = 0.7978845608028654
GELU_A = 0.044715
CONTRACT_ROWS = (((0,), (0,)), ((), ()))
CONTRACT_COLS = (((1,), (1,)), ((), ()))


def shortened(shard):
    return jax.tree.map(lambda a: a.astype(jnp.bfloat16) if a.dtype == jnp.float32 else a, shard)


def gelu_value(pre):
    return 0.5 * pre * (1.0 + jnp.tanh(GELU_C * (pre + GELU_A * pre * pre * pre)))


def gelu_slope(pre):
    tangent = jnp.tanh(GELU_C * (pre + GELU_A * pre * pre * pre))
    return 0.5 * (1.0 + tangent) + 0.5 * pre * (1.0 - tangent * tangent) * GELU_C * (
        1.0 + 3.0 * GELU_A * pre * pre
    )


def stream_position(rows, tok_dev, ctx_count):
    half = tok_dev // 2
    device = rows // tok_dev
    within = rows % tok_dev
    early = device * half + within
    late = (2 * ctx_count - 1 - device) * half + (within - half)
    return jnp.where(within < half, early, late)


def layer_norm(inputs, gain_row, shift_row):
    center = inputs - jnp.mean(inputs, axis=1, keepdims=True)
    inverse = lax.rsqrt(jnp.mean(center * center, axis=1, keepdims=True) + EPS)
    normed = center * inverse
    return (normed * gain_row + shift_row, normed, inverse)


def norm_back(upstream, normed, inverse, gain_row):
    scaled = upstream * gain_row
    mean_plain = jnp.mean(scaled, axis=1, keepdims=True)
    mean_normed = jnp.mean(scaled * normed, axis=1, keepdims=True)
    return (
        inverse * (scaled - mean_plain - normed * mean_normed),
        jnp.sum(upstream * normed, axis=0),
        jnp.sum(upstream, axis=0),
    )


def outer_rows(left, right):
    return lax.dot_general(left, right, CONTRACT_ROWS, preferred_element_type=jnp.float32)


def times_transpose(left, right):
    return lax.dot_general(left, right, CONTRACT_COLS, preferred_element_type=jnp.float32)


def plain_dot(left, right):
    return jnp.dot(left, right, preferred_element_type=jnp.float32)


def doc_index(doc_starts, positions):
    counted = jnp.sum((doc_starts[None, :] <= positions[:, None]).astype(jnp.int32), axis=1)
    return counted - 1


def pick_doc(lookup, doc_ids):
    onehot = doc_ids[:, None] == jnp.arange(lookup.shape[0], dtype=jnp.int32)[None, :]
    return jnp.sum(jnp.where(onehot, lookup[None, :], 0), axis=1)


def split_heads(matrix):
    return matrix.reshape(matrix.shape[0], HEADS, matrix.shape[1] // HEADS)


def split_pair(kv_piece):
    half_width = kv_piece.shape[1] // 2
    return (split_heads(kv_piece[:, :half_width]), split_heads(kv_piece[:, half_width:]))


def key_block(kv_whole, block_start):
    return split_pair(lax.dynamic_slice_in_dim(kv_whole, block_start, KBLOCK, 0))


def block_starts(kv_whole):
    return jnp.arange(kv_whole.shape[0] // KBLOCK, dtype=jnp.int32) * KBLOCK


def score_block(queries, key_heads):
    return jnp.einsum("qhd,khd->hqk", queries, key_heads, preferred_element_type=jnp.float32)


def attend(queries, kv_whole, allowed_fn):
    shape_stat = (queries.shape[1], queries.shape[0])

    def stat_step(state_pair, block_start):
        allowed = allowed_fn(block_start)

        def stat_compute_block(running):
            running_top, running_sum = running
            key_heads, value_heads = key_block(kv_whole, block_start)
            masked = jnp.where(allowed[None], score_block(queries, key_heads), NEG)
            new_top = jnp.maximum(running_top, jnp.max(masked, axis=2))
            exp_terms = jnp.where(allowed[None], jnp.exp(masked - new_top[:, :, None]), 0.0)
            return (
                new_top,
                running_sum * jnp.exp(running_top - new_top) + jnp.sum(exp_terms, axis=2),
            )

        return (
            lax.cond(jnp.any(allowed), stat_compute_block, lambda running: running, state_pair),
            None,
        )

    initial = (jnp.full(shape_stat, NEG, jnp.float32), jnp.zeros(shape_stat, jnp.float32))
    (final_top, final_sum), _ = lax.scan(stat_step, initial, block_starts(kv_whole))
    logsum = final_top + jnp.log(final_sum)

    def value_step(running, block_start):
        allowed = allowed_fn(block_start)

        def value_compute_block(partial_value):
            key_heads, value_heads = key_block(kv_whole, block_start)
            raw_scores = score_block(queries, key_heads)
            prob_low = jnp.where(
                allowed[None], jnp.exp(raw_scores - logsum[:, :, None]), 0.0
            ).astype(jnp.bfloat16)
            return partial_value + jnp.einsum(
                "hqk,khd->qhd", prob_low, value_heads, preferred_element_type=jnp.float32
            )

        return (
            lax.cond(
                jnp.any(allowed), value_compute_block, lambda partial_value: partial_value, running
            ),
            None,
        )

    attended, _ = lax.scan(
        value_step, jnp.zeros(queries.shape, jnp.float32), block_starts(kv_whole)
    )
    return (attended, logsum)


def score_grads(queries, key_heads, value_heads, grad_heads, logsum, row_delta, allowed):
    raw_scores = score_block(queries, key_heads)
    probs_full = jnp.where(allowed[None], jnp.exp(raw_scores - logsum[:, :, None]), 0.0)
    grad_probs = jnp.einsum(
        "qhd,khd->hqk", grad_heads, value_heads, preferred_element_type=jnp.float32
    )
    grad_scores = (probs_full * (grad_probs - row_delta[:, :, None])).astype(jnp.bfloat16)
    return (probs_full, grad_scores)


def key_terms(queries, key_heads, value_heads, grad_heads, logsum, row_delta, allowed):
    probs_full, grad_scores = score_grads(
        queries, key_heads, value_heads, grad_heads, logsum, row_delta, allowed
    )
    grad_keys = jnp.einsum("hqk,qhd->khd", grad_scores, queries, preferred_element_type=jnp.float32)
    grad_values = jnp.einsum(
        "hqk,qhd->khd",
        probs_full.astype(jnp.bfloat16),
        grad_heads,
        preferred_element_type=jnp.float32,
    )
    key_count = key_heads.shape[0]
    return jnp.concatenate(
        [grad_keys.reshape(key_count, -1), grad_values.reshape(key_count, -1)], axis=1
    )


def row_deltas(grad_heads, attended):
    return jnp.einsum("qhd,qhd->hq", grad_heads.astype(jnp.float32), attended)


def query_back(queries, kv_whole, allowed_fn, logsum, row_delta, grad_heads):

    def query_grad_step(partial_value, block_start):
        allowed = allowed_fn(block_start)

        def query_compute_block(running):
            key_heads, value_heads = key_block(kv_whole, block_start)
            probs_full, grad_scores = score_grads(
                queries, key_heads, value_heads, grad_heads, logsum, row_delta, allowed
            )
            return running + jnp.einsum(
                "hqk,khd->qhd", grad_scores, key_heads, preferred_element_type=jnp.float32
            )

        return (
            lax.cond(jnp.any(allowed), query_compute_block, lambda running: running, partial_value),
            None,
        )

    grad_query, _ = lax.scan(
        query_grad_step, jnp.zeros(queries.shape, jnp.float32), block_starts(kv_whole)
    )
    return grad_query


def attend_back(queries, kv_whole, allowed_fn, attended, logsum, grad_heads):
    row_delta = row_deltas(grad_heads, attended)

    def attend_grad_step(grad_query, block_start):
        allowed = allowed_fn(block_start)

        def attend_compute_block(partial_value):
            key_heads, value_heads = key_block(kv_whole, block_start)
            probs_full, grad_scores = score_grads(
                queries, key_heads, value_heads, grad_heads, logsum, row_delta, allowed
            )
            partial_value = partial_value + jnp.einsum(
                "hqk,khd->qhd", grad_scores, key_heads, preferred_element_type=jnp.float32
            )
            grad_keys = jnp.einsum(
                "hqk,qhd->khd", grad_scores, queries, preferred_element_type=jnp.float32
            )
            grad_values = jnp.einsum(
                "hqk,qhd->khd",
                probs_full.astype(jnp.bfloat16),
                grad_heads,
                preferred_element_type=jnp.float32,
            )
            return (
                partial_value,
                jnp.concatenate(
                    [grad_keys.reshape(KBLOCK, -1), grad_values.reshape(KBLOCK, -1)], axis=1
                ),
            )

        def attend_skip_block(partial_value):
            return (partial_value, jnp.zeros((KBLOCK, kv_whole.shape[1]), jnp.float32))

        return lax.cond(jnp.any(allowed), attend_compute_block, attend_skip_block, grad_query)

    grad_query, kv_terms = lax.scan(
        attend_grad_step, jnp.zeros(queries.shape, jnp.float32), block_starts(kv_whole)
    )
    return (grad_query, kv_terms.reshape(kv_whole.shape[0], kv_whole.shape[1]))


def owners_end(grads):
    columns = jax.tree.map(
        lambda part: part.astype(jnp.float32),
        lax.psum_scatter(shortened(grads), "ctx", scatter_dimension=1, tiled=True),
    )
    return jax.tree.map(
        lambda part: part.astype(jnp.float32),
        lax.psum_scatter(shortened(columns), "fsdp", scatter_dimension=0, tiled=True),
    )


def per_device(
    tokens,
    encoded,
    grad_out,
    doc_lengths,
    src_lengths,
    norm_gain,
    norm_bias,
    w_qkv,
    self_bias,
    w_self_out,
    w_cross_q,
    w_cross_kv,
    cross_bias,
    w_cross_out,
    w_up,
    up_bias,
    w_down,
    down_bias,
):
    q_scale = 1.0 / math.sqrt(HEAD_DIM)
    tok_rows = tokens.shape[1]
    features = tokens.shape[2]
    ctx_count = lax.axis_size("ctx")
    ctx_index = lax.axis_index("ctx")
    own_rows = ctx_index * tok_rows + jnp.arange(tok_rows, dtype=jnp.int32)
    tok_pos = stream_position(own_rows, tok_rows, ctx_count)
    lengths_row = doc_lengths[0]
    doc_starts = jnp.cumsum(lengths_row) - lengths_row
    tok_doc = doc_index(doc_starts, tok_pos)
    src_row = src_lengths[0]
    src_ends = jnp.cumsum(src_row)
    src_starts = src_ends - src_row
    span_low = pick_doc(src_starts, tok_doc)
    span_high = pick_doc(src_ends, tok_doc)

    def self_mask(key_rows):
        key_pos = stream_position(key_rows, tok_rows, ctx_count)
        key_doc = doc_index(doc_starts, key_pos)
        return (key_pos[None, :] <= tok_pos[:, None]) & (key_doc[None, :] == tok_doc[:, None])

    def self_allowed(block_start):
        return self_mask(block_start + jnp.arange(KBLOCK, dtype=jnp.int32))

    def cross_allowed(block_start):
        key_pos = block_start + jnp.arange(KBLOCK, dtype=jnp.int32)
        return (key_pos[None, :] >= span_low[:, None]) & (key_pos[None, :] < span_high[:, None])

    def gather_self():
        return (
            lax.all_gather(w_qkv, "fsdp", axis=0, tiled=True),
            lax.all_gather(w_self_out, "fsdp", axis=0, tiled=True),
        )

    def gather_cross():
        return (
            lax.all_gather(w_cross_q, "fsdp", axis=0, tiled=True),
            lax.all_gather(w_cross_kv, "fsdp", axis=0, tiled=True),
            lax.all_gather(w_cross_out, "fsdp", axis=0, tiled=True),
        )

    def gather_mlp():
        return (
            lax.all_gather(w_up, "fsdp", axis=0, tiled=True),
            lax.all_gather(w_down, "fsdp", axis=0, tiled=True),
        )

    tok_f32 = tokens[0].astype(jnp.float32)
    enc_low = encoded[0]
    ln_one, normed_one, inverse_one = layer_norm(tok_f32, norm_gain[0], norm_bias[0])
    act_one = ln_one.astype(jnp.bfloat16)
    full_qkv, full_self_out = gather_self()
    projected = plain_dot(act_one, full_qkv)
    q_self = ((projected[:, :features] + self_bias[0]) * q_scale).astype(jnp.bfloat16)
    kv_self = jnp.concatenate(
        [projected[:, features : 2 * features], projected[:, 2 * features :] + self_bias[1]], axis=1
    ).astype(jnp.bfloat16)
    kv_self_all = lax.all_gather(kv_self, "ctx", axis=0, tiled=True)
    self_heads = split_heads(q_self)
    att_self, lse_self = attend(self_heads, kv_self_all, self_allowed)
    att_self_low = att_self.reshape(tok_rows, features).astype(jnp.bfloat16)
    hidden_one = tok_f32 + plain_dot(att_self_low, full_self_out) + self_bias[2]
    ln_two, normed_two, inverse_two = layer_norm(hidden_one, norm_gain[1], norm_bias[1])
    act_two = ln_two.astype(jnp.bfloat16)
    full_cross_q, full_cross_kv, full_cross_out = gather_cross()
    q_cross = ((plain_dot(act_two, full_cross_q) + cross_bias[0]) * q_scale).astype(jnp.bfloat16)
    src_proj = plain_dot(enc_low, full_cross_kv)
    kv_cross = jnp.concatenate(
        [src_proj[:, :features], src_proj[:, features:] + cross_bias[1]], axis=1
    ).astype(jnp.bfloat16)
    kv_cross_all = lax.all_gather(kv_cross, "ctx", axis=0, tiled=True)
    cross_heads = split_heads(q_cross)
    att_cross, lse_cross = attend(cross_heads, kv_cross_all, cross_allowed)
    att_cross_low = att_cross.reshape(tok_rows, features).astype(jnp.bfloat16)
    hidden_two = hidden_one + plain_dot(att_cross_low, full_cross_out) + cross_bias[2]
    ln_three, normed_three, inverse_three = layer_norm(hidden_two, norm_gain[2], norm_bias[2])
    act_three = ln_three.astype(jnp.bfloat16)
    full_up, full_down = gather_mlp()
    pre_act = plain_dot(act_three, full_up) + up_bias
    gelu_low = gelu_value(pre_act).astype(jnp.bfloat16)
    layer_out = (hidden_two + plain_dot(gelu_low, full_down) + down_bias).astype(jnp.bfloat16)
    upstream = grad_out[0].astype(jnp.float32)
    down_grad_low = grad_out[0]
    full_up, full_down = gather_mlp()
    grad_w_down = outer_rows(gelu_low, down_grad_low)
    grad_down_bias = jnp.sum(upstream, axis=0)
    gelu_grad = times_transpose(down_grad_low, full_down)
    pre_grad_low = (gelu_grad * gelu_slope(pre_act)).astype(jnp.bfloat16)
    grad_w_up = outer_rows(act_three, pre_grad_low)
    grad_up_bias = jnp.sum(pre_grad_low.astype(jnp.float32), axis=0)
    norm_in_three, gain_grad_three, shift_grad_three = norm_back(
        times_transpose(pre_grad_low, full_up), normed_three, inverse_three, norm_gain[2]
    )
    grad_two = upstream + norm_in_three
    full_cross_q, full_cross_kv, full_cross_out = gather_cross()
    cross_grad_low = grad_two.astype(jnp.bfloat16)
    grad_w_cross_out = outer_rows(att_cross_low, cross_grad_low)
    cross_out_bias_grad = jnp.sum(cross_grad_low.astype(jnp.float32), axis=0)
    cross_att_grad = split_heads(
        times_transpose(cross_grad_low, full_cross_out).astype(jnp.bfloat16)
    )
    cross_q_grad, cross_kv_terms = attend_back(
        cross_heads, kv_cross_all, cross_allowed, att_cross, lse_cross, cross_att_grad
    )
    cross_kv_grad = lax.psum_scatter(
        cross_kv_terms.astype(jnp.bfloat16), "ctx", scatter_dimension=0, tiled=True
    )
    cross_q_low = (cross_q_grad.reshape(tok_rows, features) * q_scale).astype(jnp.bfloat16)
    grad_w_cross_q = outer_rows(act_two, cross_q_low)
    cross_q_bias_grad = jnp.sum(cross_q_low.astype(jnp.float32), axis=0)
    grad_w_cross_kv = outer_rows(enc_low, cross_kv_grad)
    cross_v_bias_grad = jnp.sum(cross_kv_grad[:, features:].astype(jnp.float32), axis=0)
    grad_encoded = times_transpose(cross_kv_grad, full_cross_kv)
    norm_in_two, gain_grad_two, shift_grad_two = norm_back(
        times_transpose(cross_q_low, full_cross_q), normed_two, inverse_two, norm_gain[1]
    )
    grad_one = grad_two + norm_in_two
    full_qkv, full_self_out = gather_self()
    self_grad_low = grad_one.astype(jnp.bfloat16)
    grad_w_self_out = outer_rows(att_self_low, self_grad_low)
    self_out_bias_grad = jnp.sum(self_grad_low.astype(jnp.float32), axis=0)
    self_att_flat = times_transpose(self_grad_low, full_self_out).astype(jnp.bfloat16)
    self_att_grad = split_heads(self_att_flat)
    self_delta = row_deltas(self_att_grad, att_self)
    self_q_grad = query_back(
        self_heads, kv_self_all, self_allowed, lse_self, self_delta, self_att_grad
    )

    def one_piece(sub_start):
        key_rows = sub_start + jnp.arange(tok_rows, dtype=jnp.int32)
        allowed = self_mask(key_rows)

        def one_compute_block(piece_start):
            key_heads, value_heads = split_pair(
                lax.dynamic_slice_in_dim(kv_self_all, piece_start, tok_rows, 0)
            )
            return key_terms(
                self_heads, key_heads, value_heads, self_att_grad, lse_self, self_delta, allowed
            )

        def one_skip_block(piece_start):
            return jnp.zeros((tok_rows, 2 * features), jnp.float32)

        return lax.cond(jnp.any(allowed), one_compute_block, one_skip_block, sub_start)

    piece_starts = (
        jnp.arange(tok_rows * lax.axis_size("ctx") // tok_rows, dtype=jnp.int32) * tok_rows
    )
    self_kv_grad = lax.psum_scatter(
        lax.map(one_piece, piece_starts)
        .reshape(tok_rows * lax.axis_size("ctx"), 2 * features)
        .astype(jnp.bfloat16),
        "ctx",
        scatter_dimension=0,
        tiled=True,
    )
    self_q_low = (self_q_grad.reshape(tok_rows, features) * q_scale).astype(jnp.bfloat16)
    proj_grad_low = jnp.concatenate([self_q_low, self_kv_grad], axis=1)
    grad_w_qkv = outer_rows(act_one, proj_grad_low)
    self_q_bias_grad = jnp.sum(self_q_low.astype(jnp.float32), axis=0)
    self_v_bias_grad = jnp.sum(self_kv_grad[:, features:].astype(jnp.float32), axis=0)
    norm_in_one, gain_grad_one, shift_grad_one = norm_back(
        times_transpose(proj_grad_low, full_qkv), normed_one, inverse_one, norm_gain[0]
    )
    grad_tokens = grad_one + norm_in_one
    owned = owners_end(
        (
            grad_w_qkv,
            grad_w_self_out,
            grad_w_cross_q,
            grad_w_cross_kv,
            grad_w_cross_out,
            grad_w_up,
            grad_w_down,
        )
    )
    gain_grads = jnp.stack([gain_grad_one, gain_grad_two, gain_grad_three])
    shift_grads = jnp.stack([shift_grad_one, shift_grad_two, shift_grad_three])
    self_bias_grads = jnp.stack([self_q_bias_grad, self_v_bias_grad, self_out_bias_grad])
    cross_bias_grads = jnp.stack([cross_q_bias_grad, cross_v_bias_grad, cross_out_bias_grad])
    summed = lax.psum(
        (gain_grads, shift_grads, self_bias_grads, cross_bias_grads, grad_up_bias, grad_down_bias),
        ("ctx", "fsdp"),
    )
    return (
        layer_out[None],
        grad_tokens[None],
        grad_encoded[None],
        summed[0],
        summed[1],
        owned[0],
        summed[2],
        owned[1],
        owned[2],
        owned[3],
        summed[3],
        owned[4],
        owned[5],
        summed[4],
        owned[6],
        summed[5],
    )


def general_solution(mesh):
    placed = (
        P("fsdp", "ctx", None),
        P("fsdp", "ctx", None),
        P("fsdp", "ctx", None),
        P("fsdp", None),
        P("fsdp", None),
        P(),
        P(),
        P("fsdp", None),
        P(),
        P("fsdp", None),
        P("fsdp", None),
        P("fsdp", None),
        P(),
        P("fsdp", None),
        P("fsdp", None),
        P(),
        P("fsdp", None),
        P(),
    )
    return jax.shard_map(
        per_device,
        mesh=mesh,
        in_specs=placed,
        out_specs=(
            P("fsdp", "ctx", None),
            P("fsdp", "ctx", None),
            P("fsdp", "ctx", None),
            P(),
            P(),
            P("fsdp", "ctx"),
            P(),
            P("fsdp", "ctx"),
            P("fsdp", "ctx"),
            P("fsdp", "ctx"),
            P(),
            P("fsdp", "ctx"),
            P("fsdp", "ctx"),
            P(),
            P("fsdp", "ctx"),
            P(),
        ),
        check_vma=False,
    )


CTX = ("cz", "cy")
FSDP = ("fx", "fc")
PLANE = ("fx", "fc", "cy")
ALL = ("cz", "cy", "fx", "fc")
ROW_BLOCK = 512
HIDDEN_BLOCK = 256
QBLOCK = 256
HALF = 128
PAIR = 2 * HEAD_DIM
MAX_KEY_BLOCKS = 5


def kernel_cost(microseconds):
    return pl.CostEstimate(
        flops=int(microseconds * 1.15e9), bytes_accessed=1 << 20, transcendentals=0
    )


def row_major(value):
    return with_layout_constraint(value, Layout(tuple(range(value.ndim))))


def doc_start_of(starts_ref, positions):
    first = jnp.zeros_like(positions)
    for doc in range(starts_ref.shape[0]):
        begin = starts_ref[doc]
        first = jnp.where(positions >= begin, begin, first)
    return first


def doc_start_scalar(starts_ref, position):
    first = jnp.int32(0)
    for doc in range(starts_ref.shape[0]):
        begin = starts_ref[doc]
        first = jnp.where(position >= begin, begin, first)
    return first


def half_row(pos_block, pos_blocks):
    early = pos_block * (2 * HALF)
    late = (pos_blocks - 1 - pos_block) * (2 * HALF) + HALF
    return pl.multiple_of(jnp.where(2 * pos_block < pos_blocks, early, late), HALF)


def slot_of(distance):
    return (distance & 1) + 2 * ((distance >> 2) & 1) + 4 * ((distance >> 1) & 1)


def slot_row(row, own):
    block = row // (2 * HALF)
    slot = slot_of(block ^ own)
    return pl.multiple_of(slot * (2 * HALF) + row - block * (2 * HALF), HALF)


def lane_mask(rows, head):
    lanes = lax.broadcasted_iota(jnp.int32, (rows, PAIR), 1)
    return (lanes >= head * HEAD_DIM) & (lanes < (head + 1) * HEAD_DIM)


def to_positions(own, src_ref, column, dst_ref):
    pos_blocks = src_ref.shape[0] // HALF

    def move(block, carry):
        row = slot_row(half_row(block, pos_blocks), own)
        dst_ref[pl.ds(pl.multiple_of(block * HALF, HALF), HALF), :] = src_ref[
            pl.ds(row, HALF), pl.ds(column, PAIR)
        ]
        return carry

    lax.fori_loop(0, pos_blocks, move, 0)


def self_forward_kernel(starts_ref, own_ref, qkv_ref, out_ref, key_ref, value_ref):
    step = pl.program_id(0)
    own = own_ref[0]
    pos_blocks = qkv_ref.shape[0] // HALF

    @pl.when(step == 0)
    def _():
        to_positions(own, qkv_ref, PAIR, key_ref)
        to_positions(own, qkv_ref, 2 * PAIR, value_ref)

    row_a = half_row(2 * step, pos_blocks)
    row_b = half_row(2 * step + 1, pos_blocks)
    slot_a, slot_b = slot_row(row_a, own), slot_row(row_b, own)
    queries = jnp.concatenate(
        [qkv_ref[pl.ds(slot_a, HALF), pl.ds(0, PAIR)], qkv_ref[pl.ds(slot_b, HALF), pl.ds(0, PAIR)]],
        axis=0,
    )
    q_start = step * QBLOCK
    first_block = doc_start_scalar(starts_ref, q_start) // QBLOCK
    count = step - first_block + 1
    q_pos = q_start + lax.broadcasted_iota(jnp.int32, (QBLOCK, 1), 0)
    q_first = doc_start_of(starts_ref, q_pos)

    def compute(blocks):
        width = blocks * QBLOCK
        k_start = pl.multiple_of(first_block * QBLOCK, QBLOCK)
        keys = key_ref[pl.ds(k_start, width), :]
        values = value_ref[pl.ds(k_start, width), :]
        k_pos = k_start + lax.broadcasted_iota(jnp.int32, (QBLOCK, width), 1)
        allowed = (k_pos >= q_first) & (k_pos <= q_pos)
        parts = []
        for head in range(2):
            picked = jnp.where(lane_mask(QBLOCK, head), queries, jnp.zeros_like(queries))
            scores = lax.dot_general(picked, keys, CONTRACT_COLS, preferred_element_type=jnp.float32)
            scores = jnp.where(allowed, scores, NEG)
            terms = jnp.exp(scores - jnp.max(scores, axis=1, keepdims=True))
            inverse = 1.0 / jnp.sum(terms, axis=1, keepdims=True)
            mixed = jnp.dot(
                (terms * inverse).astype(jnp.bfloat16), values, preferred_element_type=jnp.float32
            )
            parts.append(mixed)
        result = jnp.where(lane_mask(QBLOCK, 0), parts[0], parts[1]).astype(jnp.bfloat16)
        out_ref[pl.ds(row_a, HALF), :] = result[:HALF]
        out_ref[pl.ds(row_b, HALF), :] = result[HALF:]

    for blocks in range(1, MAX_KEY_BLOCKS + 1):
        pl.when(count == blocks)(functools.partial(compute, blocks))


def self_backward_kernel(
    starts_ref,
    own_ref,
    qkv_ref,
    grad_ref,
    slot_ref,
    key_ref,
    value_ref,
    dkey_ref,
    dvalue_ref,
):
    step = pl.program_id(0)
    own = own_ref[0]
    pos_blocks = qkv_ref.shape[0] // HALF

    @pl.when(step == 0)
    def _():
        to_positions(own, qkv_ref, PAIR, key_ref)
        to_positions(own, qkv_ref, 2 * PAIR, value_ref)
        dkey_ref[...] = jnp.zeros_like(dkey_ref)
        dvalue_ref[...] = jnp.zeros_like(dvalue_ref)

    row_a = half_row(2 * step, pos_blocks)
    row_b = half_row(2 * step + 1, pos_blocks)
    slot_a, slot_b = slot_row(row_a, own), slot_row(row_b, own)
    queries = jnp.concatenate(
        [qkv_ref[pl.ds(slot_a, HALF), pl.ds(0, PAIR)], qkv_ref[pl.ds(slot_b, HALF), pl.ds(0, PAIR)]],
        axis=0,
    )
    grads = jnp.concatenate([grad_ref[pl.ds(row_a, HALF), :], grad_ref[pl.ds(row_b, HALF), :]], axis=0)
    q_start = step * QBLOCK
    first_block = doc_start_scalar(starts_ref, q_start) // QBLOCK
    count = step - first_block + 1
    q_pos = q_start + lax.broadcasted_iota(jnp.int32, (1, QBLOCK), 1)
    q_first = doc_start_of(starts_ref, q_pos)

    def compute(blocks):
        width = blocks * QBLOCK
        k_start = pl.multiple_of(first_block * QBLOCK, QBLOCK)
        keys = key_ref[pl.ds(k_start, width), :]
        values = value_ref[pl.ds(k_start, width), :]
        k_pos = k_start + lax.broadcasted_iota(jnp.int32, (width, QBLOCK), 0)
        allowed = (k_pos >= q_first) & (k_pos <= q_pos)
        dq_parts = []
        dkey = jnp.zeros((width, PAIR), jnp.float32)
        dvalue = jnp.zeros((width, PAIR), jnp.float32)
        for head in range(2):
            inside = lane_mask(QBLOCK, head)
            picked = jnp.where(inside, queries, jnp.zeros_like(queries))
            grad = jnp.where(inside, grads, jnp.zeros_like(grads))
            scores = lax.dot_general(keys, picked, CONTRACT_COLS, preferred_element_type=jnp.float32)
            scores = jnp.where(allowed, scores, NEG)
            terms = jnp.exp(scores - jnp.max(scores, axis=0, keepdims=True))
            probs = terms * (1.0 / jnp.sum(terms, axis=0, keepdims=True))
            dprobs = lax.dot_general(
                values, grad, CONTRACT_COLS, preferred_element_type=jnp.float32
            )
            delta = jnp.sum(probs * dprobs, axis=0, keepdims=True)
            dscores = (probs * (dprobs - delta)).astype(jnp.bfloat16)
            dq_parts.append(
                lax.dot_general(dscores, keys, CONTRACT_ROWS, preferred_element_type=jnp.float32)
            )
            dkey = dkey + jnp.dot(dscores, picked, preferred_element_type=jnp.float32)
            dvalue = dvalue + jnp.dot(
                probs.astype(jnp.bfloat16), grad, preferred_element_type=jnp.float32
            )
        dkey_ref[pl.ds(k_start, width), :] += dkey
        dvalue_ref[pl.ds(k_start, width), :] += dvalue
        dq = jnp.where(lane_mask(QBLOCK, 0), dq_parts[0], dq_parts[1])
        dq = (dq * (1.0 / math.sqrt(HEAD_DIM))).astype(jnp.bfloat16)
        slot_ref[pl.ds(slot_a, HALF), pl.ds(0, PAIR)] = dq[:HALF]
        slot_ref[pl.ds(slot_b, HALF), pl.ds(0, PAIR)] = dq[HALF:]

    for blocks in range(1, MAX_KEY_BLOCKS + 1):
        pl.when(count == blocks)(functools.partial(compute, blocks))

    @pl.when(step == pl.num_programs(0) - 1)
    def _():
        def move(block, carry):
            slot = slot_row(half_row(block, pos_blocks), own)
            place = pl.ds(pl.multiple_of(block * HALF, HALF), HALF)
            dkey = dkey_ref[place, :].astype(jnp.bfloat16)
            dvalue = dvalue_ref[place, :].astype(jnp.bfloat16)
            slot_ref[pl.ds(slot, HALF), pl.ds(PAIR, PAIR)] = dkey
            slot_ref[pl.ds(slot, HALF), pl.ds(2 * PAIR, PAIR)] = dvalue
            return carry

        lax.fori_loop(0, pos_blocks, move, 0)


def cross_forward_kernel(q_ref, key_ref, value_ref, low_ref, high_ref, out_ref):
    rows, width = q_ref.shape[0], key_ref.shape[1]
    queries, keys, values = q_ref[...], key_ref[0], value_ref[0]
    k_pos = lax.broadcasted_iota(jnp.int32, (rows, width), 1)
    allowed = (k_pos >= low_ref[...]) & (k_pos < high_ref[...])
    parts = []
    for head in range(2):
        picked = jnp.where(lane_mask(rows, head), queries, jnp.zeros_like(queries))
        scores = lax.dot_general(picked, keys, CONTRACT_COLS, preferred_element_type=jnp.float32)
        scores = jnp.where(allowed, scores, NEG)
        terms = jnp.exp(scores - jnp.max(scores, axis=1, keepdims=True))
        inverse = 1.0 / jnp.sum(terms, axis=1, keepdims=True)
        parts.append(
            jnp.dot((terms * inverse).astype(jnp.bfloat16), values, preferred_element_type=jnp.float32)
        )
    out_ref[...] = jnp.where(lane_mask(rows, 0), parts[0], parts[1]).astype(jnp.bfloat16)


def cross_backward_kernel(q_ref, key_ref, value_ref, grad_ref, low_ref, high_ref, dq_ref, dkv_ref):
    rows, width = q_ref.shape[0], key_ref.shape[1]
    queries, keys, values, grads = q_ref[...], key_ref[0], value_ref[0], grad_ref[...]
    k_pos = lax.broadcasted_iota(jnp.int32, (width, rows), 0)
    allowed = (k_pos >= low_ref[...]) & (k_pos < high_ref[...])
    dq_parts = []
    dkey = jnp.zeros((width, PAIR), jnp.float32)
    dvalue = jnp.zeros((width, PAIR), jnp.float32)
    for head in range(2):
        inside = lane_mask(rows, head)
        picked = jnp.where(inside, queries, jnp.zeros_like(queries))
        grad = jnp.where(inside, grads, jnp.zeros_like(grads))
        scores = lax.dot_general(keys, picked, CONTRACT_COLS, preferred_element_type=jnp.float32)
        scores = jnp.where(allowed, scores, NEG)
        terms = jnp.exp(scores - jnp.max(scores, axis=0, keepdims=True))
        probs = terms * (1.0 / jnp.sum(terms, axis=0, keepdims=True))
        dprobs = lax.dot_general(values, grad, CONTRACT_COLS, preferred_element_type=jnp.float32)
        delta = jnp.sum(probs * dprobs, axis=0, keepdims=True)
        dscores = (probs * (dprobs - delta)).astype(jnp.bfloat16)
        dq_parts.append(
            lax.dot_general(dscores, keys, CONTRACT_ROWS, preferred_element_type=jnp.float32)
        )
        dkey = dkey + jnp.dot(dscores, picked, preferred_element_type=jnp.float32)
        dvalue = dvalue + jnp.dot(
            probs.astype(jnp.bfloat16), grad, preferred_element_type=jnp.float32
        )
    dq = jnp.where(lane_mask(rows, 0), dq_parts[0], dq_parts[1])
    dq_ref[...] = (dq * (1.0 / math.sqrt(HEAD_DIM))).astype(jnp.bfloat16)
    dkv_ref[0, 0] = dkey.astype(jnp.bfloat16)
    dkv_ref[1, 0] = dvalue.astype(jnp.bfloat16)


def kernel_params():
    return pltpu.CompilerParams(vmem_limit_bytes=48 * 1024 * 1024)


def self_forward(doc_starts, own, qkv):
    rows = qkv.shape[0]
    return pl.pallas_call(
        self_forward_kernel,
        grid=(rows // QBLOCK,),
        in_specs=[
            pl.BlockSpec(memory_space=pltpu.SMEM),
            pl.BlockSpec(memory_space=pltpu.SMEM),
            pl.BlockSpec((rows, 3 * PAIR), lambda step: (0, 0)),
        ],
        out_specs=pl.BlockSpec((rows, PAIR), lambda step: (0, 0)),
        out_shape=jax.ShapeDtypeStruct((rows, PAIR), jnp.bfloat16),
        scratch_shapes=[pltpu.VMEM((rows, PAIR), jnp.bfloat16)] * 2,
        compiler_params=kernel_params(),
        cost_estimate=kernel_cost(1),
    )(doc_starts, own, qkv)


def self_backward(doc_starts, own, qkv, grads):
    rows = qkv.shape[0]
    return pl.pallas_call(
        self_backward_kernel,
        grid=(rows // QBLOCK,),
        in_specs=[
            pl.BlockSpec(memory_space=pltpu.SMEM),
            pl.BlockSpec(memory_space=pltpu.SMEM),
            pl.BlockSpec((rows, 3 * PAIR), lambda step: (0, 0)),
            pl.BlockSpec((rows, PAIR), lambda step: (0, 0)),
        ],
        out_specs=pl.BlockSpec((rows, 3 * PAIR), lambda step: (0, 0)),
        out_shape=jax.ShapeDtypeStruct((rows, 3 * PAIR), jnp.bfloat16),
        scratch_shapes=[pltpu.VMEM((rows, PAIR), jnp.bfloat16)] * 2
        + [pltpu.VMEM((rows, PAIR), jnp.float32)] * 2,
        compiler_params=kernel_params(),
        cost_estimate=kernel_cost(1),
    )(doc_starts, own, qkv, grads)


def cross_forward(queries, kv_cross, span_low, span_high):
    rows, features = queries.shape
    pairs = features // PAIR
    src = kv_cross.shape[1]
    return pl.pallas_call(
        cross_forward_kernel,
        grid=(pairs,),
        in_specs=[
            pl.BlockSpec((rows, PAIR), lambda p: (0, p)),
            pl.BlockSpec((1, src, PAIR), lambda p: (p // 2, 0, p % 2)),
            pl.BlockSpec((1, src, PAIR), lambda p: (p // 2 + pairs // 2, 0, p % 2)),
            pl.BlockSpec((rows, 1), lambda p: (0, 0)),
            pl.BlockSpec((rows, 1), lambda p: (0, 0)),
        ],
        out_specs=pl.BlockSpec((rows, PAIR), lambda p: (0, p)),
        out_shape=jax.ShapeDtypeStruct((rows, features), jnp.bfloat16),
        compiler_params=kernel_params(),
        cost_estimate=kernel_cost(1),
    )(queries, kv_cross, kv_cross, span_low[:, None], span_high[:, None])


def cross_backward(queries, kv_cross, grads, span_low, span_high):
    rows, features = queries.shape
    pairs = features // PAIR
    src = kv_cross.shape[1]
    return pl.pallas_call(
        cross_backward_kernel,
        grid=(pairs,),
        in_specs=[
            pl.BlockSpec((rows, PAIR), lambda p: (0, p)),
            pl.BlockSpec((1, src, PAIR), lambda p: (p // 2, 0, p % 2)),
            pl.BlockSpec((1, src, PAIR), lambda p: (p // 2 + pairs // 2, 0, p % 2)),
            pl.BlockSpec((rows, PAIR), lambda p: (0, p)),
            pl.BlockSpec((1, rows), lambda p: (0, 0)),
            pl.BlockSpec((1, rows), lambda p: (0, 0)),
        ],
        out_specs=[
            pl.BlockSpec((rows, PAIR), lambda p: (0, p)),
            pl.BlockSpec((2, 1, src, PAIR), lambda p: (0, p, 0, 0)),
        ],
        out_shape=[
            jax.ShapeDtypeStruct((rows, features), jnp.bfloat16),
            jax.ShapeDtypeStruct((2, pairs, src, PAIR), jnp.bfloat16),
        ],
        compiler_params=kernel_params(),
        cost_estimate=kernel_cost(1),
    )(queries, kv_cross, kv_cross, grads, span_low[None, :], span_high[None, :])


def mlp_kernel(act_ref, grad_ref, up_ref, down_ref, bias_ref, gelu_ref, pre_ref, out_ref, sum_ref):
    @pl.when(pl.program_id(0) == 0)
    def _():
        sum_ref[...] = jnp.zeros_like(sum_ref)

    act, grad = act_ref[...], grad_ref[...]
    total = jnp.zeros(out_ref.shape, jnp.float32)
    for begin in range(0, up_ref.shape[1], HIDDEN_BLOCK):
        place = pl.ds(begin, HIDDEN_BLOCK)
        pre = jnp.dot(act, up_ref[:, place], preferred_element_type=jnp.float32) + bias_ref[:, place]
        square = pre * pre
        tangent = jnp.tanh(GELU_C * (pre + GELU_A * pre * square))
        half = 0.5 * (1.0 + tangent)
        gelu_ref[:, place] = (pre * half).astype(jnp.bfloat16)
        slope = half + 0.5 * pre * (1.0 - tangent * tangent) * (
            GELU_C + (3.0 * GELU_A * GELU_C) * square
        )
        back = lax.dot_general(
            grad, down_ref[place, :], CONTRACT_COLS, preferred_element_type=jnp.float32
        )
        pre_grad = (back * slope).astype(jnp.bfloat16)
        pre_ref[:, place] = pre_grad
        sum_ref[:, place] += jnp.sum(pre_grad.astype(jnp.float32), axis=0, keepdims=True)
        total = total + lax.dot_general(
            pre_grad, up_ref[:, place], CONTRACT_COLS, preferred_element_type=jnp.float32
        )
    out_ref[...] = total.astype(jnp.bfloat16)


def mlp_forward_back(act, grad, up_own, down_own, bias_own):
    rows, features = act.shape
    hidden = up_own.shape[1]
    return pl.pallas_call(
        mlp_kernel,
        grid=(rows // ROW_BLOCK,),
        in_specs=[
            pl.BlockSpec((ROW_BLOCK, features), lambda step: (step, 0)),
            pl.BlockSpec((ROW_BLOCK, features), lambda step: (step, 0)),
            pl.BlockSpec((features, hidden), lambda step: (0, 0)),
            pl.BlockSpec((hidden, features), lambda step: (0, 0)),
            pl.BlockSpec((1, hidden), lambda step: (0, 0)),
        ],
        out_specs=[
            pl.BlockSpec((ROW_BLOCK, hidden), lambda step: (step, 0)),
            pl.BlockSpec((ROW_BLOCK, hidden), lambda step: (step, 0)),
            pl.BlockSpec((ROW_BLOCK, features), lambda step: (step, 0)),
            pl.BlockSpec((1, hidden), lambda step: (0, 0)),
        ],
        out_shape=[
            jax.ShapeDtypeStruct((rows, hidden), jnp.bfloat16),
            jax.ShapeDtypeStruct((rows, hidden), jnp.bfloat16),
            jax.ShapeDtypeStruct((rows, features), jnp.bfloat16),
            jax.ShapeDtypeStruct((1, hidden), jnp.float32),
        ],
        compiler_params=kernel_params(),
        cost_estimate=kernel_cost(1),
    )(act, grad, up_own, down_own, bias_own)


def outer_kernel(left_ref, right_ref, left_two_ref, right_two_ref, out_ref, total_ref):
    step = pl.program_id(0)
    half = pl.num_programs(0) // 2

    def add(left, right):
        total_ref[...] += lax.dot_general(
            left[...], right[...], CONTRACT_ROWS, preferred_element_type=jnp.float32
        )

    @pl.when(step == 0)
    def _():
        total_ref[...] = jnp.zeros_like(total_ref)

    pl.when(step < half)(lambda: add(left_ref, right_ref))
    pl.when(step >= half)(lambda: add(left_two_ref, right_two_ref))

    @pl.when(step == 2 * half - 1)
    def _():
        out_ref[...] = total_ref[...].astype(out_ref.dtype)


def outer_pair(left, right, left_two, right_two):
    rows, width = left.shape
    columns = right.shape[1]
    half = rows // ROW_BLOCK
    first = lambda step: (jnp.minimum(step, half - 1), 0)
    second = lambda step: (jnp.maximum(step - half, 0), 0)
    return pl.pallas_call(
        outer_kernel,
        grid=(2 * half,),
        in_specs=[
            pl.BlockSpec((ROW_BLOCK, width), first),
            pl.BlockSpec((ROW_BLOCK, columns), first),
            pl.BlockSpec((ROW_BLOCK, width), second),
            pl.BlockSpec((ROW_BLOCK, columns), second),
        ],
        out_specs=pl.BlockSpec((width, columns), lambda step: (0, 0)),
        out_shape=jax.ShapeDtypeStruct((width, columns), jnp.bfloat16),
        scratch_shapes=[pltpu.VMEM((width, columns), jnp.float32)],
        compiler_params=kernel_params(),
        cost_estimate=kernel_cost(1),
    )(left, right, left_two, right_two)


def square_grads_kernel(core_ref, *refs):
    step = pl.program_id(0)
    side, x = step // 2, step % 2
    core = jnp.where(side == 0, 1 - core_ref[0], core_ref[0])
    pairs, (send_ref, keep_ref) = refs[:-2], refs[-2:]
    n_y, n_z, _, rows, width = send_ref.shape[1:]
    begin = pl.multiple_of((2 * x + core) * rows, rows)

    def compute(out_ref):
        for which in range(len(pairs) // 2):
            grad = lax.dot_general(
                pairs[2 * which][:, pl.ds(begin, rows)],
                pairs[2 * which + 1][...],
                CONTRACT_ROWS,
                preferred_element_type=jnp.float32,
            ).astype(jnp.bfloat16)
            for y in range(n_y):
                for z in range(n_z):
                    source = (z * n_y + y) * width
                    out_ref[0, y, z, which] = grad[:, source : source + width]

    pl.when(side == 0)(lambda: compute(send_ref))
    pl.when(side == 1)(lambda: compute(keep_ref))


def square_grads(core, pairs, n_y, n_z):
    flat = [array for pair in pairs for array in pair]
    tokens, features = flat[0].shape
    rows = features // 4
    block = (1, n_y, n_z, len(pairs), rows, features // (n_y * n_z))
    shape = jax.ShapeDtypeStruct((2,) + block[1:], jnp.bfloat16)
    return pl.pallas_call(
        square_grads_kernel,
        grid=(4,),
        in_specs=[pl.BlockSpec(memory_space=pltpu.SMEM)]
        + [pl.BlockSpec((tokens, features), lambda step: (0, 0))] * len(flat),
        out_specs=[
            pl.BlockSpec(block, lambda step: (jnp.minimum(step, 1), 0, 0, 0, 0, 0)),
            pl.BlockSpec(block, lambda step: (jnp.maximum(step - 2, 0), 0, 0, 0, 0, 0)),
        ],
        out_shape=[shape, shape],
        compiler_params=kernel_params(),
        cost_estimate=kernel_cost(15),
    )(core, *flat)


tie = lax.optimization_barrier


def low(value):
    return value.astype(jnp.bfloat16)


def wide(value):
    return value.astype(jnp.float32)


def plus(left, right):
    return low(wide(left) + wide(right))


def over(axis, distance, value):
    count = lax.axis_size(axis)
    return lax.ppermute(value, axis, [(i, i ^ distance) for i in range(count)])


def over_core(value):
    return over("fc", 1, value)


def over_x(value):
    return over("fx", 1, value)


def over_y(value):
    return over("cy", 1, value)


def trade_places(value):
    n_z, n_y, n_f = lax.axis_size("cz"), lax.axis_size("cy"), lax.axis_size(FSDP)
    pairs = [
        ((z * n_y + y) * n_f + f, (f * n_y + y) * n_f + z)
        for z in range(n_z)
        for y in range(n_y)
        for f in range(n_f)
    ]
    return lax.ppermute(value, ALL, pairs)


def at(value, index, axis):
    return lax.dynamic_index_in_dim(value, index, axis, keepdims=False)


def pack_kernel(index_ref, *refs):
    begin = 0
    for ref in refs[:-1]:
        size = ref.shape[1]
        refs[-1][:, begin : begin + size] = ref[...]
        begin += size


def swap_columns(w_qkv, w_cross_kv, w_up):
    own, me_y, n_y = lax.axis_index(FSDP), lax.axis_index("cy"), lax.axis_size("cy")
    rows = w_up.shape[0]
    count = lax.axis_size(FSDP) * n_y
    owners = jnp.stack([(own ^ distance) * n_y + me_y for distance in (2, 3, 1, 0)])
    sizes = [PAIR] * 3 + [w_cross_kv.shape[1] // count, w_up.shape[1] // count]
    pieces = pl.pallas_call(
        pack_kernel,
        grid_spec=pltpu.PrefetchScalarGridSpec(
            num_scalar_prefetch=1,
            grid=(4,),
            in_specs=[
                pl.BlockSpec(
                    (rows, PAIR), lambda step, index, part=part: (0, part * count + index[step])
                )
                for part in range(3)
            ]
            + [pl.BlockSpec((rows, size), lambda step, index: (0, index[step])) for size in sizes[3:]],
            out_specs=pl.BlockSpec((rows, sum(sizes)), lambda step, index: (step, 0)),
        ),
        out_shape=jax.ShapeDtypeStruct((4 * rows, sum(sizes)), w_up.dtype),
        compiler_params=kernel_params(),
        cost_estimate=kernel_cost(1),
    )(owners.astype(jnp.int32), w_qkv, w_qkv, w_qkv, w_cross_kv, w_up)
    from_x = over_x(pieces[: 2 * rows])
    from_core = over_core(
        row_major(jnp.concatenate([pieces[2 * rows : 3 * rows], from_x[rows:]], axis=0))
    )
    return [pieces[3 * rows :], from_core[:rows], from_x[:rows], from_core[rows:]]


def rows_in_order(pieces, begin, size):
    own = lax.axis_index(FSDP)
    rows = pieces[0].shape[0]
    whole = jnp.zeros((len(pieces) * rows, size), pieces[0].dtype)
    for distance, piece in enumerate(pieces):
        whole = lax.dynamic_update_slice_in_dim(
            whole, piece[:, begin : begin + size], (own ^ distance) * rows, 0
        )
    return whole


def gather_rows(shard):
    own, me_y = lax.axis_index(FSDP), lax.axis_index("cy")
    rows, columns = shard.shape
    half = rows // 2
    from_x = over_x(lax.dynamic_slice_in_dim(shard, me_y * half, half, 0))
    from_y = over_y(from_x)
    both = jnp.concatenate(
        [shard, jnp.where(me_y == 0, from_x, from_y), jnp.where(me_y == 0, from_y, from_x)], axis=0
    )
    from_core = over_core(row_major(both))
    whole = jnp.zeros((4 * rows, columns), shard.dtype)
    for distance, piece in (
        (0, both[:rows]),
        (2, both[rows:]),
        (1, from_core[:rows]),
        (3, from_core[rows:]),
    ):
        whole = lax.dynamic_update_slice_in_dim(whole, piece, (own ^ distance) * rows, 0)
    return whole


def gather_rest(block, from_y, from_x):
    half = block.shape[0] // 2
    top = over_x(from_y[:half])
    bottom = over_y(from_x[half:])
    mine = jnp.concatenate([block, from_y, from_x, top, bottom], axis=0)
    return mine, over_core(mine)


def gather_plane(block):
    return gather_rest(block, over_y(block), over_x(block))


def scatter_plane(mine, theirs, fill=(None, None, None)):
    rows = mine.shape[0] // 4
    half = rows // 2
    done = []

    def beside(received, work):
        if work is None:
            return received
        received, result = tie((received, work()))
        done.append(result)
        return received

    total = plus(mine, beside(over_core(theirs), fill[0]))
    own, for_y, for_x, diag = (total[i * rows : (i + 1) * rows] for i in range(4))
    top, bottom = beside((over_x(diag[:half]), over_y(diag[half:])), fill[1])
    for_y = jnp.concatenate([plus(for_y[:half], top), for_y[half:]], axis=0)
    for_x = jnp.concatenate([for_x[:half], plus(for_x[half:], bottom)], axis=0)
    from_y, from_x = beside((over_y(for_y), over_x(for_x)), fill[2])
    return wide(own) + wide(from_y) + wide(from_x), done


def sum_everywhere(value, event):
    value = later(value, event)
    for step in (over_core, over_x, over_y):
        value = value + step(value)
    for distance in (1, 2):
        value = value + over("cz", distance, value)
    return value


def after(value, *events):
    return lax.optimization_barrier((value,) + events)[0]


def later(value, event):
    scalar = event[(0,) * event.ndim]
    nothing = jnp.where(scalar != scalar, scalar, jnp.zeros_like(scalar))
    return value + nothing.astype(value.dtype)


def scatter_bits(value, axes=(0, 1, 2)):
    me_f, me_y = lax.axis_index(FSDP), lax.axis_index("cy")
    me_x, me_core = me_f // 2, me_f % 2
    axis_x, axis_core, axis_y = axes
    value = plus(at(value, me_core, axis_core), over_core(at(value, 1 - me_core, axis_core)))
    axis_x -= axis_x > axis_core
    axis_y -= axis_y > axis_core
    value = plus(at(value, me_x, axis_x), over_x(at(value, 1 - me_x, axis_x)))
    axis_y -= axis_y > axis_x
    return plus(at(value, me_y, axis_y), over_y(at(value, 1 - me_y, axis_y)))


def planned_device(
    tokens,
    encoded,
    grad_out,
    doc_lengths,
    src_lengths,
    norm_gain,
    norm_bias,
    w_qkv,
    self_bias,
    w_self_out,
    w_cross_q,
    w_cross_kv,
    cross_bias,
    w_cross_out,
    w_up,
    up_bias,
    w_down,
    down_bias,
):
    q_scale = 1.0 / math.sqrt(HEAD_DIM)
    rows, features = tokens.shape[1:]
    src_own = encoded.shape[1]
    n_z, n_y, n_f = lax.axis_size("cz"), lax.axis_size("cy"), lax.axis_size(FSDP)
    n_ctx = n_z * n_y
    me_y, me_f = lax.axis_index("cy"), lax.axis_index(FSDP)
    own = me_f * n_y + me_y
    shard, hidden = w_up.shape
    slab = hidden // n_ctx
    width = features // n_ctx
    column = 2 * features // n_ctx

    moved = trade_places(jnp.concatenate([tokens[0], encoded[0]], axis=0))
    tok_low, enc_low = moved[:rows], moved[rows:]
    lengths = trade_places(jnp.concatenate([doc_lengths, src_lengths], axis=0))
    head_w = swap_columns(w_qkv, w_cross_kv, w_up)
    tok_low, enc_low, lengths = tie((tok_low, enc_low, lengths))
    qkv_own = rows_in_order(head_w, 0, 3 * PAIR)
    kv_own = rows_in_order(head_w, 3 * PAIR, column)
    up_own = rows_in_order(head_w, 3 * PAIR + column, slab)
    square = gather_rows(jnp.concatenate([w_self_out, w_cross_q, w_cross_out], axis=1))

    own_rows = own * rows + jnp.arange(rows, dtype=jnp.int32)
    tok_pos = stream_position(own_rows, rows, n_ctx)
    doc_starts = jnp.cumsum(lengths[0]) - lengths[0]
    tok_doc = doc_index(doc_starts, tok_pos)
    src_ends = jnp.cumsum(lengths[1])
    span_low = pick_doc(src_ends - lengths[1], tok_doc)
    span_high = pick_doc(src_ends, tok_doc)
    own_index = own.astype(jnp.int32)[None]

    tok_f32 = wide(tok_low)
    ln_one, normed_one, inverse_one = layer_norm(tok_f32, norm_gain[0], norm_bias[0])
    act_one = low(ln_one)
    from_y, from_x = over_y(act_one), over_x(act_one)
    enc_all = lax.all_gather(enc_low, PLANE, axis=0, tiled=True)
    act_mine, act_theirs = gather_rest(act_one, from_y, from_x)
    down_grad_low = trade_places(grad_out[0])
    grad_all = lax.all_gather(down_grad_low, PLANE, axis=0, tiled=False)
    full_self_out, full_cross_q, full_cross_out = (
        square[:, i * features : (i + 1) * features] for i in range(3)
    )

    head_bias = lax.dynamic_slice_in_dim(self_bias, own * PAIR, PAIR, 1)
    qkv_bias = jnp.concatenate([head_bias[0], jnp.zeros_like(head_bias[0]), head_bias[1]])
    qkv_factor = jnp.concatenate([jnp.full((PAIR,), q_scale), jnp.ones((2 * PAIR,))])

    def project(acts):
        return low((plain_dot(acts, qkv_own) + qkv_bias) * qkv_factor.astype(jnp.float32))

    qkv_heads = jnp.concatenate([project(act_mine), project(act_theirs)], axis=0)
    kv_bias = jnp.concatenate([jnp.zeros((features,), jnp.float32), cross_bias[1]])
    kv_columns = low(
        plain_dot(enc_all, kv_own) + lax.dynamic_slice_in_dim(kv_bias, own * column, column, 0)
    )
    kv_cross = lax.all_gather(after(kv_columns, grad_all), PLANE, axis=0, tiled=False)
    down_own = lax.dynamic_slice_in_dim(w_down, me_y * slab, slab, 0)
    att_heads = self_forward(doc_starts, own_index, qkv_heads)
    att_heads, down_own, up_own = tie((att_heads, down_own, up_own))
    att_self = lax.all_to_all(att_heads, PLANE, 0, 1, tiled=True)
    order = (0, 1, 4, 5, 2, 3, 6, 7)
    grad_mine = jnp.concatenate([at(grad_all, own ^ k, 0) for k in order[:4]], axis=0)
    grad_theirs = jnp.concatenate([at(grad_all, own ^ k, 0) for k in order[4:]], axis=0)

    hidden_one = tok_f32 + plain_dot(att_self, full_self_out) + self_bias[2]
    ln_two, normed_two, inverse_two = layer_norm(hidden_one, norm_gain[1], norm_bias[1])
    act_two = low(ln_two)
    q_cross = low((plain_dot(act_two, full_cross_q) + cross_bias[0]) * q_scale)
    att_cross = cross_forward(q_cross, kv_cross, span_low, span_high)
    hidden_two = hidden_one + plain_dot(att_cross, full_cross_out) + cross_bias[2]

    ln_three, normed_three, inverse_three = layer_norm(hidden_two, norm_gain[2], norm_bias[2])
    three_mine, three_theirs = gather_plane(low(ln_three))
    bias_own = lax.dynamic_slice_in_dim(up_bias, own * slab, slab, 0).reshape(1, -1)
    gelu_theirs, pre_theirs, part_theirs, sum_theirs = mlp_forward_back(
        three_theirs, grad_theirs, up_own, down_own, bias_own
    )
    gelu_mine, pre_mine, part_mine, sum_mine = mlp_forward_back(
        three_mine, grad_mine, up_own, down_own, bias_own
    )

    part_mine, three_mine, three_theirs, grad_mine, grad_theirs, act_mine, act_theirs = tie(
        (part_mine, three_mine, three_theirs, grad_mine, grad_theirs, act_mine, act_theirs)
    )
    act_grad, (up_grad, down_grad, out_sent) = scatter_plane(
        part_mine,
        part_theirs,
        (
            lambda: outer_pair(three_mine, pre_mine, three_theirs, pre_theirs),
            lambda: outer_pair(grad_mine, gelu_mine, grad_theirs, gelu_theirs),
            lambda: low(plain_dot(gelu_theirs, down_own)),
        ),
    )
    up_grad = lax.psum_scatter(up_grad, "cz", scatter_dimension=0, tiled=True)
    down_grad = lax.psum_scatter(down_grad, "cz", scatter_dimension=0, tiled=True)
    out_mine = low(plain_dot(gelu_mine, down_own))

    upstream = wide(down_grad_low)
    grad_down_bias = jnp.sum(upstream, axis=0)
    norm_in_three, gain_grad_three, shift_grad_three = norm_back(
        act_grad, normed_three, inverse_three, norm_gain[2]
    )
    grad_two = upstream + norm_in_three
    cross_grad_low = low(grad_two)
    cross_out_bias_grad = jnp.sum(wide(cross_grad_low), axis=0)
    cross_att_grad = low(times_transpose(cross_grad_low, full_cross_out))
    cross_v_bias_grad = jnp.sum(wide(cross_att_grad), axis=0)

    up_bias_grad = (sum_mine + sum_theirs)[0]

    me_x, me_core = me_f // 2, me_f % 2
    cross_q_low, cross_kv_part = cross_backward(
        q_cross, kv_cross, cross_att_grad, span_low, span_high
    )
    cross_q_bias_grad = jnp.sum(wide(cross_q_low), axis=0)
    norm_in_two, gain_grad_two, shift_grad_two = norm_back(
        times_transpose(cross_q_low, full_cross_q), normed_two, inverse_two, norm_gain[1]
    )
    grad_one = grad_two + norm_in_two
    self_grad_low = low(grad_one)
    self_att_grad = low(times_transpose(self_grad_low, full_self_out))
    self_v_bias_grad = jnp.sum(wide(self_att_grad), axis=0)
    kv_part = cross_kv_part.reshape(2, 2, 2, 2, enc_all.shape[0], PAIR)
    kv_other = over_core(at(kv_part, 1 - me_core, 1))
    self_att_grad, up_grad, kv_other = tie((self_att_grad, up_grad, kv_other))
    att_grad_heads = lax.all_to_all(self_att_grad, PLANE, 1, 0, tiled=True)
    kv_part = plus(at(kv_part, me_core, 1), kv_other)
    kv_other = over_x(at(kv_part, 1 - me_x, 0))

    send, keep = square_grads(
        me_core.astype(jnp.int32)[None],
        (
            (att_self, after(self_grad_low, self_att_grad)),
            (act_two, cross_q_low),
            (att_cross, cross_grad_low),
        ),
        n_y,
        n_z,
    )
    self_out_bias_grad = jnp.sum(wide(self_grad_low), axis=0)
    three = plus(keep, over_core(send))
    out_sum = plus(out_mine, over_core(after(out_sent, self_att_grad)))
    att_grad_heads, kv_other, three, out_sum = tie((att_grad_heads, kv_other, three, out_sum))
    kv_part = plus(at(kv_part, me_x, 0), kv_other)
    kv_other = over_y(at(kv_part, 1 - me_y, 0))
    left, right = three[:, :, : n_z // 2], three[:, :, n_z // 2 :]
    left_other = over_x(at(left, 1 - me_x, 0))
    right_other = over_y(at(right, 1 - me_y, 1))
    out_own, out_y, out_x, out_diag = (out_sum[i * rows : (i + 1) * rows] for i in range(4))
    half_rows = rows // 2
    out_top, out_bottom = over_x(out_diag[:half_rows]), over_y(out_diag[half_rows:])

    proj_grad = self_backward(doc_starts, own_index, qkv_heads, att_grad_heads)
    half = proj_grad.shape[0] // 2

    def lane_blocks(value):
        return [
            value[:, i : i + PAIR].reshape(n_z, 1, shard, PAIR)
            for i in range(0, value.shape[1], PAIR)
        ]

    def project_back():
        weight = outer_rows(act_mine, proj_grad[:half]) + outer_rows(act_theirs, proj_grad[half:])
        sums = jnp.sum(wide(proj_grad), axis=0)[None]
        shift = jnp.sum(wide(qkv_own) * sums, axis=1)
        gain = jnp.sum(wide(qkv_own) * weight, axis=1) - norm_bias[0] * shift
        return row_major(low(weight)), sums[0], gain / norm_gain[0], shift

    act_grad, ((qkv_grad, proj_sums, gain_grad_one, shift_grad_one),) = scatter_plane(
        low(times_transpose(proj_grad[:half], qkv_own)),
        low(times_transpose(proj_grad[half:], qkv_own)),
        (project_back, None, None),
    )
    down_cols = later(down_grad, act_grad).reshape(n_y, width, slab)
    other = over_y(at(down_cols, 1 - me_y, 0))
    mine = at(down_cols, me_y, 0)

    left = later(plus(at(left, me_x, 0), left_other), act_grad)
    right = later(plus(at(right, me_y, 1), right_other), act_grad)
    left, left_send = at(left, me_y, 0), at(left, 1 - me_y, 0)
    right, right_send = at(right, me_x, 0), at(right, 1 - me_x, 0)
    out_y = jnp.concatenate([plus(out_y[:half_rows], out_top), out_y[half_rows:]], axis=0)
    out_x = jnp.concatenate([out_x[:half_rows], plus(out_x[half_rows:], out_bottom)], axis=0)
    out_y, out_x = later(out_y, act_grad), later(out_x, act_grad)
    mlp_out = wide(out_own) + wide(over_y(out_y)) + wide(over_x(out_x))
    layer_out = trade_places(low(hidden_two + mlp_out + down_bias))
    self_q_bias_grad = proj_sums[:PAIR]
    cross_kv_grad = plus(at(kv_part, me_y, 0), kv_other)
    cross_kv_grad = jnp.concatenate([cross_kv_grad[0], cross_kv_grad[1]], axis=1)
    grad_encoded = wide(
        trade_places(
            scatter_bits(
                after(low(times_transpose(cross_kv_grad, kv_own)), act_grad).reshape(
                    2, 2, 2, src_own, features
                )
            )
        )
    )
    cross_kv_grad = low(outer_rows(enc_all, cross_kv_grad))
    rest = jnp.concatenate(lane_blocks(cross_kv_grad) + lane_blocks(qkv_grad), axis=1)
    rest = lax.psum_scatter(row_major(rest), "cz", scatter_dimension=0, tiled=False)
    three = jnp.concatenate(
        [
            later(plus(left, over_y(left_send)), rest),
            later(plus(right, over_x(right_send)), rest),
        ],
        axis=0,
    )
    three = wide(lax.psum_scatter(row_major(three), "cz", scatter_dimension=0, tiled=False))
    kv_blocks = trade_places(rest[:2])
    grad_w_cross_kv = wide(jnp.concatenate([kv_blocks[0], kv_blocks[1]], axis=1))
    qkv_grad = rest[2:]

    norm_in_one, _, _ = norm_back(act_grad, normed_one, inverse_one, norm_gain[0])
    grad_tokens = low(grad_one + norm_in_one)
    grad_w_up = wide(trade_places(later(up_grad, proj_grad)))
    grad_tokens = wide(trade_places(grad_tokens))

    down_halves = jnp.stack([jnp.where(me_y == 0, mine, other), jnp.where(me_y == 0, other, mine)])
    grad_w_down = wide(jnp.transpose(down_halves, (0, 2, 1)).reshape(n_y * slab, width))

    qkv_blocks = []
    inverse_of_three = pow(3, -1, n_ctx)
    for slot in range(3):
        pairs = []
        for dest in range(n_ctx):
            source = (3 * dest + slot) % n_ctx
            for z in range(n_z):
                pairs.append(
                    ((z * n_y + source % n_y) * n_f + source // n_y, dest * n_f + z)
                )
        part = (3 * ((inverse_of_three * (own - slot)) % n_ctx) + slot) // n_ctx
        qkv_blocks.append(lax.ppermute(at(qkv_grad, part, 0), ALL, pairs))
    grad_w_qkv = wide(jnp.concatenate(qkv_blocks, axis=1))

    def placed(part):
        whole = jnp.zeros((n_ctx * part.shape[0],), jnp.float32)
        return lax.dynamic_update_slice_in_dim(whole, part, own * part.shape[0], 0).reshape(
            -1, features
        )

    level = jnp.stack(
        [
            gain_grad_one,
            gain_grad_two,
            gain_grad_three,
            shift_grad_one,
            shift_grad_two,
            shift_grad_three,
            self_v_bias_grad,
            self_out_bias_grad,
            cross_q_bias_grad,
            cross_v_bias_grad,
            cross_out_bias_grad,
            grad_down_bias,
        ]
    )
    level = sum_everywhere(
        jnp.concatenate([level, placed(self_q_bias_grad), placed(up_bias_grad)], axis=0), act_grad
    )
    grad_up_bias = level[13:].reshape(hidden)

    return (
        layer_out[None],
        grad_tokens[None],
        grad_encoded[None],
        level[0:3],
        level[3:6],
        grad_w_qkv,
        jnp.concatenate([level[12:13], level[6:8]], axis=0),
        three[0],
        three[1],
        grad_w_cross_kv,
        level[8:11],
        three[2],
        grad_w_up,
        grad_up_bias,
        grad_w_down,
        level[11],
    )


def planned_solution(mesh):
    n_ctx, n_f = mesh.shape["ctx"], mesh.shape["fsdp"]
    split = Mesh(mesh.devices.reshape(n_ctx // 2, 2, n_f // 2, 2), ALL)
    token = P(FSDP, CTX, None)
    row = P(FSDP, None)
    owned = P(FSDP, CTX)
    return jax.shard_map(
        planned_device,
        mesh=split,
        in_specs=(token, token, token, row, row, P(), P(), row, P(), row, row, row, P(), row)
        + (row, P(), row, P()),
        out_specs=(token, token, token, P(), P(), owned, P(), owned, owned, owned, P(), owned)
        + (owned, P(), owned, P()),
        check_vma=False,
    )


def solution(mesh):
    if mesh.shape["ctx"] * 2 == HEADS and mesh.shape["fsdp"] * 2 == mesh.shape["ctx"]:
        return planned_solution(mesh)
    return general_solution(mesh)
```

```python
import functools
import math

import jax
import jax.numpy as jnp
from jax import lax
from jax.experimental import pallas as pl
from jax.experimental.layout import Layout, with_layout_constraint
from jax.experimental.pallas import tpu as pltpu
from jax.sharding import Mesh
from jax.sharding import PartitionSpec as P

HEADS = 16
HEAD_DIM = 64
KBLOCK = 512


EPS = 1e-05
NEG = -1e30
GELU_C = 0.7978845608028654
GELU_A = 0.044715
CONTRACT_ROWS = (((0,), (0,)), ((), ()))
CONTRACT_COLS = (((1,), (1,)), ((), ()))


def shortened(shard):
    return jax.tree.map(lambda a: a.astype(jnp.bfloat16) if a.dtype == jnp.float32 else a, shard)


def gelu_value(pre):
    return 0.5 * pre * (1.0 + jnp.tanh(GELU_C * (pre + GELU_A * pre * pre * pre)))


def gelu_slope(pre):
    tangent = jnp.tanh(GELU_C * (pre + GELU_A * pre * pre * pre))
    return 0.5 * (1.0 + tangent) + 0.5 * pre * (1.0 - tangent * tangent) * GELU_C * (
        1.0 + 3.0 * GELU_A * pre * pre
    )


def stream_position(rows, tok_dev, ctx_count):
    half = tok_dev // 2
    device = rows // tok_dev
    within = rows % tok_dev
    early = device * half + within
    late = (2 * ctx_count - 1 - device) * half + (within - half)
    return jnp.where(within < half, early, late)


def layer_norm(inputs, gain_row, shift_row):
    center = inputs - jnp.mean(inputs, axis=1, keepdims=True)
    inverse = lax.rsqrt(jnp.mean(center * center, axis=1, keepdims=True) + EPS)
    normed = center * inverse
    return (normed * gain_row + shift_row, normed, inverse)


def norm_back(upstream, normed, inverse, gain_row):
    scaled = upstream * gain_row
    mean_plain = jnp.mean(scaled, axis=1, keepdims=True)
    mean_normed = jnp.mean(scaled * normed, axis=1, keepdims=True)
    return (
        inverse * (scaled - mean_plain - normed * mean_normed),
        jnp.sum(upstream * normed, axis=0),
        jnp.sum(upstream, axis=0),
    )


def outer_rows(left, right):
    return lax.dot_general(left, right, CONTRACT_ROWS, preferred_element_type=jnp.float32)


def times_transpose(left, right):
    return lax.dot_general(left, right, CONTRACT_COLS, preferred_element_type=jnp.float32)


def plain_dot(left, right):
    return jnp.dot(left, right, preferred_element_type=jnp.float32)


def doc_index(doc_starts, positions):
    counted = jnp.sum((doc_starts[None, :] <= positions[:, None]).astype(jnp.int32), axis=1)
    return counted - 1


def pick_doc(lookup, doc_ids):
    onehot = doc_ids[:, None] == jnp.arange(lookup.shape[0], dtype=jnp.int32)[None, :]
    return jnp.sum(jnp.where(onehot, lookup[None, :], 0), axis=1)


def split_heads(matrix):
    return matrix.reshape(matrix.shape[0], HEADS, matrix.shape[1] // HEADS)


def split_pair(kv_piece):
    half_width = kv_piece.shape[1] // 2
    return (split_heads(kv_piece[:, :half_width]), split_heads(kv_piece[:, half_width:]))


def key_block(kv_whole, block_start):
    return split_pair(lax.dynamic_slice_in_dim(kv_whole, block_start, KBLOCK, 0))


def block_starts(kv_whole):
    return jnp.arange(kv_whole.shape[0] // KBLOCK, dtype=jnp.int32) * KBLOCK


def score_block(queries, key_heads):
    return jnp.einsum("qhd,khd->hqk", queries, key_heads, preferred_element_type=jnp.float32)


def attend(queries, kv_whole, allowed_fn):
    shape_stat = (queries.shape[1], queries.shape[0])

    def stat_step(state_pair, block_start):
        allowed = allowed_fn(block_start)

        def stat_compute_block(running):
            running_top, running_sum = running
            key_heads, value_heads = key_block(kv_whole, block_start)
            masked = jnp.where(allowed[None], score_block(queries, key_heads), NEG)
            new_top = jnp.maximum(running_top, jnp.max(masked, axis=2))
            exp_terms = jnp.where(allowed[None], jnp.exp(masked - new_top[:, :, None]), 0.0)
            return (
                new_top,
                running_sum * jnp.exp(running_top - new_top) + jnp.sum(exp_terms, axis=2),
            )

        return (
            lax.cond(jnp.any(allowed), stat_compute_block, lambda running: running, state_pair),
            None,
        )

    initial = (jnp.full(shape_stat, NEG, jnp.float32), jnp.zeros(shape_stat, jnp.float32))
    (final_top, final_sum), _ = lax.scan(stat_step, initial, block_starts(kv_whole))
    logsum = final_top + jnp.log(final_sum)

    def value_step(running, block_start):
        allowed = allowed_fn(block_start)

        def value_compute_block(partial_value):
            key_heads, value_heads = key_block(kv_whole, block_start)
            raw_scores = score_block(queries, key_heads)
            prob_low = jnp.where(
                allowed[None], jnp.exp(raw_scores - logsum[:, :, None]), 0.0
            ).astype(jnp.bfloat16)
            return partial_value + jnp.einsum(
                "hqk,khd->qhd", prob_low, value_heads, preferred_element_type=jnp.float32
            )

        return (
            lax.cond(
                jnp.any(allowed), value_compute_block, lambda partial_value: partial_value, running
            ),
            None,
        )

    attended, _ = lax.scan(
        value_step, jnp.zeros(queries.shape, jnp.float32), block_starts(kv_whole)
    )
    return (attended, logsum)


def score_grads(queries, key_heads, value_heads, grad_heads, logsum, row_delta, allowed):
    raw_scores = score_block(queries, key_heads)
    probs_full = jnp.where(allowed[None], jnp.exp(raw_scores - logsum[:, :, None]), 0.0)
    grad_probs = jnp.einsum(
        "qhd,khd->hqk", grad_heads, value_heads, preferred_element_type=jnp.float32
    )
    grad_scores = (probs_full * (grad_probs - row_delta[:, :, None])).astype(jnp.bfloat16)
    return (probs_full, grad_scores)


def key_terms(queries, key_heads, value_heads, grad_heads, logsum, row_delta, allowed):
    probs_full, grad_scores = score_grads(
        queries, key_heads, value_heads, grad_heads, logsum, row_delta, allowed
    )
    grad_keys = jnp.einsum("hqk,qhd->khd", grad_scores, queries, preferred_element_type=jnp.float32)
    grad_values = jnp.einsum(
        "hqk,qhd->khd",
        probs_full.astype(jnp.bfloat16),
        grad_heads,
        preferred_element_type=jnp.float32,
    )
    key_count = key_heads.shape[0]
    return jnp.concatenate(
        [grad_keys.reshape(key_count, -1), grad_values.reshape(key_count, -1)], axis=1
    )


def row_deltas(grad_heads, attended):
    return jnp.einsum("qhd,qhd->hq", grad_heads.astype(jnp.float32), attended)


def query_back(queries, kv_whole, allowed_fn, logsum, row_delta, grad_heads):

    def query_grad_step(partial_value, block_start):
        allowed = allowed_fn(block_start)

        def query_compute_block(running):
            key_heads, value_heads = key_block(kv_whole, block_start)
            probs_full, grad_scores = score_grads(
                queries, key_heads, value_heads, grad_heads, logsum, row_delta, allowed
            )
            return running + jnp.einsum(
                "hqk,khd->qhd", grad_scores, key_heads, preferred_element_type=jnp.float32
            )

        return (
            lax.cond(jnp.any(allowed), query_compute_block, lambda running: running, partial_value),
            None,
        )

    grad_query, _ = lax.scan(
        query_grad_step, jnp.zeros(queries.shape, jnp.float32), block_starts(kv_whole)
    )
    return grad_query


def attend_back(queries, kv_whole, allowed_fn, attended, logsum, grad_heads):
    row_delta = row_deltas(grad_heads, attended)

    def attend_grad_step(grad_query, block_start):
        allowed = allowed_fn(block_start)

        def attend_compute_block(partial_value):
            key_heads, value_heads = key_block(kv_whole, block_start)
            probs_full, grad_scores = score_grads(
                queries, key_heads, value_heads, grad_heads, logsum, row_delta, allowed
            )
            partial_value = partial_value + jnp.einsum(
                "hqk,khd->qhd", grad_scores, key_heads, preferred_element_type=jnp.float32
            )
            grad_keys = jnp.einsum(
                "hqk,qhd->khd", grad_scores, queries, preferred_element_type=jnp.float32
            )
            grad_values = jnp.einsum(
                "hqk,qhd->khd",
                probs_full.astype(jnp.bfloat16),
                grad_heads,
                preferred_element_type=jnp.float32,
            )
            return (
                partial_value,
                jnp.concatenate(
                    [grad_keys.reshape(KBLOCK, -1), grad_values.reshape(KBLOCK, -1)], axis=1
                ),
            )

        def attend_skip_block(partial_value):
            return (partial_value, jnp.zeros((KBLOCK, kv_whole.shape[1]), jnp.float32))

        return lax.cond(jnp.any(allowed), attend_compute_block, attend_skip_block, grad_query)

    grad_query, kv_terms = lax.scan(
        attend_grad_step, jnp.zeros(queries.shape, jnp.float32), block_starts(kv_whole)
    )
    return (grad_query, kv_terms.reshape(kv_whole.shape[0], kv_whole.shape[1]))


def owners_end(grads):
    columns = jax.tree.map(
        lambda part: part.astype(jnp.float32),
        lax.psum_scatter(shortened(grads), "ctx", scatter_dimension=1, tiled=True),
    )
    return jax.tree.map(
        lambda part: part.astype(jnp.float32),
        lax.psum_scatter(shortened(columns), "fsdp", scatter_dimension=0, tiled=True),
    )


def per_device(
    tokens,
    encoded,
    grad_out,
    doc_lengths,
    src_lengths,
    norm_gain,
    norm_bias,
    w_qkv,
    self_bias,
    w_self_out,
    w_cross_q,
    w_cross_kv,
    cross_bias,
    w_cross_out,
    w_up,
    up_bias,
    w_down,
    down_bias,
):
    q_scale = 1.0 / math.sqrt(HEAD_DIM)
    tok_rows = tokens.shape[1]
    features = tokens.shape[2]
    ctx_count = lax.axis_size("ctx")
    ctx_index = lax.axis_index("ctx")
    own_rows = ctx_index * tok_rows + jnp.arange(tok_rows, dtype=jnp.int32)
    tok_pos = stream_position(own_rows, tok_rows, ctx_count)
    lengths_row = doc_lengths[0]
    doc_starts = jnp.cumsum(lengths_row) - lengths_row
    tok_doc = doc_index(doc_starts, tok_pos)
    src_row = src_lengths[0]
    src_ends = jnp.cumsum(src_row)
    src_starts = src_ends - src_row
    span_low = pick_doc(src_starts, tok_doc)
    span_high = pick_doc(src_ends, tok_doc)

    def self_mask(key_rows):
        key_pos = stream_position(key_rows, tok_rows, ctx_count)
        key_doc = doc_index(doc_starts, key_pos)
        return (key_pos[None, :] <= tok_pos[:, None]) & (key_doc[None, :] == tok_doc[:, None])

    def self_allowed(block_start):
        return self_mask(block_start + jnp.arange(KBLOCK, dtype=jnp.int32))

    def cross_allowed(block_start):
        key_pos = block_start + jnp.arange(KBLOCK, dtype=jnp.int32)
        return (key_pos[None, :] >= span_low[:, None]) & (key_pos[None, :] < span_high[:, None])

    def gather_self():
        return (
            lax.all_gather(w_qkv, "fsdp", axis=0, tiled=True),
            lax.all_gather(w_self_out, "fsdp", axis=0, tiled=True),
        )

    def gather_cross():
        return (
            lax.all_gather(w_cross_q, "fsdp", axis=0, tiled=True),
            lax.all_gather(w_cross_kv, "fsdp", axis=0, tiled=True),
            lax.all_gather(w_cross_out, "fsdp", axis=0, tiled=True),
        )

    def gather_mlp():
        return (
            lax.all_gather(w_up, "fsdp", axis=0, tiled=True),
            lax.all_gather(w_down, "fsdp", axis=0, tiled=True),
        )

    tok_f32 = tokens[0].astype(jnp.float32)
    enc_low = encoded[0]
    ln_one, normed_one, inverse_one = layer_norm(tok_f32, norm_gain[0], norm_bias[0])
    act_one = ln_one.astype(jnp.bfloat16)
    full_qkv, full_self_out = gather_self()
    projected = plain_dot(act_one, full_qkv)
    q_self = ((projected[:, :features] + self_bias[0]) * q_scale).astype(jnp.bfloat16)
    kv_self = jnp.concatenate(
        [projected[:, features : 2 * features], projected[:, 2 * features :] + self_bias[1]], axis=1
    ).astype(jnp.bfloat16)
    kv_self_all = lax.all_gather(kv_self, "ctx", axis=0, tiled=True)
    self_heads = split_heads(q_self)
    att_self, lse_self = attend(self_heads, kv_self_all, self_allowed)
    att_self_low = att_self.reshape(tok_rows, features).astype(jnp.bfloat16)
    hidden_one = tok_f32 + plain_dot(att_self_low, full_self_out) + self_bias[2]
    ln_two, normed_two, inverse_two = layer_norm(hidden_one, norm_gain[1], norm_bias[1])
    act_two = ln_two.astype(jnp.bfloat16)
    full_cross_q, full_cross_kv, full_cross_out = gather_cross()
    q_cross = ((plain_dot(act_two, full_cross_q) + cross_bias[0]) * q_scale).astype(jnp.bfloat16)
    src_proj = plain_dot(enc_low, full_cross_kv)
    kv_cross = jnp.concatenate(
        [src_proj[:, :features], src_proj[:, features:] + cross_bias[1]], axis=1
    ).astype(jnp.bfloat16)
    kv_cross_all = lax.all_gather(kv_cross, "ctx", axis=0, tiled=True)
    cross_heads = split_heads(q_cross)
    att_cross, lse_cross = attend(cross_heads, kv_cross_all, cross_allowed)
    att_cross_low = att_cross.reshape(tok_rows, features).astype(jnp.bfloat16)
    hidden_two = hidden_one + plain_dot(att_cross_low, full_cross_out) + cross_bias[2]
    ln_three, normed_three, inverse_three = layer_norm(hidden_two, norm_gain[2], norm_bias[2])
    act_three = ln_three.astype(jnp.bfloat16)
    full_up, full_down = gather_mlp()
    pre_act = plain_dot(act_three, full_up) + up_bias
    gelu_low = gelu_value(pre_act).astype(jnp.bfloat16)
    layer_out = (hidden_two + plain_dot(gelu_low, full_down) + down_bias).astype(jnp.bfloat16)
    upstream = grad_out[0].astype(jnp.float32)
    down_grad_low = grad_out[0]
    full_up, full_down = gather_mlp()
    grad_w_down = outer_rows(gelu_low, down_grad_low)
    grad_down_bias = jnp.sum(upstream, axis=0)
    gelu_grad = times_transpose(down_grad_low, full_down)
    pre_grad_low = (gelu_grad * gelu_slope(pre_act)).astype(jnp.bfloat16)
    grad_w_up = outer_rows(act_three, pre_grad_low)
    grad_up_bias = jnp.sum(pre_grad_low.astype(jnp.float32), axis=0)
    norm_in_three, gain_grad_three, shift_grad_three = norm_back(
        times_transpose(pre_grad_low, full_up), normed_three, inverse_three, norm_gain[2]
    )
    grad_two = upstream + norm_in_three
    full_cross_q, full_cross_kv, full_cross_out = gather_cross()
    cross_grad_low = grad_two.astype(jnp.bfloat16)
    grad_w_cross_out = outer_rows(att_cross_low, cross_grad_low)
    cross_out_bias_grad = jnp.sum(cross_grad_low.astype(jnp.float32), axis=0)
    cross_att_grad = split_heads(
        times_transpose(cross_grad_low, full_cross_out).astype(jnp.bfloat16)
    )
    cross_q_grad, cross_kv_terms = attend_back(
        cross_heads, kv_cross_all, cross_allowed, att_cross, lse_cross, cross_att_grad
    )
    cross_kv_grad = lax.psum_scatter(
        cross_kv_terms.astype(jnp.bfloat16), "ctx", scatter_dimension=0, tiled=True
    )
    cross_q_low = (cross_q_grad.reshape(tok_rows, features) * q_scale).astype(jnp.bfloat16)
    grad_w_cross_q = outer_rows(act_two, cross_q_low)
    cross_q_bias_grad = jnp.sum(cross_q_low.astype(jnp.float32), axis=0)
    grad_w_cross_kv = outer_rows(enc_low, cross_kv_grad)
    cross_v_bias_grad = jnp.sum(cross_kv_grad[:, features:].astype(jnp.float32), axis=0)
    grad_encoded = times_transpose(cross_kv_grad, full_cross_kv)
    norm_in_two, gain_grad_two, shift_grad_two = norm_back(
        times_transpose(cross_q_low, full_cross_q), normed_two, inverse_two, norm_gain[1]
    )
    grad_one = grad_two + norm_in_two
    full_qkv, full_self_out = gather_self()
    self_grad_low = grad_one.astype(jnp.bfloat16)
    grad_w_self_out = outer_rows(att_self_low, self_grad_low)
    self_out_bias_grad = jnp.sum(self_grad_low.astype(jnp.float32), axis=0)
    self_att_flat = times_transpose(self_grad_low, full_self_out).astype(jnp.bfloat16)
    self_att_grad = split_heads(self_att_flat)
    self_delta = row_deltas(self_att_grad, att_self)
    self_q_grad = query_back(
        self_heads, kv_self_all, self_allowed, lse_self, self_delta, self_att_grad
    )

    def one_piece(sub_start):
        key_rows = sub_start + jnp.arange(tok_rows, dtype=jnp.int32)
        allowed = self_mask(key_rows)

        def one_compute_block(piece_start):
            key_heads, value_heads = split_pair(
                lax.dynamic_slice_in_dim(kv_self_all, piece_start, tok_rows, 0)
            )
            return key_terms(
                self_heads, key_heads, value_heads, self_att_grad, lse_self, self_delta, allowed
            )

        def one_skip_block(piece_start):
            return jnp.zeros((tok_rows, 2 * features), jnp.float32)

        return lax.cond(jnp.any(allowed), one_compute_block, one_skip_block, sub_start)

    piece_starts = (
        jnp.arange(tok_rows * lax.axis_size("ctx") // tok_rows, dtype=jnp.int32) * tok_rows
    )
    self_kv_grad = lax.psum_scatter(
        lax.map(one_piece, piece_starts)
        .reshape(tok_rows * lax.axis_size("ctx"), 2 * features)
        .astype(jnp.bfloat16),
        "ctx",
        scatter_dimension=0,
        tiled=True,
    )
    self_q_low = (self_q_grad.reshape(tok_rows, features) * q_scale).astype(jnp.bfloat16)
    proj_grad_low = jnp.concatenate([self_q_low, self_kv_grad], axis=1)
    grad_w_qkv = outer_rows(act_one, proj_grad_low)
    self_q_bias_grad = jnp.sum(self_q_low.astype(jnp.float32), axis=0)
    self_v_bias_grad = jnp.sum(self_kv_grad[:, features:].astype(jnp.float32), axis=0)
    norm_in_one, gain_grad_one, shift_grad_one = norm_back(
        times_transpose(proj_grad_low, full_qkv), normed_one, inverse_one, norm_gain[0]
    )
    grad_tokens = grad_one + norm_in_one
    owned = owners_end(
        (
            grad_w_qkv,
            grad_w_self_out,
            grad_w_cross_q,
            grad_w_cross_kv,
            grad_w_cross_out,
            grad_w_up,
            grad_w_down,
        )
    )
    gain_grads = jnp.stack([gain_grad_one, gain_grad_two, gain_grad_three])
    shift_grads = jnp.stack([shift_grad_one, shift_grad_two, shift_grad_three])
    self_bias_grads = jnp.stack([self_q_bias_grad, self_v_bias_grad, self_out_bias_grad])
    cross_bias_grads = jnp.stack([cross_q_bias_grad, cross_v_bias_grad, cross_out_bias_grad])
    summed = lax.psum(
        (gain_grads, shift_grads, self_bias_grads, cross_bias_grads, grad_up_bias, grad_down_bias),
        ("ctx", "fsdp"),
    )
    return (
        layer_out[None],
        grad_tokens[None],
        grad_encoded[None],
        summed[0],
        summed[1],
        owned[0],
        summed[2],
        owned[1],
        owned[2],
        owned[3],
        summed[3],
        owned[4],
        owned[5],
        summed[4],
        owned[6],
        summed[5],
    )


def general_solution(mesh):
    placed = (
        P("fsdp", "ctx", None),
        P("fsdp", "ctx", None),
        P("fsdp", "ctx", None),
        P("fsdp", None),
        P("fsdp", None),
        P(),
        P(),
        P("fsdp", None),
        P(),
        P("fsdp", None),
        P("fsdp", None),
        P("fsdp", None),
        P(),
        P("fsdp", None),
        P("fsdp", None),
        P(),
        P("fsdp", None),
        P(),
    )
    return jax.shard_map(
        per_device,
        mesh=mesh,
        in_specs=placed,
        out_specs=(
            P("fsdp", "ctx", None),
            P("fsdp", "ctx", None),
            P("fsdp", "ctx", None),
            P(),
            P(),
            P("fsdp", "ctx"),
            P(),
            P("fsdp", "ctx"),
            P("fsdp", "ctx"),
            P("fsdp", "ctx"),
            P(),
            P("fsdp", "ctx"),
            P("fsdp", "ctx"),
            P(),
            P("fsdp", "ctx"),
            P(),
        ),
        check_vma=False,
    )


CTX = ("cz", "cy")
FSDP = ("fx", "fc")
PLANE = ("fx", "fc", "cy")
ALL = ("cz", "cy", "fx", "fc")
ROW_BLOCK = 512
HIDDEN_BLOCK = 256
QBLOCK = 256
HALF = 128
PAIR = 2 * HEAD_DIM
MAX_KEY_BLOCKS = 5


def kernel_cost(microseconds):
    return pl.CostEstimate(
        flops=int(microseconds * 1.15e9), bytes_accessed=1 << 20, transcendentals=0
    )


def row_major(value):
    return with_layout_constraint(value, Layout(tuple(range(value.ndim))))


def doc_start_of(starts_ref, positions):
    first = jnp.zeros_like(positions)
    for doc in range(starts_ref.shape[0]):
        begin = starts_ref[doc]
        first = jnp.where(positions >= begin, begin, first)
    return first


def doc_start_scalar(starts_ref, position):
    first = jnp.int32(0)
    for doc in range(starts_ref.shape[0]):
        begin = starts_ref[doc]
        first = jnp.where(position >= begin, begin, first)
    return first


def half_row(pos_block, pos_blocks):
    early = pos_block * (2 * HALF)
    late = (pos_blocks - 1 - pos_block) * (2 * HALF) + HALF
    return pl.multiple_of(jnp.where(2 * pos_block < pos_blocks, early, late), HALF)


def slot_of(distance):
    return (distance & 1) + 2 * ((distance >> 2) & 1) + 4 * ((distance >> 1) & 1)


def slot_row(row, own):
    block = row // (2 * HALF)
    slot = slot_of(block ^ own)
    return pl.multiple_of(slot * (2 * HALF) + row - block * (2 * HALF), HALF)


def lane_mask(rows, head):
    lanes = lax.broadcasted_iota(jnp.int32, (rows, PAIR), 1)
    return (lanes >= head * HEAD_DIM) & (lanes < (head + 1) * HEAD_DIM)


def to_positions(own, src_ref, column, dst_ref):
    pos_blocks = src_ref.shape[0] // HALF

    def move(block, carry):
        row = slot_row(half_row(block, pos_blocks), own)
        dst_ref[pl.ds(pl.multiple_of(block * HALF, HALF), HALF), :] = src_ref[
            pl.ds(row, HALF), pl.ds(column, PAIR)
        ]
        return carry

    lax.fori_loop(0, pos_blocks, move, 0)


def self_forward_kernel(starts_ref, own_ref, qkv_ref, out_ref, key_ref, value_ref):
    step = pl.program_id(0)
    own = own_ref[0]
    pos_blocks = qkv_ref.shape[0] // HALF

    @pl.when(step == 0)
    def _():
        to_positions(own, qkv_ref, PAIR, key_ref)
        to_positions(own, qkv_ref, 2 * PAIR, value_ref)

    row_a = half_row(2 * step, pos_blocks)
    row_b = half_row(2 * step + 1, pos_blocks)
    slot_a, slot_b = slot_row(row_a, own), slot_row(row_b, own)
    queries = jnp.concatenate(
        [qkv_ref[pl.ds(slot_a, HALF), pl.ds(0, PAIR)], qkv_ref[pl.ds(slot_b, HALF), pl.ds(0, PAIR)]],
        axis=0,
    )
    q_start = step * QBLOCK
    first_block = doc_start_scalar(starts_ref, q_start) // QBLOCK
    count = step - first_block + 1
    q_pos = q_start + lax.broadcasted_iota(jnp.int32, (QBLOCK, 1), 0)
    q_first = doc_start_of(starts_ref, q_pos)

    def compute(blocks):
        width = blocks * QBLOCK
        k_start = pl.multiple_of(first_block * QBLOCK, QBLOCK)
        keys = key_ref[pl.ds(k_start, width), :]
        values = value_ref[pl.ds(k_start, width), :]
        k_pos = k_start + lax.broadcasted_iota(jnp.int32, (QBLOCK, width), 1)
        allowed = (k_pos >= q_first) & (k_pos <= q_pos)
        parts = []
        for head in range(2):
            picked = jnp.where(lane_mask(QBLOCK, head), queries, jnp.zeros_like(queries))
            scores = lax.dot_general(picked, keys, CONTRACT_COLS, preferred_element_type=jnp.float32)
            scores = jnp.where(allowed, scores, NEG)
            terms = jnp.exp(scores - jnp.max(scores, axis=1, keepdims=True))
            inverse = 1.0 / jnp.sum(terms, axis=1, keepdims=True)
            mixed = jnp.dot(
                (terms * inverse).astype(jnp.bfloat16), values, preferred_element_type=jnp.float32
            )
            parts.append(mixed)
        result = jnp.where(lane_mask(QBLOCK, 0), parts[0], parts[1]).astype(jnp.bfloat16)
        out_ref[pl.ds(row_a, HALF), :] = result[:HALF]
        out_ref[pl.ds(row_b, HALF), :] = result[HALF:]

    for blocks in range(1, MAX_KEY_BLOCKS + 1):
        pl.when(count == blocks)(functools.partial(compute, blocks))


def self_backward_kernel(
    starts_ref,
    own_ref,
    qkv_ref,
    grad_ref,
    slot_ref,
    key_ref,
    value_ref,
    dkey_ref,
    dvalue_ref,
):
    step = pl.program_id(0)
    own = own_ref[0]
    pos_blocks = qkv_ref.shape[0] // HALF

    @pl.when(step == 0)
    def _():
        to_positions(own, qkv_ref, PAIR, key_ref)
        to_positions(own, qkv_ref, 2 * PAIR, value_ref)
        dkey_ref[...] = jnp.zeros_like(dkey_ref)
        dvalue_ref[...] = jnp.zeros_like(dvalue_ref)

    row_a = half_row(2 * step, pos_blocks)
    row_b = half_row(2 * step + 1, pos_blocks)
    slot_a, slot_b = slot_row(row_a, own), slot_row(row_b, own)
    queries = jnp.concatenate(
        [qkv_ref[pl.ds(slot_a, HALF), pl.ds(0, PAIR)], qkv_ref[pl.ds(slot_b, HALF), pl.ds(0, PAIR)]],
        axis=0,
    )
    grads = jnp.concatenate([grad_ref[pl.ds(row_a, HALF), :], grad_ref[pl.ds(row_b, HALF), :]], axis=0)
    q_start = step * QBLOCK
    first_block = doc_start_scalar(starts_ref, q_start) // QBLOCK
    count = step - first_block + 1
    q_pos = q_start + lax.broadcasted_iota(jnp.int32, (1, QBLOCK), 1)
    q_first = doc_start_of(starts_ref, q_pos)

    def compute(blocks):
        width = blocks * QBLOCK
        k_start = pl.multiple_of(first_block * QBLOCK, QBLOCK)
        keys = key_ref[pl.ds(k_start, width), :]
        values = value_ref[pl.ds(k_start, width), :]
        k_pos = k_start + lax.broadcasted_iota(jnp.int32, (width, QBLOCK), 0)
        allowed = (k_pos >= q_first) & (k_pos <= q_pos)
        dq_parts = []
        dkey = jnp.zeros((width, PAIR), jnp.float32)
        dvalue = jnp.zeros((width, PAIR), jnp.float32)
        for head in range(2):
            inside = lane_mask(QBLOCK, head)
            picked = jnp.where(inside, queries, jnp.zeros_like(queries))
            grad = jnp.where(inside, grads, jnp.zeros_like(grads))
            scores = lax.dot_general(keys, picked, CONTRACT_COLS, preferred_element_type=jnp.float32)
            scores = jnp.where(allowed, scores, NEG)
            terms = jnp.exp(scores - jnp.max(scores, axis=0, keepdims=True))
            probs = terms * (1.0 / jnp.sum(terms, axis=0, keepdims=True))
            dprobs = lax.dot_general(
                values, grad, CONTRACT_COLS, preferred_element_type=jnp.float32
            )
            delta = jnp.sum(probs * dprobs, axis=0, keepdims=True)
            dscores = (probs * (dprobs - delta)).astype(jnp.bfloat16)
            dq_parts.append(
                lax.dot_general(dscores, keys, CONTRACT_ROWS, preferred_element_type=jnp.float32)
            )
            dkey = dkey + jnp.dot(dscores, picked, preferred_element_type=jnp.float32)
            dvalue = dvalue + jnp.dot(
                probs.astype(jnp.bfloat16), grad, preferred_element_type=jnp.float32
            )
        dkey_ref[pl.ds(k_start, width), :] += dkey
        dvalue_ref[pl.ds(k_start, width), :] += dvalue
        dq = jnp.where(lane_mask(QBLOCK, 0), dq_parts[0], dq_parts[1])
        dq = (dq * (1.0 / math.sqrt(HEAD_DIM))).astype(jnp.bfloat16)
        slot_ref[pl.ds(slot_a, HALF), pl.ds(0, PAIR)] = dq[:HALF]
        slot_ref[pl.ds(slot_b, HALF), pl.ds(0, PAIR)] = dq[HALF:]

    for blocks in range(1, MAX_KEY_BLOCKS + 1):
        pl.when(count == blocks)(functools.partial(compute, blocks))

    @pl.when(step == pl.num_programs(0) - 1)
    def _():
        def move(block, carry):
            slot = slot_row(half_row(block, pos_blocks), own)
            place = pl.ds(pl.multiple_of(block * HALF, HALF), HALF)
            dkey = dkey_ref[place, :].astype(jnp.bfloat16)
            dvalue = dvalue_ref[place, :].astype(jnp.bfloat16)
            slot_ref[pl.ds(slot, HALF), pl.ds(PAIR, PAIR)] = dkey
            slot_ref[pl.ds(slot, HALF), pl.ds(2 * PAIR, PAIR)] = dvalue
            return carry

        lax.fori_loop(0, pos_blocks, move, 0)


def cross_forward_kernel(q_ref, key_ref, value_ref, low_ref, high_ref, out_ref):
    rows, width = q_ref.shape[0], key_ref.shape[1]
    queries, keys, values = q_ref[...], key_ref[0], value_ref[0]
    k_pos = lax.broadcasted_iota(jnp.int32, (rows, width), 1)
    allowed = (k_pos >= low_ref[...]) & (k_pos < high_ref[...])
    parts = []
    for head in range(2):
        picked = jnp.where(lane_mask(rows, head), queries, jnp.zeros_like(queries))
        scores = lax.dot_general(picked, keys, CONTRACT_COLS, preferred_element_type=jnp.float32)
        scores = jnp.where(allowed, scores, NEG)
        terms = jnp.exp(scores - jnp.max(scores, axis=1, keepdims=True))
        inverse = 1.0 / jnp.sum(terms, axis=1, keepdims=True)
        parts.append(
            jnp.dot((terms * inverse).astype(jnp.bfloat16), values, preferred_element_type=jnp.float32)
        )
    out_ref[...] = jnp.where(lane_mask(rows, 0), parts[0], parts[1]).astype(jnp.bfloat16)


def cross_backward_kernel(q_ref, key_ref, value_ref, grad_ref, low_ref, high_ref, dq_ref, dkv_ref):
    rows, width = q_ref.shape[0], key_ref.shape[1]
    queries, keys, values, grads = q_ref[...], key_ref[0], value_ref[0], grad_ref[...]
    k_pos = lax.broadcasted_iota(jnp.int32, (width, rows), 0)
    allowed = (k_pos >= low_ref[...]) & (k_pos < high_ref[...])
    dq_parts = []
    dkey = jnp.zeros((width, PAIR), jnp.float32)
    dvalue = jnp.zeros((width, PAIR), jnp.float32)
    for head in range(2):
        inside = lane_mask(rows, head)
        picked = jnp.where(inside, queries, jnp.zeros_like(queries))
        grad = jnp.where(inside, grads, jnp.zeros_like(grads))
        scores = lax.dot_general(keys, picked, CONTRACT_COLS, preferred_element_type=jnp.float32)
        scores = jnp.where(allowed, scores, NEG)
        terms = jnp.exp(scores - jnp.max(scores, axis=0, keepdims=True))
        probs = terms * (1.0 / jnp.sum(terms, axis=0, keepdims=True))
        dprobs = lax.dot_general(values, grad, CONTRACT_COLS, preferred_element_type=jnp.float32)
        delta = jnp.sum(probs * dprobs, axis=0, keepdims=True)
        dscores = (probs * (dprobs - delta)).astype(jnp.bfloat16)
        dq_parts.append(
            lax.dot_general(dscores, keys, CONTRACT_ROWS, preferred_element_type=jnp.float32)
        )
        dkey = dkey + jnp.dot(dscores, picked, preferred_element_type=jnp.float32)
        dvalue = dvalue + jnp.dot(
            probs.astype(jnp.bfloat16), grad, preferred_element_type=jnp.float32
        )
    dq = jnp.where(lane_mask(rows, 0), dq_parts[0], dq_parts[1])
    dq_ref[...] = (dq * (1.0 / math.sqrt(HEAD_DIM))).astype(jnp.bfloat16)
    dkv_ref[0, 0] = dkey.astype(jnp.bfloat16)
    dkv_ref[1, 0] = dvalue.astype(jnp.bfloat16)


def kernel_params():
    return pltpu.CompilerParams(vmem_limit_bytes=48 * 1024 * 1024)


def self_forward(doc_starts, own, qkv):
    rows = qkv.shape[0]
    return pl.pallas_call(
        self_forward_kernel,
        grid=(rows // QBLOCK,),
        in_specs=[
            pl.BlockSpec(memory_space=pltpu.SMEM),
            pl.BlockSpec(memory_space=pltpu.SMEM),
            pl.BlockSpec((rows, 3 * PAIR), lambda step: (0, 0)),
        ],
        out_specs=pl.BlockSpec((rows, PAIR), lambda step: (0, 0)),
        out_shape=jax.ShapeDtypeStruct((rows, PAIR), jnp.bfloat16),
        scratch_shapes=[pltpu.VMEM((rows, PAIR), jnp.bfloat16)] * 2,
        compiler_params=kernel_params(),
        cost_estimate=kernel_cost(1),
    )(doc_starts, own, qkv)


def self_backward(doc_starts, own, qkv, grads):
    rows = qkv.shape[0]
    return pl.pallas_call(
        self_backward_kernel,
        grid=(rows // QBLOCK,),
        in_specs=[
            pl.BlockSpec(memory_space=pltpu.SMEM),
            pl.BlockSpec(memory_space=pltpu.SMEM),
            pl.BlockSpec((rows, 3 * PAIR), lambda step: (0, 0)),
            pl.BlockSpec((rows, PAIR), lambda step: (0, 0)),
        ],
        out_specs=pl.BlockSpec((rows, 3 * PAIR), lambda step: (0, 0)),
        out_shape=jax.ShapeDtypeStruct((rows, 3 * PAIR), jnp.bfloat16),
        scratch_shapes=[pltpu.VMEM((rows, PAIR), jnp.bfloat16)] * 2
        + [pltpu.VMEM((rows, PAIR), jnp.float32)] * 2,
        compiler_params=kernel_params(),
        cost_estimate=kernel_cost(1),
    )(doc_starts, own, qkv, grads)


def cross_forward(queries, kv_cross, span_low, span_high):
    rows, features = queries.shape
    pairs = features // PAIR
    src = kv_cross.shape[1]
    return pl.pallas_call(
        cross_forward_kernel,
        grid=(pairs,),
        in_specs=[
            pl.BlockSpec((rows, PAIR), lambda p: (0, p)),
            pl.BlockSpec((1, src, PAIR), lambda p: (p // 2, 0, p % 2)),
            pl.BlockSpec((1, src, PAIR), lambda p: (p // 2 + pairs // 2, 0, p % 2)),
            pl.BlockSpec((rows, 1), lambda p: (0, 0)),
            pl.BlockSpec((rows, 1), lambda p: (0, 0)),
        ],
        out_specs=pl.BlockSpec((rows, PAIR), lambda p: (0, p)),
        out_shape=jax.ShapeDtypeStruct((rows, features), jnp.bfloat16),
        compiler_params=kernel_params(),
        cost_estimate=kernel_cost(1),
    )(queries, kv_cross, kv_cross, span_low[:, None], span_high[:, None])


def cross_backward(queries, kv_cross, grads, span_low, span_high):
    rows, features = queries.shape
    pairs = features // PAIR
    src = kv_cross.shape[1]
    return pl.pallas_call(
        cross_backward_kernel,
        grid=(pairs,),
        in_specs=[
            pl.BlockSpec((rows, PAIR), lambda p: (0, p)),
            pl.BlockSpec((1, src, PAIR), lambda p: (p // 2, 0, p % 2)),
            pl.BlockSpec((1, src, PAIR), lambda p: (p // 2 + pairs // 2, 0, p % 2)),
            pl.BlockSpec((rows, PAIR), lambda p: (0, p)),
            pl.BlockSpec((1, rows), lambda p: (0, 0)),
            pl.BlockSpec((1, rows), lambda p: (0, 0)),
        ],
        out_specs=[
            pl.BlockSpec((rows, PAIR), lambda p: (0, p)),
            pl.BlockSpec((2, 1, src, PAIR), lambda p: (0, p, 0, 0)),
        ],
        out_shape=[
            jax.ShapeDtypeStruct((rows, features), jnp.bfloat16),
            jax.ShapeDtypeStruct((2, pairs, src, PAIR), jnp.bfloat16),
        ],
        compiler_params=kernel_params(),
        cost_estimate=kernel_cost(1),
    )(queries, kv_cross, kv_cross, grads, span_low[None, :], span_high[None, :])


def mlp_kernel(act_ref, grad_ref, up_ref, down_ref, bias_ref, gelu_ref, pre_ref, out_ref, sum_ref):
    @pl.when(pl.program_id(0) == 0)
    def _():
        sum_ref[...] = jnp.zeros_like(sum_ref)

    act, grad = act_ref[...], grad_ref[...]
    total = jnp.zeros(out_ref.shape, jnp.float32)
    for begin in range(0, up_ref.shape[1], HIDDEN_BLOCK):
        place = pl.ds(begin, HIDDEN_BLOCK)
        pre = jnp.dot(act, up_ref[:, place], preferred_element_type=jnp.float32) + bias_ref[:, place]
        square = pre * pre
        tangent = jnp.tanh(GELU_C * (pre + GELU_A * pre * square))
        half = 0.5 * (1.0 + tangent)
        gelu_ref[:, place] = (pre * half).astype(jnp.bfloat16)
        slope = half + 0.5 * pre * (1.0 - tangent * tangent) * (
            GELU_C + (3.0 * GELU_A * GELU_C) * square
        )
        back = lax.dot_general(
            grad, down_ref[place, :], CONTRACT_COLS, preferred_element_type=jnp.float32
        )
        pre_grad = (back * slope).astype(jnp.bfloat16)
        pre_ref[:, place] = pre_grad
        sum_ref[:, place] += jnp.sum(pre_grad.astype(jnp.float32), axis=0, keepdims=True)
        total = total + lax.dot_general(
            pre_grad, up_ref[:, place], CONTRACT_COLS, preferred_element_type=jnp.float32
        )
    out_ref[...] = total.astype(jnp.bfloat16)


def mlp_forward_back(act, grad, up_own, down_own, bias_own):
    rows, features = act.shape
    hidden = up_own.shape[1]
    return pl.pallas_call(
        mlp_kernel,
        grid=(rows // ROW_BLOCK,),
        in_specs=[
            pl.BlockSpec((ROW_BLOCK, features), lambda step: (step, 0)),
            pl.BlockSpec((ROW_BLOCK, features), lambda step: (step, 0)),
            pl.BlockSpec((features, hidden), lambda step: (0, 0)),
            pl.BlockSpec((hidden, features), lambda step: (0, 0)),
            pl.BlockSpec((1, hidden), lambda step: (0, 0)),
        ],
        out_specs=[
            pl.BlockSpec((ROW_BLOCK, hidden), lambda step: (step, 0)),
            pl.BlockSpec((ROW_BLOCK, hidden), lambda step: (step, 0)),
            pl.BlockSpec((ROW_BLOCK, features), lambda step: (step, 0)),
            pl.BlockSpec((1, hidden), lambda step: (0, 0)),
        ],
        out_shape=[
            jax.ShapeDtypeStruct((rows, hidden), jnp.bfloat16),
            jax.ShapeDtypeStruct((rows, hidden), jnp.bfloat16),
            jax.ShapeDtypeStruct((rows, features), jnp.bfloat16),
            jax.ShapeDtypeStruct((1, hidden), jnp.float32),
        ],
        compiler_params=kernel_params(),
        cost_estimate=kernel_cost(1),
    )(act, grad, up_own, down_own, bias_own)


def outer_kernel(left_ref, right_ref, left_two_ref, right_two_ref, out_ref, total_ref):
    step = pl.program_id(0)
    half = pl.num_programs(0) // 2

    def add(left, right):
        total_ref[...] += lax.dot_general(
            left[...], right[...], CONTRACT_ROWS, preferred_element_type=jnp.float32
        )

    @pl.when(step == 0)
    def _():
        total_ref[...] = jnp.zeros_like(total_ref)

    pl.when(step < half)(lambda: add(left_ref, right_ref))
    pl.when(step >= half)(lambda: add(left_two_ref, right_two_ref))

    @pl.when(step == 2 * half - 1)
    def _():
        out_ref[...] = total_ref[...].astype(out_ref.dtype)


def outer_pair(left, right, left_two, right_two):
    rows, width = left.shape
    columns = right.shape[1]
    half = rows // ROW_BLOCK
    first = lambda step: (jnp.minimum(step, half - 1), 0)
    second = lambda step: (jnp.maximum(step - half, 0), 0)
    return pl.pallas_call(
        outer_kernel,
        grid=(2 * half,),
        in_specs=[
            pl.BlockSpec((ROW_BLOCK, width), first),
            pl.BlockSpec((ROW_BLOCK, columns), first),
            pl.BlockSpec((ROW_BLOCK, width), second),
            pl.BlockSpec((ROW_BLOCK, columns), second),
        ],
        out_specs=pl.BlockSpec((width, columns), lambda step: (0, 0)),
        out_shape=jax.ShapeDtypeStruct((width, columns), jnp.bfloat16),
        scratch_shapes=[pltpu.VMEM((width, columns), jnp.float32)],
        compiler_params=kernel_params(),
        cost_estimate=kernel_cost(1),
    )(left, right, left_two, right_two)


def square_grads_kernel(core_ref, *refs):
    step = pl.program_id(0)
    side, x = step // 2, step % 2
    core = jnp.where(side == 0, 1 - core_ref[0], core_ref[0])
    pairs, (send_ref, keep_ref) = refs[:-2], refs[-2:]
    n_y, n_z, _, rows, width = send_ref.shape[1:]
    begin = pl.multiple_of((2 * x + core) * rows, rows)

    def compute(out_ref):
        for which in range(len(pairs) // 2):
            grad = lax.dot_general(
                pairs[2 * which][:, pl.ds(begin, rows)],
                pairs[2 * which + 1][...],
                CONTRACT_ROWS,
                preferred_element_type=jnp.float32,
            ).astype(jnp.bfloat16)
            for y in range(n_y):
                for z in range(n_z):
                    source = (z * n_y + y) * width
                    out_ref[0, y, z, which] = grad[:, source : source + width]

    pl.when(side == 0)(lambda: compute(send_ref))
    pl.when(side == 1)(lambda: compute(keep_ref))


def square_grads(core, pairs, n_y, n_z):
    flat = [array for pair in pairs for array in pair]
    tokens, features = flat[0].shape
    rows = features // 4
    block = (1, n_y, n_z, len(pairs), rows, features // (n_y * n_z))
    shape = jax.ShapeDtypeStruct((2,) + block[1:], jnp.bfloat16)
    return pl.pallas_call(
        square_grads_kernel,
        grid=(4,),
        in_specs=[pl.BlockSpec(memory_space=pltpu.SMEM)]
        + [pl.BlockSpec((tokens, features), lambda step: (0, 0))] * len(flat),
        out_specs=[
            pl.BlockSpec(block, lambda step: (jnp.minimum(step, 1), 0, 0, 0, 0, 0)),
            pl.BlockSpec(block, lambda step: (jnp.maximum(step - 2, 0), 0, 0, 0, 0, 0)),
        ],
        out_shape=[shape, shape],
        compiler_params=kernel_params(),
        cost_estimate=kernel_cost(15),
    )(core, *flat)


tie = lax.optimization_barrier


def low(value):
    return value.astype(jnp.bfloat16)


def wide(value):
    return value.astype(jnp.float32)


def plus(left, right):
    return low(wide(left) + wide(right))


def over(axis, distance, value):
    count = lax.axis_size(axis)
    return lax.ppermute(value, axis, [(i, i ^ distance) for i in range(count)])


def over_core(value):
    return over("fc", 1, value)


def over_x(value):
    return over("fx", 1, value)


def over_y(value):
    return over("cy", 1, value)


def trade_places(value):
    n_z, n_y, n_f = lax.axis_size("cz"), lax.axis_size("cy"), lax.axis_size(FSDP)
    pairs = [
        ((z * n_y + y) * n_f + f, (f * n_y + y) * n_f + z)
        for z in range(n_z)
        for y in range(n_y)
        for f in range(n_f)
    ]
    return lax.ppermute(value, ALL, pairs)


def at(value, index, axis):
    return lax.dynamic_index_in_dim(value, index, axis, keepdims=False)


def pack_kernel(index_ref, *refs):
    begin = 0
    for ref in refs[:-1]:
        size = ref.shape[1]
        refs[-1][:, begin : begin + size] = ref[...]
        begin += size


def swap_columns(w_qkv, w_cross_kv, w_up):
    own, me_y, n_y = lax.axis_index(FSDP), lax.axis_index("cy"), lax.axis_size("cy")
    rows = w_up.shape[0]
    count = lax.axis_size(FSDP) * n_y
    owners = jnp.stack([(own ^ distance) * n_y + me_y for distance in (2, 3, 1, 0)])
    sizes = [PAIR] * 3 + [w_cross_kv.shape[1] // count, w_up.shape[1] // count]
    pieces = pl.pallas_call(
        pack_kernel,
        grid_spec=pltpu.PrefetchScalarGridSpec(
            num_scalar_prefetch=1,
            grid=(4,),
            in_specs=[
                pl.BlockSpec(
                    (rows, PAIR), lambda step, index, part=part: (0, part * count + index[step])
                )
                for part in range(3)
            ]
            + [pl.BlockSpec((rows, size), lambda step, index: (0, index[step])) for size in sizes[3:]],
            out_specs=pl.BlockSpec((rows, sum(sizes)), lambda step, index: (step, 0)),
        ),
        out_shape=jax.ShapeDtypeStruct((4 * rows, sum(sizes)), w_up.dtype),
        compiler_params=kernel_params(),
        cost_estimate=kernel_cost(1),
    )(owners.astype(jnp.int32), w_qkv, w_qkv, w_qkv, w_cross_kv, w_up)
    from_x = over_x(pieces[: 2 * rows])
    from_core = over_core(
        row_major(jnp.concatenate([pieces[2 * rows : 3 * rows], from_x[rows:]], axis=0))
    )
    return [pieces[3 * rows :], from_core[:rows], from_x[:rows], from_core[rows:]]


def rows_in_order(pieces, begin, size):
    own = lax.axis_index(FSDP)
    rows = pieces[0].shape[0]
    whole = jnp.zeros((len(pieces) * rows, size), pieces[0].dtype)
    for distance, piece in enumerate(pieces):
        whole = lax.dynamic_update_slice_in_dim(
            whole, piece[:, begin : begin + size], (own ^ distance) * rows, 0
        )
    return whole


def gather_rows(shard):
    own, me_y = lax.axis_index(FSDP), lax.axis_index("cy")
    rows, columns = shard.shape
    half = rows // 2
    from_x = over_x(lax.dynamic_slice_in_dim(shard, me_y * half, half, 0))
    from_y = over_y(from_x)
    both = jnp.concatenate(
        [shard, jnp.where(me_y == 0, from_x, from_y), jnp.where(me_y == 0, from_y, from_x)], axis=0
    )
    from_core = over_core(row_major(both))
    whole = jnp.zeros((4 * rows, columns), shard.dtype)
    for distance, piece in (
        (0, both[:rows]),
        (2, both[rows:]),
        (1, from_core[:rows]),
        (3, from_core[rows:]),
    ):
        whole = lax.dynamic_update_slice_in_dim(whole, piece, (own ^ distance) * rows, 0)
    return whole


def gather_rest(block, from_y, from_x):
    half = block.shape[0] // 2
    top = over_x(from_y[:half])
    bottom = over_y(from_x[half:])
    mine = jnp.concatenate([block, from_y, from_x, top, bottom], axis=0)
    return mine, over_core(mine)


def gather_plane(block):
    return gather_rest(block, over_y(block), over_x(block))


def scatter_plane(mine, theirs, fill=(None, None, None)):
    rows = mine.shape[0] // 4
    half = rows // 2
    done = []

    def beside(received, work):
        if work is None:
            return received
        received, result = tie((received, work()))
        done.append(result)
        return received

    total = plus(mine, beside(over_core(theirs), fill[0]))
    own, for_y, for_x, diag = (total[i * rows : (i + 1) * rows] for i in range(4))
    top, bottom = beside((over_x(diag[:half]), over_y(diag[half:])), fill[1])
    for_y = jnp.concatenate([plus(for_y[:half], top), for_y[half:]], axis=0)
    for_x = jnp.concatenate([for_x[:half], plus(for_x[half:], bottom)], axis=0)
    from_y, from_x = beside((over_y(for_y), over_x(for_x)), fill[2])
    return wide(own) + wide(from_y) + wide(from_x), done


def sum_everywhere(value, event):
    value = later(value, event)
    for step in (over_core, over_x, over_y):
        value = value + step(value)
    for distance in (1, 2):
        value = value + over("cz", distance, value)
    return value


def after(value, *events):
    return lax.optimization_barrier((value,) + events)[0]


def later(value, event):
    scalar = event[(0,) * event.ndim]
    nothing = jnp.where(scalar != scalar, scalar, jnp.zeros_like(scalar))
    return value + nothing.astype(value.dtype)


def scatter_bits(value, axes=(0, 1, 2)):
    me_f, me_y = lax.axis_index(FSDP), lax.axis_index("cy")
    me_x, me_core = me_f // 2, me_f % 2
    axis_x, axis_core, axis_y = axes
    value = plus(at(value, me_core, axis_core), over_core(at(value, 1 - me_core, axis_core)))
    axis_x -= axis_x > axis_core
    axis_y -= axis_y > axis_core
    value = plus(at(value, me_x, axis_x), over_x(at(value, 1 - me_x, axis_x)))
    axis_y -= axis_y > axis_x
    return plus(at(value, me_y, axis_y), over_y(at(value, 1 - me_y, axis_y)))


def planned_device(
    tokens,
    encoded,
    grad_out,
    doc_lengths,
    src_lengths,
    norm_gain,
    norm_bias,
    w_qkv,
    self_bias,
    w_self_out,
    w_cross_q,
    w_cross_kv,
    cross_bias,
    w_cross_out,
    w_up,
    up_bias,
    w_down,
    down_bias,
):
    q_scale = 1.0 / math.sqrt(HEAD_DIM)
    rows, features = tokens.shape[1:]
    src_own = encoded.shape[1]
    n_z, n_y, n_f = lax.axis_size("cz"), lax.axis_size("cy"), lax.axis_size(FSDP)
    n_ctx = n_z * n_y
    me_y, me_f = lax.axis_index("cy"), lax.axis_index(FSDP)
    own = me_f * n_y + me_y
    shard, hidden = w_up.shape
    slab = hidden // n_ctx
    width = features // n_ctx
    column = 2 * features // n_ctx

    moved = trade_places(jnp.concatenate([tokens[0], encoded[0]], axis=0))
    tok_low, enc_low = moved[:rows], moved[rows:]
    lengths = trade_places(jnp.concatenate([doc_lengths, src_lengths], axis=0))
    head_w = swap_columns(w_qkv, w_cross_kv, w_up)
    tok_low, enc_low, lengths = tie((tok_low, enc_low, lengths))
    qkv_own = rows_in_order(head_w, 0, 3 * PAIR)
    kv_own = rows_in_order(head_w, 3 * PAIR, column)
    up_own = rows_in_order(head_w, 3 * PAIR + column, slab)
    square = gather_rows(jnp.concatenate([w_self_out, w_cross_q, w_cross_out], axis=1))

    own_rows = own * rows + jnp.arange(rows, dtype=jnp.int32)
    tok_pos = stream_position(own_rows, rows, n_ctx)
    doc_starts = jnp.cumsum(lengths[0]) - lengths[0]
    tok_doc = doc_index(doc_starts, tok_pos)
    src_ends = jnp.cumsum(lengths[1])
    span_low = pick_doc(src_ends - lengths[1], tok_doc)
    span_high = pick_doc(src_ends, tok_doc)
    own_index = own.astype(jnp.int32)[None]

    tok_f32 = wide(tok_low)
    ln_one, normed_one, inverse_one = layer_norm(tok_f32, norm_gain[0], norm_bias[0])
    act_one = low(ln_one)
    from_y, from_x = over_y(act_one), over_x(act_one)
    enc_all = lax.all_gather(enc_low, PLANE, axis=0, tiled=True)
    act_mine, act_theirs = gather_rest(act_one, from_y, from_x)
    down_grad_low = trade_places(grad_out[0])
    grad_all = lax.all_gather(down_grad_low, PLANE, axis=0, tiled=False)
    full_self_out, full_cross_q, full_cross_out = (
        square[:, i * features : (i + 1) * features] for i in range(3)
    )

    head_bias = lax.dynamic_slice_in_dim(self_bias, own * PAIR, PAIR, 1)
    qkv_bias = jnp.concatenate([head_bias[0], jnp.zeros_like(head_bias[0]), head_bias[1]])
    qkv_factor = jnp.concatenate([jnp.full((PAIR,), q_scale), jnp.ones((2 * PAIR,))])

    def project(acts):
        return low((plain_dot(acts, qkv_own) + qkv_bias) * qkv_factor.astype(jnp.float32))

    qkv_heads = jnp.concatenate([project(act_mine), project(act_theirs)], axis=0)
    kv_bias = jnp.concatenate([jnp.zeros((features,), jnp.float32), cross_bias[1]])
    kv_columns = low(
        plain_dot(enc_all, kv_own) + lax.dynamic_slice_in_dim(kv_bias, own * column, column, 0)
    )
    kv_cross = lax.all_gather(after(kv_columns, grad_all), PLANE, axis=0, tiled=False)
    down_own = lax.dynamic_slice_in_dim(w_down, me_y * slab, slab, 0)
    att_heads = self_forward(doc_starts, own_index, qkv_heads)
    att_heads, down_own, up_own = tie((att_heads, down_own, up_own))
    att_self = lax.all_to_all(att_heads, PLANE, 0, 1, tiled=True)
    order = (0, 1, 4, 5, 2, 3, 6, 7)
    grad_mine = jnp.concatenate([at(grad_all, own ^ k, 0) for k in order[:4]], axis=0)
    grad_theirs = jnp.concatenate([at(grad_all, own ^ k, 0) for k in order[4:]], axis=0)

    hidden_one = tok_f32 + plain_dot(att_self, full_self_out) + self_bias[2]
    ln_two, normed_two, inverse_two = layer_norm(hidden_one, norm_gain[1], norm_bias[1])
    act_two = low(ln_two)
    q_cross = low((plain_dot(act_two, full_cross_q) + cross_bias[0]) * q_scale)
    att_cross = cross_forward(q_cross, kv_cross, span_low, span_high)
    hidden_two = hidden_one + plain_dot(att_cross, full_cross_out) + cross_bias[2]

    ln_three, normed_three, inverse_three = layer_norm(hidden_two, norm_gain[2], norm_bias[2])
    three_mine, three_theirs = gather_plane(low(ln_three))
    bias_own = lax.dynamic_slice_in_dim(up_bias, own * slab, slab, 0).reshape(1, -1)
    gelu_theirs, pre_theirs, part_theirs, sum_theirs = mlp_forward_back(
        three_theirs, grad_theirs, up_own, down_own, bias_own
    )
    gelu_mine, pre_mine, part_mine, sum_mine = mlp_forward_back(
        three_mine, grad_mine, up_own, down_own, bias_own
    )

    part_mine, three_mine, three_theirs, grad_mine, grad_theirs, act_mine, act_theirs = tie(
        (part_mine, three_mine, three_theirs, grad_mine, grad_theirs, act_mine, act_theirs)
    )
    act_grad, (up_grad, down_grad, out_sent) = scatter_plane(
        part_mine,
        part_theirs,
        (
            lambda: outer_pair(three_mine, pre_mine, three_theirs, pre_theirs),
            lambda: outer_pair(grad_mine, gelu_mine, grad_theirs, gelu_theirs),
            lambda: low(plain_dot(gelu_theirs, down_own)),
        ),
    )
    up_grad = lax.psum_scatter(up_grad, "cz", scatter_dimension=0, tiled=True)
    down_grad = lax.psum_scatter(down_grad, "cz", scatter_dimension=0, tiled=True)
    out_mine = low(plain_dot(gelu_mine, down_own))

    upstream = wide(down_grad_low)
    grad_down_bias = jnp.sum(upstream, axis=0)
    norm_in_three, gain_grad_three, shift_grad_three = norm_back(
        act_grad, normed_three, inverse_three, norm_gain[2]
    )
    grad_two = upstream + norm_in_three
    cross_grad_low = low(grad_two)
    cross_out_bias_grad = jnp.sum(wide(cross_grad_low), axis=0)
    cross_att_grad = low(times_transpose(cross_grad_low, full_cross_out))
    cross_v_bias_grad = jnp.sum(wide(cross_att_grad), axis=0)

    up_bias_grad = (sum_mine + sum_theirs)[0]

    me_x, me_core = me_f // 2, me_f % 2
    cross_q_low, cross_kv_part = cross_backward(
        q_cross, kv_cross, cross_att_grad, span_low, span_high
    )
    cross_q_bias_grad = jnp.sum(wide(cross_q_low), axis=0)
    norm_in_two, gain_grad_two, shift_grad_two = norm_back(
        times_transpose(cross_q_low, full_cross_q), normed_two, inverse_two, norm_gain[1]
    )
    grad_one = grad_two + norm_in_two
    self_grad_low = low(grad_one)
    self_att_grad = low(times_transpose(self_grad_low, full_self_out))
    self_v_bias_grad = jnp.sum(wide(self_att_grad), axis=0)
    kv_part = cross_kv_part.reshape(2, 2, 2, 2, enc_all.shape[0], PAIR)
    kv_other = over_core(at(kv_part, 1 - me_core, 1))
    self_att_grad, up_grad, kv_other = tie((self_att_grad, up_grad, kv_other))
    att_grad_heads = lax.all_to_all(self_att_grad, PLANE, 1, 0, tiled=True)
    kv_part = plus(at(kv_part, me_core, 1), kv_other)
    kv_other = over_x(at(kv_part, 1 - me_x, 0))

    send, keep = square_grads(
        me_core.astype(jnp.int32)[None],
        (
            (att_self, after(self_grad_low, self_att_grad)),
            (act_two, cross_q_low),
            (att_cross, cross_grad_low),
        ),
        n_y,
        n_z,
    )
    self_out_bias_grad = jnp.sum(wide(self_grad_low), axis=0)
    three = plus(keep, row_major(over_core(send)))
    out_sum = plus(out_mine, over_core(after(out_sent, self_att_grad)))
    att_grad_heads, kv_other, three, out_sum = tie((att_grad_heads, kv_other, three, out_sum))
    kv_part = plus(at(kv_part, me_x, 0), kv_other)
    kv_other = over_y(at(kv_part, 1 - me_y, 0))
    left, right = three[:, :, : n_z // 2], three[:, :, n_z // 2 :]
    left_other = over_x(at(left, 1 - me_x, 0))
    right_other = over_y(at(right, 1 - me_y, 1))
    out_own, out_y, out_x, out_diag = (out_sum[i * rows : (i + 1) * rows] for i in range(4))
    half_rows = rows // 2
    out_top, out_bottom = over_x(out_diag[:half_rows]), over_y(out_diag[half_rows:])

    proj_grad = self_backward(doc_starts, own_index, qkv_heads, att_grad_heads)
    half = proj_grad.shape[0] // 2

    def lane_blocks(value):
        return [
            value[:, i : i + PAIR].reshape(n_z, 1, shard, PAIR)
            for i in range(0, value.shape[1], PAIR)
        ]

    def project_back():
        weight = outer_rows(act_mine, proj_grad[:half]) + outer_rows(act_theirs, proj_grad[half:])
        sums = jnp.sum(wide(proj_grad), axis=0)[None]
        shift = jnp.sum(wide(qkv_own) * sums, axis=1)
        gain = jnp.sum(wide(qkv_own) * weight, axis=1) - norm_bias[0] * shift
        return row_major(low(weight)), sums[0], gain / norm_gain[0], shift

    act_grad, ((qkv_grad, proj_sums, gain_grad_one, shift_grad_one),) = scatter_plane(
        low(times_transpose(proj_grad[:half], qkv_own)),
        low(times_transpose(proj_grad[half:], qkv_own)),
        (project_back, None, None),
    )
    down_cols = later(down_grad, act_grad).reshape(n_y, width, slab)
    other = over_y(at(down_cols, 1 - me_y, 0))
    mine = at(down_cols, me_y, 0)

    left = later(plus(at(left, me_x, 0), left_other), act_grad)
    right = later(plus(at(right, me_y, 1), right_other), act_grad)
    left, left_send = at(left, me_y, 0), at(left, 1 - me_y, 0)
    right, right_send = at(right, me_x, 0), at(right, 1 - me_x, 0)
    out_y = jnp.concatenate([plus(out_y[:half_rows], out_top), out_y[half_rows:]], axis=0)
    out_x = jnp.concatenate([out_x[:half_rows], plus(out_x[half_rows:], out_bottom)], axis=0)
    out_y, out_x = later(out_y, act_grad), later(out_x, act_grad)
    mlp_out = wide(out_own) + wide(over_y(out_y)) + wide(over_x(out_x))
    layer_out = trade_places(low(hidden_two + mlp_out + down_bias))
    self_q_bias_grad = proj_sums[:PAIR]
    cross_kv_grad = plus(at(kv_part, me_y, 0), kv_other)
    cross_kv_grad = jnp.concatenate([cross_kv_grad[0], cross_kv_grad[1]], axis=1)
    grad_encoded = wide(
        trade_places(
            scatter_bits(
                after(low(times_transpose(cross_kv_grad, kv_own)), act_grad).reshape(
                    2, 2, 2, src_own, features
                )
            )
        )
    )
    cross_kv_grad = low(outer_rows(enc_all, cross_kv_grad))
    rest = jnp.concatenate(lane_blocks(cross_kv_grad) + lane_blocks(qkv_grad), axis=1)
    rest = lax.psum_scatter(row_major(rest), "cz", scatter_dimension=0, tiled=False)
    three = jnp.concatenate(
        [
            later(plus(left, over_y(left_send)), rest),
            later(plus(right, over_x(right_send)), rest),
        ],
        axis=0,
    )
    three = wide(lax.psum_scatter(row_major(three), "cz", scatter_dimension=0, tiled=False))
    kv_blocks = trade_places(rest[:2])
    grad_w_cross_kv = wide(jnp.concatenate([kv_blocks[0], kv_blocks[1]], axis=1))
    qkv_grad = rest[2:]

    norm_in_one, _, _ = norm_back(act_grad, normed_one, inverse_one, norm_gain[0])
    grad_tokens = low(grad_one + norm_in_one)
    grad_w_up = wide(trade_places(later(up_grad, proj_grad)))
    grad_tokens = wide(trade_places(grad_tokens))

    down_halves = jnp.stack([jnp.where(me_y == 0, mine, other), jnp.where(me_y == 0, other, mine)])
    grad_w_down = wide(jnp.transpose(down_halves, (0, 2, 1)).reshape(n_y * slab, width))

    qkv_blocks = []
    inverse_of_three = pow(3, -1, n_ctx)
    for slot in range(3):
        pairs = []
        for dest in range(n_ctx):
            source = (3 * dest + slot) % n_ctx
            for z in range(n_z):
                pairs.append(
                    ((z * n_y + source % n_y) * n_f + source // n_y, dest * n_f + z)
                )
        part = (3 * ((inverse_of_three * (own - slot)) % n_ctx) + slot) // n_ctx
        qkv_blocks.append(lax.ppermute(at(qkv_grad, part, 0), ALL, pairs))
    grad_w_qkv = wide(jnp.concatenate(qkv_blocks, axis=1))

    def placed(part):
        whole = jnp.zeros((n_ctx * part.shape[0],), jnp.float32)
        return lax.dynamic_update_slice_in_dim(whole, part, own * part.shape[0], 0).reshape(
            -1, features
        )

    level = jnp.stack(
        [
            gain_grad_one,
            gain_grad_two,
            gain_grad_three,
            shift_grad_one,
            shift_grad_two,
            shift_grad_three,
            self_v_bias_grad,
            self_out_bias_grad,
            cross_q_bias_grad,
            cross_v_bias_grad,
            cross_out_bias_grad,
            grad_down_bias,
        ]
    )
    level = sum_everywhere(
        jnp.concatenate([level, placed(self_q_bias_grad), placed(up_bias_grad)], axis=0), act_grad
    )
    grad_up_bias = level[13:].reshape(hidden)

    return (
        layer_out[None],
        grad_tokens[None],
        grad_encoded[None],
        level[0:3],
        level[3:6],
        grad_w_qkv,
        jnp.concatenate([level[12:13], level[6:8]], axis=0),
        three[0],
        three[1],
        grad_w_cross_kv,
        level[8:11],
        three[2],
        grad_w_up,
        grad_up_bias,
        grad_w_down,
        level[11],
    )


def planned_solution(mesh):
    n_ctx, n_f = mesh.shape["ctx"], mesh.shape["fsdp"]
    split = Mesh(mesh.devices.reshape(n_ctx // 2, 2, n_f // 2, 2), ALL)
    token = P(FSDP, CTX, None)
    row = P(FSDP, None)
    owned = P(FSDP, CTX)
    return jax.shard_map(
        planned_device,
        mesh=split,
        in_specs=(token, token, token, row, row, P(), P(), row, P(), row, row, row, P(), row)
        + (row, P(), row, P()),
        out_specs=(token, token, token, P(), P(), owned, P(), owned, owned, owned, P(), owned)
        + (owned, P(), owned, P()),
        check_vma=False,
    )


def solution(mesh):
    if mesh.shape["ctx"] * 2 == HEADS and mesh.shape["fsdp"] * 2 == mesh.shape["ctx"]:
        return planned_solution(mesh)
    return general_solution(mesh)
```

```python
import functools
import math

import jax
import jax.numpy as jnp
from jax import lax
from jax.experimental import pallas as pl
from jax.experimental.layout import Layout, with_layout_constraint
from jax.experimental.pallas import tpu as pltpu
from jax.sharding import Mesh
from jax.sharding import PartitionSpec as P

HEADS = 16
HEAD_DIM = 64
KBLOCK = 512


EPS = 1e-05
NEG = -1e30
GELU_C = 0.7978845608028654
GELU_A = 0.044715
CONTRACT_ROWS = (((0,), (0,)), ((), ()))
CONTRACT_COLS = (((1,), (1,)), ((), ()))


def shortened(shard):
    return jax.tree.map(lambda a: a.astype(jnp.bfloat16) if a.dtype == jnp.float32 else a, shard)


def gelu_value(pre):
    return 0.5 * pre * (1.0 + jnp.tanh(GELU_C * (pre + GELU_A * pre * pre * pre)))


def gelu_slope(pre):
    tangent = jnp.tanh(GELU_C * (pre + GELU_A * pre * pre * pre))
    return 0.5 * (1.0 + tangent) + 0.5 * pre * (1.0 - tangent * tangent) * GELU_C * (
        1.0 + 3.0 * GELU_A * pre * pre
    )


def stream_position(rows, tok_dev, ctx_count):
    half = tok_dev // 2
    device = rows // tok_dev
    within = rows % tok_dev
    early = device * half + within
    late = (2 * ctx_count - 1 - device) * half + (within - half)
    return jnp.where(within < half, early, late)


def layer_norm(inputs, gain_row, shift_row):
    center = inputs - jnp.mean(inputs, axis=1, keepdims=True)
    inverse = lax.rsqrt(jnp.mean(center * center, axis=1, keepdims=True) + EPS)
    normed = center * inverse
    return (normed * gain_row + shift_row, normed, inverse)


def norm_back(upstream, normed, inverse, gain_row):
    scaled = upstream * gain_row
    mean_plain = jnp.mean(scaled, axis=1, keepdims=True)
    mean_normed = jnp.mean(scaled * normed, axis=1, keepdims=True)
    return (
        inverse * (scaled - mean_plain - normed * mean_normed),
        jnp.sum(upstream * normed, axis=0),
        jnp.sum(upstream, axis=0),
    )


def outer_rows(left, right):
    return lax.dot_general(left, right, CONTRACT_ROWS, preferred_element_type=jnp.float32)


def times_transpose(left, right):
    return lax.dot_general(left, right, CONTRACT_COLS, preferred_element_type=jnp.float32)


def plain_dot(left, right):
    return jnp.dot(left, right, preferred_element_type=jnp.float32)


def doc_index(doc_starts, positions):
    counted = jnp.sum((doc_starts[None, :] <= positions[:, None]).astype(jnp.int32), axis=1)
    return counted - 1


def pick_doc(lookup, doc_ids):
    onehot = doc_ids[:, None] == jnp.arange(lookup.shape[0], dtype=jnp.int32)[None, :]
    return jnp.sum(jnp.where(onehot, lookup[None, :], 0), axis=1)


def split_heads(matrix):
    return matrix.reshape(matrix.shape[0], HEADS, matrix.shape[1] // HEADS)


def split_pair(kv_piece):
    half_width = kv_piece.shape[1] // 2
    return (split_heads(kv_piece[:, :half_width]), split_heads(kv_piece[:, half_width:]))


def key_block(kv_whole, block_start):
    return split_pair(lax.dynamic_slice_in_dim(kv_whole, block_start, KBLOCK, 0))


def block_starts(kv_whole):
    return jnp.arange(kv_whole.shape[0] // KBLOCK, dtype=jnp.int32) * KBLOCK


def score_block(queries, key_heads):
    return jnp.einsum("qhd,khd->hqk", queries, key_heads, preferred_element_type=jnp.float32)


def attend(queries, kv_whole, allowed_fn):
    shape_stat = (queries.shape[1], queries.shape[0])

    def stat_step(state_pair, block_start):
        allowed = allowed_fn(block_start)

        def stat_compute_block(running):
            running_top, running_sum = running
            key_heads, value_heads = key_block(kv_whole, block_start)
            masked = jnp.where(allowed[None], score_block(queries, key_heads), NEG)
            new_top = jnp.maximum(running_top, jnp.max(masked, axis=2))
            exp_terms = jnp.where(allowed[None], jnp.exp(masked - new_top[:, :, None]), 0.0)
            return (
                new_top,
                running_sum * jnp.exp(running_top - new_top) + jnp.sum(exp_terms, axis=2),
            )

        return (
            lax.cond(jnp.any(allowed), stat_compute_block, lambda running: running, state_pair),
            None,
        )

    initial = (jnp.full(shape_stat, NEG, jnp.float32), jnp.zeros(shape_stat, jnp.float32))
    (final_top, final_sum), _ = lax.scan(stat_step, initial, block_starts(kv_whole))
    logsum = final_top + jnp.log(final_sum)

    def value_step(running, block_start):
        allowed = allowed_fn(block_start)

        def value_compute_block(partial_value):
            key_heads, value_heads = key_block(kv_whole, block_start)
            raw_scores = score_block(queries, key_heads)
            prob_low = jnp.where(
                allowed[None], jnp.exp(raw_scores - logsum[:, :, None]), 0.0
            ).astype(jnp.bfloat16)
            return partial_value + jnp.einsum(
                "hqk,khd->qhd", prob_low, value_heads, preferred_element_type=jnp.float32
            )

        return (
            lax.cond(
                jnp.any(allowed), value_compute_block, lambda partial_value: partial_value, running
            ),
            None,
        )

    attended, _ = lax.scan(
        value_step, jnp.zeros(queries.shape, jnp.float32), block_starts(kv_whole)
    )
    return (attended, logsum)


def score_grads(queries, key_heads, value_heads, grad_heads, logsum, row_delta, allowed):
    raw_scores = score_block(queries, key_heads)
    probs_full = jnp.where(allowed[None], jnp.exp(raw_scores - logsum[:, :, None]), 0.0)
    grad_probs = jnp.einsum(
        "qhd,khd->hqk", grad_heads, value_heads, preferred_element_type=jnp.float32
    )
    grad_scores = (probs_full * (grad_probs - row_delta[:, :, None])).astype(jnp.bfloat16)
    return (probs_full, grad_scores)


def key_terms(queries, key_heads, value_heads, grad_heads, logsum, row_delta, allowed):
    probs_full, grad_scores = score_grads(
        queries, key_heads, value_heads, grad_heads, logsum, row_delta, allowed
    )
    grad_keys = jnp.einsum("hqk,qhd->khd", grad_scores, queries, preferred_element_type=jnp.float32)
    grad_values = jnp.einsum(
        "hqk,qhd->khd",
        probs_full.astype(jnp.bfloat16),
        grad_heads,
        preferred_element_type=jnp.float32,
    )
    key_count = key_heads.shape[0]
    return jnp.concatenate(
        [grad_keys.reshape(key_count, -1), grad_values.reshape(key_count, -1)], axis=1
    )


def row_deltas(grad_heads, attended):
    return jnp.einsum("qhd,qhd->hq", grad_heads.astype(jnp.float32), attended)


def query_back(queries, kv_whole, allowed_fn, logsum, row_delta, grad_heads):

    def query_grad_step(partial_value, block_start):
        allowed = allowed_fn(block_start)

        def query_compute_block(running):
            key_heads, value_heads = key_block(kv_whole, block_start)
            probs_full, grad_scores = score_grads(
                queries, key_heads, value_heads, grad_heads, logsum, row_delta, allowed
            )
            return running + jnp.einsum(
                "hqk,khd->qhd", grad_scores, key_heads, preferred_element_type=jnp.float32
            )

        return (
            lax.cond(jnp.any(allowed), query_compute_block, lambda running: running, partial_value),
            None,
        )

    grad_query, _ = lax.scan(
        query_grad_step, jnp.zeros(queries.shape, jnp.float32), block_starts(kv_whole)
    )
    return grad_query


def attend_back(queries, kv_whole, allowed_fn, attended, logsum, grad_heads):
    row_delta = row_deltas(grad_heads, attended)

    def attend_grad_step(grad_query, block_start):
        allowed = allowed_fn(block_start)

        def attend_compute_block(partial_value):
            key_heads, value_heads = key_block(kv_whole, block_start)
            probs_full, grad_scores = score_grads(
                queries, key_heads, value_heads, grad_heads, logsum, row_delta, allowed
            )
            partial_value = partial_value + jnp.einsum(
                "hqk,khd->qhd", grad_scores, key_heads, preferred_element_type=jnp.float32
            )
            grad_keys = jnp.einsum(
                "hqk,qhd->khd", grad_scores, queries, preferred_element_type=jnp.float32
            )
            grad_values = jnp.einsum(
                "hqk,qhd->khd",
                probs_full.astype(jnp.bfloat16),
                grad_heads,
                preferred_element_type=jnp.float32,
            )
            return (
                partial_value,
                jnp.concatenate(
                    [grad_keys.reshape(KBLOCK, -1), grad_values.reshape(KBLOCK, -1)], axis=1
                ),
            )

        def attend_skip_block(partial_value):
            return (partial_value, jnp.zeros((KBLOCK, kv_whole.shape[1]), jnp.float32))

        return lax.cond(jnp.any(allowed), attend_compute_block, attend_skip_block, grad_query)

    grad_query, kv_terms = lax.scan(
        attend_grad_step, jnp.zeros(queries.shape, jnp.float32), block_starts(kv_whole)
    )
    return (grad_query, kv_terms.reshape(kv_whole.shape[0], kv_whole.shape[1]))


def owners_end(grads):
    columns = jax.tree.map(
        lambda part: part.astype(jnp.float32),
        lax.psum_scatter(shortened(grads), "ctx", scatter_dimension=1, tiled=True),
    )
    return jax.tree.map(
        lambda part: part.astype(jnp.float32),
        lax.psum_scatter(shortened(columns), "fsdp", scatter_dimension=0, tiled=True),
    )


def per_device(
    tokens,
    encoded,
    grad_out,
    doc_lengths,
    src_lengths,
    norm_gain,
    norm_bias,
    w_qkv,
    self_bias,
    w_self_out,
    w_cross_q,
    w_cross_kv,
    cross_bias,
    w_cross_out,
    w_up,
    up_bias,
    w_down,
    down_bias,
):
    q_scale = 1.0 / math.sqrt(HEAD_DIM)
    tok_rows = tokens.shape[1]
    features = tokens.shape[2]
    ctx_count = lax.axis_size("ctx")
    ctx_index = lax.axis_index("ctx")
    own_rows = ctx_index * tok_rows + jnp.arange(tok_rows, dtype=jnp.int32)
    tok_pos = stream_position(own_rows, tok_rows, ctx_count)
    lengths_row = doc_lengths[0]
    doc_starts = jnp.cumsum(lengths_row) - lengths_row
    tok_doc = doc_index(doc_starts, tok_pos)
    src_row = src_lengths[0]
    src_ends = jnp.cumsum(src_row)
    src_starts = src_ends - src_row
    span_low = pick_doc(src_starts, tok_doc)
    span_high = pick_doc(src_ends, tok_doc)

    def self_mask(key_rows):
        key_pos = stream_position(key_rows, tok_rows, ctx_count)
        key_doc = doc_index(doc_starts, key_pos)
        return (key_pos[None, :] <= tok_pos[:, None]) & (key_doc[None, :] == tok_doc[:, None])

    def self_allowed(block_start):
        return self_mask(block_start + jnp.arange(KBLOCK, dtype=jnp.int32))

    def cross_allowed(block_start):
        key_pos = block_start + jnp.arange(KBLOCK, dtype=jnp.int32)
        return (key_pos[None, :] >= span_low[:, None]) & (key_pos[None, :] < span_high[:, None])

    def gather_self():
        return (
            lax.all_gather(w_qkv, "fsdp", axis=0, tiled=True),
            lax.all_gather(w_self_out, "fsdp", axis=0, tiled=True),
        )

    def gather_cross():
        return (
            lax.all_gather(w_cross_q, "fsdp", axis=0, tiled=True),
            lax.all_gather(w_cross_kv, "fsdp", axis=0, tiled=True),
            lax.all_gather(w_cross_out, "fsdp", axis=0, tiled=True),
        )

    def gather_mlp():
        return (
            lax.all_gather(w_up, "fsdp", axis=0, tiled=True),
            lax.all_gather(w_down, "fsdp", axis=0, tiled=True),
        )

    tok_f32 = tokens[0].astype(jnp.float32)
    enc_low = encoded[0]
    ln_one, normed_one, inverse_one = layer_norm(tok_f32, norm_gain[0], norm_bias[0])
    act_one = ln_one.astype(jnp.bfloat16)
    full_qkv, full_self_out = gather_self()
    projected = plain_dot(act_one, full_qkv)
    q_self = ((projected[:, :features] + self_bias[0]) * q_scale).astype(jnp.bfloat16)
    kv_self = jnp.concatenate(
        [projected[:, features : 2 * features], projected[:, 2 * features :] + self_bias[1]], axis=1
    ).astype(jnp.bfloat16)
    kv_self_all = lax.all_gather(kv_self, "ctx", axis=0, tiled=True)
    self_heads = split_heads(q_self)
    att_self, lse_self = attend(self_heads, kv_self_all, self_allowed)
    att_self_low = att_self.reshape(tok_rows, features).astype(jnp.bfloat16)
    hidden_one = tok_f32 + plain_dot(att_self_low, full_self_out) + self_bias[2]
    ln_two, normed_two, inverse_two = layer_norm(hidden_one, norm_gain[1], norm_bias[1])
    act_two = ln_two.astype(jnp.bfloat16)
    full_cross_q, full_cross_kv, full_cross_out = gather_cross()
    q_cross = ((plain_dot(act_two, full_cross_q) + cross_bias[0]) * q_scale).astype(jnp.bfloat16)
    src_proj = plain_dot(enc_low, full_cross_kv)
    kv_cross = jnp.concatenate(
        [src_proj[:, :features], src_proj[:, features:] + cross_bias[1]], axis=1
    ).astype(jnp.bfloat16)
    kv_cross_all = lax.all_gather(kv_cross, "ctx", axis=0, tiled=True)
    cross_heads = split_heads(q_cross)
    att_cross, lse_cross = attend(cross_heads, kv_cross_all, cross_allowed)
    att_cross_low = att_cross.reshape(tok_rows, features).astype(jnp.bfloat16)
    hidden_two = hidden_one + plain_dot(att_cross_low, full_cross_out) + cross_bias[2]
    ln_three, normed_three, inverse_three = layer_norm(hidden_two, norm_gain[2], norm_bias[2])
    act_three = ln_three.astype(jnp.bfloat16)
    full_up, full_down = gather_mlp()
    pre_act = plain_dot(act_three, full_up) + up_bias
    gelu_low = gelu_value(pre_act).astype(jnp.bfloat16)
    layer_out = (hidden_two + plain_dot(gelu_low, full_down) + down_bias).astype(jnp.bfloat16)
    upstream = grad_out[0].astype(jnp.float32)
    down_grad_low = grad_out[0]
    full_up, full_down = gather_mlp()
    grad_w_down = outer_rows(gelu_low, down_grad_low)
    grad_down_bias = jnp.sum(upstream, axis=0)
    gelu_grad = times_transpose(down_grad_low, full_down)
    pre_grad_low = (gelu_grad * gelu_slope(pre_act)).astype(jnp.bfloat16)
    grad_w_up = outer_rows(act_three, pre_grad_low)
    grad_up_bias = jnp.sum(pre_grad_low.astype(jnp.float32), axis=0)
    norm_in_three, gain_grad_three, shift_grad_three = norm_back(
        times_transpose(pre_grad_low, full_up), normed_three, inverse_three, norm_gain[2]
    )
    grad_two = upstream + norm_in_three
    full_cross_q, full_cross_kv, full_cross_out = gather_cross()
    cross_grad_low = grad_two.astype(jnp.bfloat16)
    grad_w_cross_out = outer_rows(att_cross_low, cross_grad_low)
    cross_out_bias_grad = jnp.sum(cross_grad_low.astype(jnp.float32), axis=0)
    cross_att_grad = split_heads(
        times_transpose(cross_grad_low, full_cross_out).astype(jnp.bfloat16)
    )
    cross_q_grad, cross_kv_terms = attend_back(
        cross_heads, kv_cross_all, cross_allowed, att_cross, lse_cross, cross_att_grad
    )
    cross_kv_grad = lax.psum_scatter(
        cross_kv_terms.astype(jnp.bfloat16), "ctx", scatter_dimension=0, tiled=True
    )
    cross_q_low = (cross_q_grad.reshape(tok_rows, features) * q_scale).astype(jnp.bfloat16)
    grad_w_cross_q = outer_rows(act_two, cross_q_low)
    cross_q_bias_grad = jnp.sum(cross_q_low.astype(jnp.float32), axis=0)
    grad_w_cross_kv = outer_rows(enc_low, cross_kv_grad)
    cross_v_bias_grad = jnp.sum(cross_kv_grad[:, features:].astype(jnp.float32), axis=0)
    grad_encoded = times_transpose(cross_kv_grad, full_cross_kv)
    norm_in_two, gain_grad_two, shift_grad_two = norm_back(
        times_transpose(cross_q_low, full_cross_q), normed_two, inverse_two, norm_gain[1]
    )
    grad_one = grad_two + norm_in_two
    full_qkv, full_self_out = gather_self()
    self_grad_low = grad_one.astype(jnp.bfloat16)
    grad_w_self_out = outer_rows(att_self_low, self_grad_low)
    self_out_bias_grad = jnp.sum(self_grad_low.astype(jnp.float32), axis=0)
    self_att_flat = times_transpose(self_grad_low, full_self_out).astype(jnp.bfloat16)
    self_att_grad = split_heads(self_att_flat)
    self_delta = row_deltas(self_att_grad, att_self)
    self_q_grad = query_back(
        self_heads, kv_self_all, self_allowed, lse_self, self_delta, self_att_grad
    )

    def one_piece(sub_start):
        key_rows = sub_start + jnp.arange(tok_rows, dtype=jnp.int32)
        allowed = self_mask(key_rows)

        def one_compute_block(piece_start):
            key_heads, value_heads = split_pair(
                lax.dynamic_slice_in_dim(kv_self_all, piece_start, tok_rows, 0)
            )
            return key_terms(
                self_heads, key_heads, value_heads, self_att_grad, lse_self, self_delta, allowed
            )

        def one_skip_block(piece_start):
            return jnp.zeros((tok_rows, 2 * features), jnp.float32)

        return lax.cond(jnp.any(allowed), one_compute_block, one_skip_block, sub_start)

    piece_starts = (
        jnp.arange(tok_rows * lax.axis_size("ctx") // tok_rows, dtype=jnp.int32) * tok_rows
    )
    self_kv_grad = lax.psum_scatter(
        lax.map(one_piece, piece_starts)
        .reshape(tok_rows * lax.axis_size("ctx"), 2 * features)
        .astype(jnp.bfloat16),
        "ctx",
        scatter_dimension=0,
        tiled=True,
    )
    self_q_low = (self_q_grad.reshape(tok_rows, features) * q_scale).astype(jnp.bfloat16)
    proj_grad_low = jnp.concatenate([self_q_low, self_kv_grad], axis=1)
    grad_w_qkv = outer_rows(act_one, proj_grad_low)
    self_q_bias_grad = jnp.sum(self_q_low.astype(jnp.float32), axis=0)
    self_v_bias_grad = jnp.sum(self_kv_grad[:, features:].astype(jnp.float32), axis=0)
    norm_in_one, gain_grad_one, shift_grad_one = norm_back(
        times_transpose(proj_grad_low, full_qkv), normed_one, inverse_one, norm_gain[0]
    )
    grad_tokens = grad_one + norm_in_one
    owned = owners_end(
        (
            grad_w_qkv,
            grad_w_self_out,
            grad_w_cross_q,
            grad_w_cross_kv,
            grad_w_cross_out,
            grad_w_up,
            grad_w_down,
        )
    )
    gain_grads = jnp.stack([gain_grad_one, gain_grad_two, gain_grad_three])
    shift_grads = jnp.stack([shift_grad_one, shift_grad_two, shift_grad_three])
    self_bias_grads = jnp.stack([self_q_bias_grad, self_v_bias_grad, self_out_bias_grad])
    cross_bias_grads = jnp.stack([cross_q_bias_grad, cross_v_bias_grad, cross_out_bias_grad])
    summed = lax.psum(
        (gain_grads, shift_grads, self_bias_grads, cross_bias_grads, grad_up_bias, grad_down_bias),
        ("ctx", "fsdp"),
    )
    return (
        layer_out[None],
        grad_tokens[None],
        grad_encoded[None],
        summed[0],
        summed[1],
        owned[0],
        summed[2],
        owned[1],
        owned[2],
        owned[3],
        summed[3],
        owned[4],
        owned[5],
        summed[4],
        owned[6],
        summed[5],
    )


def general_solution(mesh):
    placed = (
        P("fsdp", "ctx", None),
        P("fsdp", "ctx", None),
        P("fsdp", "ctx", None),
        P("fsdp", None),
        P("fsdp", None),
        P(),
        P(),
        P("fsdp", None),
        P(),
        P("fsdp", None),
        P("fsdp", None),
        P("fsdp", None),
        P(),
        P("fsdp", None),
        P("fsdp", None),
        P(),
        P("fsdp", None),
        P(),
    )
    return jax.shard_map(
        per_device,
        mesh=mesh,
        in_specs=placed,
        out_specs=(
            P("fsdp", "ctx", None),
            P("fsdp", "ctx", None),
            P("fsdp", "ctx", None),
            P(),
            P(),
            P("fsdp", "ctx"),
            P(),
            P("fsdp", "ctx"),
            P("fsdp", "ctx"),
            P("fsdp", "ctx"),
            P(),
            P("fsdp", "ctx"),
            P("fsdp", "ctx"),
            P(),
            P("fsdp", "ctx"),
            P(),
        ),
        check_vma=False,
    )


CTX = ("cz", "cy")
FSDP = ("fx", "fc")
PLANE = ("fx", "fc", "cy")
ALL = ("cz", "cy", "fx", "fc")
ROW_BLOCK = 512
HIDDEN_BLOCK = 256
QBLOCK = 256
HALF = 128
PAIR = 2 * HEAD_DIM
MAX_KEY_BLOCKS = 5


def kernel_cost(microseconds):
    return pl.CostEstimate(
        flops=int(microseconds * 1.15e9), bytes_accessed=1 << 20, transcendentals=0
    )


def row_major(value):
    return with_layout_constraint(value, Layout(tuple(range(value.ndim))))


def doc_start_of(starts_ref, positions):
    first = jnp.zeros_like(positions)
    for doc in range(starts_ref.shape[0]):
        begin = starts_ref[doc]
        first = jnp.where(positions >= begin, begin, first)
    return first


def doc_start_scalar(starts_ref, position):
    first = jnp.int32(0)
    for doc in range(starts_ref.shape[0]):
        begin = starts_ref[doc]
        first = jnp.where(position >= begin, begin, first)
    return first


def half_row(pos_block, pos_blocks):
    early = pos_block * (2 * HALF)
    late = (pos_blocks - 1 - pos_block) * (2 * HALF) + HALF
    return pl.multiple_of(jnp.where(2 * pos_block < pos_blocks, early, late), HALF)


def slot_of(distance):
    return (distance & 1) + 2 * ((distance >> 2) & 1) + 4 * ((distance >> 1) & 1)


def slot_row(row, own):
    block = row // (2 * HALF)
    slot = slot_of(block ^ own)
    return pl.multiple_of(slot * (2 * HALF) + row - block * (2 * HALF), HALF)


def lane_mask(rows, head):
    lanes = lax.broadcasted_iota(jnp.int32, (rows, PAIR), 1)
    return (lanes >= head * HEAD_DIM) & (lanes < (head + 1) * HEAD_DIM)


def to_positions(own, src_ref, column, dst_ref):
    pos_blocks = src_ref.shape[0] // HALF

    def move(block, carry):
        row = slot_row(half_row(block, pos_blocks), own)
        dst_ref[pl.ds(pl.multiple_of(block * HALF, HALF), HALF), :] = src_ref[
            pl.ds(row, HALF), pl.ds(column, PAIR)
        ]
        return carry

    lax.fori_loop(0, pos_blocks, move, 0)


def self_forward_kernel(starts_ref, own_ref, qkv_ref, out_ref, key_ref, value_ref):
    step = pl.program_id(0)
    own = own_ref[0]
    pos_blocks = qkv_ref.shape[0] // HALF

    @pl.when(step == 0)
    def _():
        to_positions(own, qkv_ref, PAIR, key_ref)
        to_positions(own, qkv_ref, 2 * PAIR, value_ref)

    row_a = half_row(2 * step, pos_blocks)
    row_b = half_row(2 * step + 1, pos_blocks)
    slot_a, slot_b = slot_row(row_a, own), slot_row(row_b, own)
    queries = jnp.concatenate(
        [qkv_ref[pl.ds(slot_a, HALF), pl.ds(0, PAIR)], qkv_ref[pl.ds(slot_b, HALF), pl.ds(0, PAIR)]],
        axis=0,
    )
    q_start = step * QBLOCK
    first_block = doc_start_scalar(starts_ref, q_start) // QBLOCK
    count = step - first_block + 1
    q_pos = q_start + lax.broadcasted_iota(jnp.int32, (QBLOCK, 1), 0)
    q_first = doc_start_of(starts_ref, q_pos)

    def compute(blocks):
        width = blocks * QBLOCK
        k_start = pl.multiple_of(first_block * QBLOCK, QBLOCK)
        keys = key_ref[pl.ds(k_start, width), :]
        values = value_ref[pl.ds(k_start, width), :]
        k_pos = k_start + lax.broadcasted_iota(jnp.int32, (QBLOCK, width), 1)
        allowed = (k_pos >= q_first) & (k_pos <= q_pos)
        parts = []
        for head in range(2):
            picked = jnp.where(lane_mask(QBLOCK, head), queries, jnp.zeros_like(queries))
            scores = lax.dot_general(picked, keys, CONTRACT_COLS, preferred_element_type=jnp.float32)
            scores = jnp.where(allowed, scores, NEG)
            terms = jnp.exp(scores - jnp.max(scores, axis=1, keepdims=True))
            inverse = 1.0 / jnp.sum(terms, axis=1, keepdims=True)
            mixed = jnp.dot(
                (terms * inverse).astype(jnp.bfloat16), values, preferred_element_type=jnp.float32
            )
            parts.append(mixed)
        result = jnp.where(lane_mask(QBLOCK, 0), parts[0], parts[1]).astype(jnp.bfloat16)
        out_ref[pl.ds(row_a, HALF), :] = result[:HALF]
        out_ref[pl.ds(row_b, HALF), :] = result[HALF:]

    for blocks in range(1, MAX_KEY_BLOCKS + 1):
        pl.when(count == blocks)(functools.partial(compute, blocks))


def self_backward_kernel(
    starts_ref,
    own_ref,
    qkv_ref,
    grad_ref,
    slot_ref,
    key_ref,
    value_ref,
    dkey_ref,
    dvalue_ref,
):
    step = pl.program_id(0)
    own = own_ref[0]
    pos_blocks = qkv_ref.shape[0] // HALF

    @pl.when(step == 0)
    def _():
        to_positions(own, qkv_ref, PAIR, key_ref)
        to_positions(own, qkv_ref, 2 * PAIR, value_ref)
        dkey_ref[...] = jnp.zeros_like(dkey_ref)
        dvalue_ref[...] = jnp.zeros_like(dvalue_ref)

    row_a = half_row(2 * step, pos_blocks)
    row_b = half_row(2 * step + 1, pos_blocks)
    slot_a, slot_b = slot_row(row_a, own), slot_row(row_b, own)
    queries = jnp.concatenate(
        [qkv_ref[pl.ds(slot_a, HALF), pl.ds(0, PAIR)], qkv_ref[pl.ds(slot_b, HALF), pl.ds(0, PAIR)]],
        axis=0,
    )
    grads = jnp.concatenate([grad_ref[pl.ds(row_a, HALF), :], grad_ref[pl.ds(row_b, HALF), :]], axis=0)
    q_start = step * QBLOCK
    first_block = doc_start_scalar(starts_ref, q_start) // QBLOCK
    count = step - first_block + 1
    q_pos = q_start + lax.broadcasted_iota(jnp.int32, (1, QBLOCK), 1)
    q_first = doc_start_of(starts_ref, q_pos)

    def compute(blocks):
        width = blocks * QBLOCK
        k_start = pl.multiple_of(first_block * QBLOCK, QBLOCK)
        keys = key_ref[pl.ds(k_start, width), :]
        values = value_ref[pl.ds(k_start, width), :]
        k_pos = k_start + lax.broadcasted_iota(jnp.int32, (width, QBLOCK), 0)
        allowed = (k_pos >= q_first) & (k_pos <= q_pos)
        dq_parts = []
        dkey = jnp.zeros((width, PAIR), jnp.float32)
        dvalue = jnp.zeros((width, PAIR), jnp.float32)
        for head in range(2):
            inside = lane_mask(QBLOCK, head)
            picked = jnp.where(inside, queries, jnp.zeros_like(queries))
            grad = jnp.where(inside, grads, jnp.zeros_like(grads))
            scores = lax.dot_general(keys, picked, CONTRACT_COLS, preferred_element_type=jnp.float32)
            scores = jnp.where(allowed, scores, NEG)
            terms = jnp.exp(scores - jnp.max(scores, axis=0, keepdims=True))
            probs = terms * (1.0 / jnp.sum(terms, axis=0, keepdims=True))
            dprobs = lax.dot_general(
                values, grad, CONTRACT_COLS, preferred_element_type=jnp.float32
            )
            delta = jnp.sum(probs * dprobs, axis=0, keepdims=True)
            dscores = (probs * (dprobs - delta)).astype(jnp.bfloat16)
            dq_parts.append(
                lax.dot_general(dscores, keys, CONTRACT_ROWS, preferred_element_type=jnp.float32)
            )
            dkey = dkey + jnp.dot(dscores, picked, preferred_element_type=jnp.float32)
            dvalue = dvalue + jnp.dot(
                probs.astype(jnp.bfloat16), grad, preferred_element_type=jnp.float32
            )
        dkey_ref[pl.ds(k_start, width), :] += dkey
        dvalue_ref[pl.ds(k_start, width), :] += dvalue
        dq = jnp.where(lane_mask(QBLOCK, 0), dq_parts[0], dq_parts[1])
        dq = (dq * (1.0 / math.sqrt(HEAD_DIM))).astype(jnp.bfloat16)
        slot_ref[pl.ds(slot_a, HALF), pl.ds(0, PAIR)] = dq[:HALF]
        slot_ref[pl.ds(slot_b, HALF), pl.ds(0, PAIR)] = dq[HALF:]

    for blocks in range(1, MAX_KEY_BLOCKS + 1):
        pl.when(count == blocks)(functools.partial(compute, blocks))

    @pl.when(step == pl.num_programs(0) - 1)
    def _():
        def move(block, carry):
            slot = slot_row(half_row(block, pos_blocks), own)
            place = pl.ds(pl.multiple_of(block * HALF, HALF), HALF)
            dkey = dkey_ref[place, :].astype(jnp.bfloat16)
            dvalue = dvalue_ref[place, :].astype(jnp.bfloat16)
            slot_ref[pl.ds(slot, HALF), pl.ds(PAIR, PAIR)] = dkey
            slot_ref[pl.ds(slot, HALF), pl.ds(2 * PAIR, PAIR)] = dvalue
            return carry

        lax.fori_loop(0, pos_blocks, move, 0)


def cross_forward_kernel(q_ref, key_ref, value_ref, low_ref, high_ref, out_ref, bar_ref):
    rows, width = q_ref.shape[0], key_ref.shape[1]
    queries, keys, values = q_ref[...], key_ref[0], value_ref[0]

    @pl.when(pl.program_id(0) == 0)
    def _():
        k_pos = lax.broadcasted_iota(jnp.int32, (rows, width), 1)
        allowed = (k_pos >= low_ref[...]) & (k_pos < high_ref[...])
        bar_ref[...] = jnp.where(allowed, 0.0, NEG)

    parts = []
    for head in range(2):
        picked = jnp.where(lane_mask(rows, head), queries, jnp.zeros_like(queries))
        scores = lax.dot_general(picked, keys, CONTRACT_COLS, preferred_element_type=jnp.float32)
        scores = scores + bar_ref[...]
        terms = jnp.exp(scores - jnp.max(scores, axis=1, keepdims=True))
        inverse = 1.0 / jnp.sum(terms, axis=1, keepdims=True)
        parts.append(
            jnp.dot((terms * inverse).astype(jnp.bfloat16), values, preferred_element_type=jnp.float32)
        )
    out_ref[...] = jnp.where(lane_mask(rows, 0), parts[0], parts[1]).astype(jnp.bfloat16)


def cross_backward_kernel(q_ref, key_ref, value_ref, grad_ref, low_ref, high_ref, dq_ref, dkv_ref, bar_ref):
    rows, width = q_ref.shape[0], key_ref.shape[1]
    queries, keys, values, grads = q_ref[...], key_ref[0], value_ref[0], grad_ref[...]

    @pl.when(pl.program_id(0) == 0)
    def _():
        k_pos = lax.broadcasted_iota(jnp.int32, (width, rows), 0)
        allowed = (k_pos >= low_ref[...]) & (k_pos < high_ref[...])
        bar_ref[...] = jnp.where(allowed, 0.0, NEG)

    dq_parts = []
    dkey = jnp.zeros((width, PAIR), jnp.float32)
    dvalue = jnp.zeros((width, PAIR), jnp.float32)
    for head in range(2):
        inside = lane_mask(rows, head)
        picked = jnp.where(inside, queries, jnp.zeros_like(queries))
        grad = jnp.where(inside, grads, jnp.zeros_like(grads))
        scores = lax.dot_general(keys, picked, CONTRACT_COLS, preferred_element_type=jnp.float32)
        scores = scores + bar_ref[...]
        terms = jnp.exp(scores - jnp.max(scores, axis=0, keepdims=True))
        probs = terms * (1.0 / jnp.sum(terms, axis=0, keepdims=True))
        dprobs = lax.dot_general(values, grad, CONTRACT_COLS, preferred_element_type=jnp.float32)
        delta = jnp.sum(probs * dprobs, axis=0, keepdims=True)
        dscores = (probs * (dprobs - delta)).astype(jnp.bfloat16)
        dq_parts.append(
            lax.dot_general(dscores, keys, CONTRACT_ROWS, preferred_element_type=jnp.float32)
        )
        dkey = dkey + jnp.dot(dscores, picked, preferred_element_type=jnp.float32)
        dvalue = dvalue + jnp.dot(
            probs.astype(jnp.bfloat16), grad, preferred_element_type=jnp.float32
        )
    dq = jnp.where(lane_mask(rows, 0), dq_parts[0], dq_parts[1])
    dq_ref[...] = (dq * (1.0 / math.sqrt(HEAD_DIM))).astype(jnp.bfloat16)
    dkv_ref[0, 0] = dkey.astype(jnp.bfloat16)
    dkv_ref[1, 0] = dvalue.astype(jnp.bfloat16)


def kernel_params():
    return pltpu.CompilerParams(vmem_limit_bytes=48 * 1024 * 1024)


def self_forward(doc_starts, own, qkv):
    rows = qkv.shape[0]
    return pl.pallas_call(
        self_forward_kernel,
        grid=(rows // QBLOCK,),
        in_specs=[
            pl.BlockSpec(memory_space=pltpu.SMEM),
            pl.BlockSpec(memory_space=pltpu.SMEM),
            pl.BlockSpec((rows, 3 * PAIR), lambda step: (0, 0)),
        ],
        out_specs=pl.BlockSpec((rows, PAIR), lambda step: (0, 0)),
        out_shape=jax.ShapeDtypeStruct((rows, PAIR), jnp.bfloat16),
        scratch_shapes=[pltpu.VMEM((rows, PAIR), jnp.bfloat16)] * 2,
        compiler_params=kernel_params(),
        cost_estimate=kernel_cost(1),
    )(doc_starts, own, qkv)


def self_backward(doc_starts, own, qkv, grads):
    rows = qkv.shape[0]
    return pl.pallas_call(
        self_backward_kernel,
        grid=(rows // QBLOCK,),
        in_specs=[
            pl.BlockSpec(memory_space=pltpu.SMEM),
            pl.BlockSpec(memory_space=pltpu.SMEM),
            pl.BlockSpec((rows, 3 * PAIR), lambda step: (0, 0)),
            pl.BlockSpec((rows, PAIR), lambda step: (0, 0)),
        ],
        out_specs=pl.BlockSpec((rows, 3 * PAIR), lambda step: (0, 0)),
        out_shape=jax.ShapeDtypeStruct((rows, 3 * PAIR), jnp.bfloat16),
        scratch_shapes=[pltpu.VMEM((rows, PAIR), jnp.bfloat16)] * 2
        + [pltpu.VMEM((rows, PAIR), jnp.float32)] * 2,
        compiler_params=kernel_params(),
        cost_estimate=kernel_cost(1),
    )(doc_starts, own, qkv, grads)


def cross_forward(queries, kv_cross, span_low, span_high):
    rows, features = queries.shape
    pairs = features // PAIR
    src = kv_cross.shape[1]
    return pl.pallas_call(
        cross_forward_kernel,
        grid=(pairs,),
        in_specs=[
            pl.BlockSpec((rows, PAIR), lambda p: (0, p)),
            pl.BlockSpec((1, src, PAIR), lambda p: (p // 2, 0, p % 2)),
            pl.BlockSpec((1, src, PAIR), lambda p: (p // 2 + pairs // 2, 0, p % 2)),
            pl.BlockSpec((rows, 1), lambda p: (0, 0)),
            pl.BlockSpec((rows, 1), lambda p: (0, 0)),
        ],
        out_specs=pl.BlockSpec((rows, PAIR), lambda p: (0, p)),
        out_shape=jax.ShapeDtypeStruct((rows, features), jnp.bfloat16),
        scratch_shapes=[pltpu.VMEM((rows, src), jnp.float32)],
        compiler_params=kernel_params(),
        cost_estimate=kernel_cost(1),
    )(queries, kv_cross, kv_cross, span_low[:, None], span_high[:, None])


def cross_backward(queries, kv_cross, grads, span_low, span_high):
    rows, features = queries.shape
    pairs = features // PAIR
    src = kv_cross.shape[1]
    return pl.pallas_call(
        cross_backward_kernel,
        grid=(pairs,),
        in_specs=[
            pl.BlockSpec((rows, PAIR), lambda p: (0, p)),
            pl.BlockSpec((1, src, PAIR), lambda p: (p // 2, 0, p % 2)),
            pl.BlockSpec((1, src, PAIR), lambda p: (p // 2 + pairs // 2, 0, p % 2)),
            pl.BlockSpec((rows, PAIR), lambda p: (0, p)),
            pl.BlockSpec((1, rows), lambda p: (0, 0)),
            pl.BlockSpec((1, rows), lambda p: (0, 0)),
        ],
        out_specs=[
            pl.BlockSpec((rows, PAIR), lambda p: (0, p)),
            pl.BlockSpec((2, 1, src, PAIR), lambda p: (0, p, 0, 0)),
        ],
        out_shape=[
            jax.ShapeDtypeStruct((rows, features), jnp.bfloat16),
            jax.ShapeDtypeStruct((2, pairs, src, PAIR), jnp.bfloat16),
        ],
        scratch_shapes=[pltpu.VMEM((src, rows), jnp.float32)],
        compiler_params=kernel_params(),
        cost_estimate=kernel_cost(1),
    )(queries, kv_cross, kv_cross, grads, span_low[None, :], span_high[None, :])


def mlp_kernel(act_ref, grad_ref, up_ref, down_ref, bias_ref, gelu_ref, pre_ref, out_ref, sum_ref):
    @pl.when(pl.program_id(0) == 0)
    def _():
        sum_ref[...] = jnp.zeros_like(sum_ref)

    act, grad = act_ref[...], grad_ref[...]
    total = jnp.zeros(out_ref.shape, jnp.float32)
    for begin in range(0, up_ref.shape[1], HIDDEN_BLOCK):
        place = pl.ds(begin, HIDDEN_BLOCK)
        pre = jnp.dot(act, up_ref[:, place], preferred_element_type=jnp.float32) + bias_ref[:, place]
        square = pre * pre
        tangent = jnp.tanh(GELU_C * (pre + GELU_A * pre * square))
        half = 0.5 * (1.0 + tangent)
        gelu_ref[:, place] = (pre * half).astype(jnp.bfloat16)
        slope = half + 0.5 * pre * (1.0 - tangent * tangent) * (
            GELU_C + (3.0 * GELU_A * GELU_C) * square
        )
        back = lax.dot_general(
            grad, down_ref[place, :], CONTRACT_COLS, preferred_element_type=jnp.float32
        )
        pre_grad = (back * slope).astype(jnp.bfloat16)
        pre_ref[:, place] = pre_grad
        sum_ref[:, place] += jnp.sum(pre_grad.astype(jnp.float32), axis=0, keepdims=True)
        total = total + lax.dot_general(
            pre_grad, up_ref[:, place], CONTRACT_COLS, preferred_element_type=jnp.float32
        )
    out_ref[...] = total.astype(jnp.bfloat16)


def mlp_forward_back(act, grad, up_own, down_own, bias_own):
    rows, features = act.shape
    hidden = up_own.shape[1]
    return pl.pallas_call(
        mlp_kernel,
        grid=(rows // ROW_BLOCK,),
        in_specs=[
            pl.BlockSpec((ROW_BLOCK, features), lambda step: (step, 0)),
            pl.BlockSpec((ROW_BLOCK, features), lambda step: (step, 0)),
            pl.BlockSpec((features, hidden), lambda step: (0, 0)),
            pl.BlockSpec((hidden, features), lambda step: (0, 0)),
            pl.BlockSpec((1, hidden), lambda step: (0, 0)),
        ],
        out_specs=[
            pl.BlockSpec((ROW_BLOCK, hidden), lambda step: (step, 0)),
            pl.BlockSpec((ROW_BLOCK, hidden), lambda step: (step, 0)),
            pl.BlockSpec((ROW_BLOCK, features), lambda step: (step, 0)),
            pl.BlockSpec((1, hidden), lambda step: (0, 0)),
        ],
        out_shape=[
            jax.ShapeDtypeStruct((rows, hidden), jnp.bfloat16),
            jax.ShapeDtypeStruct((rows, hidden), jnp.bfloat16),
            jax.ShapeDtypeStruct((rows, features), jnp.bfloat16),
            jax.ShapeDtypeStruct((1, hidden), jnp.float32),
        ],
        compiler_params=kernel_params(),
        cost_estimate=kernel_cost(1),
    )(act, grad, up_own, down_own, bias_own)


def outer_kernel(left_ref, right_ref, left_two_ref, right_two_ref, out_ref, total_ref):
    step = pl.program_id(0)
    half = pl.num_programs(0) // 2

    def add(left, right):
        total_ref[...] += lax.dot_general(
            left[...], right[...], CONTRACT_ROWS, preferred_element_type=jnp.float32
        )

    @pl.when(step == 0)
    def _():
        total_ref[...] = jnp.zeros_like(total_ref)

    pl.when(step < half)(lambda: add(left_ref, right_ref))
    pl.when(step >= half)(lambda: add(left_two_ref, right_two_ref))

    @pl.when(step == 2 * half - 1)
    def _():
        out_ref[...] = total_ref[...].astype(out_ref.dtype)


def outer_pair(left, right, left_two, right_two):
    rows, width = left.shape
    columns = right.shape[1]
    half = rows // ROW_BLOCK
    first = lambda step: (jnp.minimum(step, half - 1), 0)
    second = lambda step: (jnp.maximum(step - half, 0), 0)
    return pl.pallas_call(
        outer_kernel,
        grid=(2 * half,),
        in_specs=[
            pl.BlockSpec((ROW_BLOCK, width), first),
            pl.BlockSpec((ROW_BLOCK, columns), first),
            pl.BlockSpec((ROW_BLOCK, width), second),
            pl.BlockSpec((ROW_BLOCK, columns), second),
        ],
        out_specs=pl.BlockSpec((width, columns), lambda step: (0, 0)),
        out_shape=jax.ShapeDtypeStruct((width, columns), jnp.bfloat16),
        scratch_shapes=[pltpu.VMEM((width, columns), jnp.float32)],
        compiler_params=kernel_params(),
        cost_estimate=kernel_cost(1),
    )(left, right, left_two, right_two)


def square_grads_kernel(core_ref, *refs):
    step = pl.program_id(0)
    side, x = step // 2, step % 2
    core = jnp.where(side == 0, 1 - core_ref[0], core_ref[0])
    pairs, (send_ref, keep_ref) = refs[:-2], refs[-2:]
    n_y, n_z, _, rows, width = send_ref.shape[1:]
    begin = pl.multiple_of((2 * x + core) * rows, rows)

    def compute(out_ref):
        for which in range(len(pairs) // 2):
            grad = lax.dot_general(
                pairs[2 * which][:, pl.ds(begin, rows)],
                pairs[2 * which + 1][...],
                CONTRACT_ROWS,
                preferred_element_type=jnp.float32,
            ).astype(jnp.bfloat16)
            for y in range(n_y):
                for z in range(n_z):
                    source = (z * n_y + y) * width
                    out_ref[0, y, z, which] = grad[:, source : source + width]

    pl.when(side == 0)(lambda: compute(send_ref))
    pl.when(side == 1)(lambda: compute(keep_ref))


def square_grads(core, pairs, n_y, n_z):
    flat = [array for pair in pairs for array in pair]
    tokens, features = flat[0].shape
    rows = features // 4
    block = (1, n_y, n_z, len(pairs), rows, features // (n_y * n_z))
    shape = jax.ShapeDtypeStruct((2,) + block[1:], jnp.bfloat16)
    return pl.pallas_call(
        square_grads_kernel,
        grid=(4,),
        in_specs=[pl.BlockSpec(memory_space=pltpu.SMEM)]
        + [pl.BlockSpec((tokens, features), lambda step: (0, 0))] * len(flat),
        out_specs=[
            pl.BlockSpec(block, lambda step: (jnp.minimum(step, 1), 0, 0, 0, 0, 0)),
            pl.BlockSpec(block, lambda step: (jnp.maximum(step - 2, 0), 0, 0, 0, 0, 0)),
        ],
        out_shape=[shape, shape],
        compiler_params=kernel_params(),
        cost_estimate=kernel_cost(15),
    )(core, *flat)


tie = lax.optimization_barrier


def low(value):
    return value.astype(jnp.bfloat16)


def wide(value):
    return value.astype(jnp.float32)


def plus(left, right):
    return low(wide(left) + wide(right))


def over(axis, distance, value):
    count = lax.axis_size(axis)
    return lax.ppermute(value, axis, [(i, i ^ distance) for i in range(count)])


def over_core(value):
    return over("fc", 1, value)


def over_x(value):
    return over("fx", 1, value)


def over_y(value):
    return over("cy", 1, value)


def trade_places(value):
    n_z, n_y, n_f = lax.axis_size("cz"), lax.axis_size("cy"), lax.axis_size(FSDP)
    pairs = [
        ((z * n_y + y) * n_f + f, (f * n_y + y) * n_f + z)
        for z in range(n_z)
        for y in range(n_y)
        for f in range(n_f)
    ]
    return lax.ppermute(value, ALL, pairs)


def at(value, index, axis):
    return lax.dynamic_index_in_dim(value, index, axis, keepdims=False)


def pack_kernel(index_ref, *refs):
    begin = 0
    for ref in refs[:-1]:
        size = ref.shape[1]
        refs[-1][:, begin : begin + size] = ref[...]
        begin += size


def swap_columns(w_qkv, w_cross_kv, w_up):
    own, me_y, n_y = lax.axis_index(FSDP), lax.axis_index("cy"), lax.axis_size("cy")
    rows = w_up.shape[0]
    count = lax.axis_size(FSDP) * n_y
    owners = jnp.stack([(own ^ distance) * n_y + me_y for distance in (2, 3, 1, 0)])
    sizes = [PAIR] * 3 + [w_cross_kv.shape[1] // count, w_up.shape[1] // count]
    pieces = pl.pallas_call(
        pack_kernel,
        grid_spec=pltpu.PrefetchScalarGridSpec(
            num_scalar_prefetch=1,
            grid=(4,),
            in_specs=[
                pl.BlockSpec(
                    (rows, PAIR), lambda step, index, part=part: (0, part * count + index[step])
                )
                for part in range(3)
            ]
            + [pl.BlockSpec((rows, size), lambda step, index: (0, index[step])) for size in sizes[3:]],
            out_specs=pl.BlockSpec((rows, sum(sizes)), lambda step, index: (step, 0)),
        ),
        out_shape=jax.ShapeDtypeStruct((4 * rows, sum(sizes)), w_up.dtype),
        compiler_params=kernel_params(),
        cost_estimate=kernel_cost(1),
    )(owners.astype(jnp.int32), w_qkv, w_qkv, w_qkv, w_cross_kv, w_up)
    from_x = over_x(pieces[: 2 * rows])
    from_core = over_core(
        row_major(jnp.concatenate([pieces[2 * rows : 3 * rows], from_x[rows:]], axis=0))
    )
    return [pieces[3 * rows :], from_core[:rows], from_x[:rows], from_core[rows:]]


def rows_in_order(pieces, begin, size):
    own = lax.axis_index(FSDP)
    rows = pieces[0].shape[0]
    whole = jnp.zeros((len(pieces) * rows, size), pieces[0].dtype)
    for distance, piece in enumerate(pieces):
        whole = lax.dynamic_update_slice_in_dim(
            whole, piece[:, begin : begin + size], (own ^ distance) * rows, 0
        )
    return whole


def gather_rows(shard):
    own, me_y = lax.axis_index(FSDP), lax.axis_index("cy")
    rows, columns = shard.shape
    half = rows // 2
    from_x = over_x(lax.dynamic_slice_in_dim(shard, me_y * half, half, 0))
    from_y = over_y(from_x)
    both = jnp.concatenate(
        [shard, jnp.where(me_y == 0, from_x, from_y), jnp.where(me_y == 0, from_y, from_x)], axis=0
    )
    from_core = over_core(row_major(both))
    whole = jnp.zeros((4 * rows, columns), shard.dtype)
    for distance, piece in (
        (0, both[:rows]),
        (2, both[rows:]),
        (1, from_core[:rows]),
        (3, from_core[rows:]),
    ):
        whole = lax.dynamic_update_slice_in_dim(whole, piece, (own ^ distance) * rows, 0)
    return whole


def gather_rest(block, from_y, from_x):
    half = block.shape[0] // 2
    top = over_x(from_y[:half])
    bottom = over_y(from_x[half:])
    mine = jnp.concatenate([block, from_y, from_x, top, bottom], axis=0)
    return mine, over_core(mine)


def gather_plane(block):
    return gather_rest(block, over_y(block), over_x(block))


def scatter_plane(mine, theirs, fill=(None, None, None)):
    rows = mine.shape[0] // 4
    half = rows // 2
    done = []

    def beside(received, work):
        if work is None:
            return received
        received, result = tie((received, work()))
        done.append(result)
        return received

    total = plus(mine, beside(over_core(theirs), fill[0]))
    own, for_y, for_x, diag = (total[i * rows : (i + 1) * rows] for i in range(4))
    top, bottom = beside((over_x(diag[:half]), over_y(diag[half:])), fill[1])
    for_y = jnp.concatenate([plus(for_y[:half], top), for_y[half:]], axis=0)
    for_x = jnp.concatenate([for_x[:half], plus(for_x[half:], bottom)], axis=0)
    from_y, from_x = beside((over_y(for_y), over_x(for_x)), fill[2])
    return wide(own) + wide(from_y) + wide(from_x), done


def sum_everywhere(value, event):
    value = later(value, event)
    for step in (over_core, over_x, over_y):
        value = value + step(value)
    for distance in (1, 2):
        value = value + over("cz", distance, value)
    return value


def after(value, *events):
    return lax.optimization_barrier((value,) + events)[0]


def later(value, event):
    scalar = event[(0,) * event.ndim]
    nothing = jnp.where(scalar != scalar, scalar, jnp.zeros_like(scalar))
    return value + nothing.astype(value.dtype)


def scatter_bits(value, axes=(0, 1, 2)):
    me_f, me_y = lax.axis_index(FSDP), lax.axis_index("cy")
    me_x, me_core = me_f // 2, me_f % 2
    axis_x, axis_core, axis_y = axes
    value = plus(at(value, me_core, axis_core), over_core(at(value, 1 - me_core, axis_core)))
    axis_x -= axis_x > axis_core
    axis_y -= axis_y > axis_core
    value = plus(at(value, me_x, axis_x), over_x(at(value, 1 - me_x, axis_x)))
    axis_y -= axis_y > axis_x
    return plus(at(value, me_y, axis_y), over_y(at(value, 1 - me_y, axis_y)))


def planned_device(
    tokens,
    encoded,
    grad_out,
    doc_lengths,
    src_lengths,
    norm_gain,
    norm_bias,
    w_qkv,
    self_bias,
    w_self_out,
    w_cross_q,
    w_cross_kv,
    cross_bias,
    w_cross_out,
    w_up,
    up_bias,
    w_down,
    down_bias,
):
    q_scale = 1.0 / math.sqrt(HEAD_DIM)
    rows, features = tokens.shape[1:]
    src_own = encoded.shape[1]
    n_z, n_y, n_f = lax.axis_size("cz"), lax.axis_size("cy"), lax.axis_size(FSDP)
    n_ctx = n_z * n_y
    me_y, me_f = lax.axis_index("cy"), lax.axis_index(FSDP)
    own = me_f * n_y + me_y
    shard, hidden = w_up.shape
    slab = hidden // n_ctx
    width = features // n_ctx
    column = 2 * features // n_ctx

    moved = trade_places(jnp.concatenate([tokens[0], encoded[0]], axis=0))
    tok_low, enc_low = moved[:rows], moved[rows:]
    lengths = trade_places(jnp.concatenate([doc_lengths, src_lengths], axis=0))
    head_w = swap_columns(w_qkv, w_cross_kv, w_up)
    tok_low, enc_low, lengths = tie((tok_low, enc_low, lengths))
    qkv_own = rows_in_order(head_w, 0, 3 * PAIR)
    kv_own = rows_in_order(head_w, 3 * PAIR, column)
    up_own = rows_in_order(head_w, 3 * PAIR + column, slab)
    square = gather_rows(jnp.concatenate([w_self_out, w_cross_q, w_cross_out], axis=1))

    own_rows = own * rows + jnp.arange(rows, dtype=jnp.int32)
    tok_pos = stream_position(own_rows, rows, n_ctx)
    doc_starts = jnp.cumsum(lengths[0]) - lengths[0]
    tok_doc = doc_index(doc_starts, tok_pos)
    src_ends = jnp.cumsum(lengths[1])
    span_low = pick_doc(src_ends - lengths[1], tok_doc)
    span_high = pick_doc(src_ends, tok_doc)
    own_index = own.astype(jnp.int32)[None]

    tok_f32 = wide(tok_low)
    ln_one, normed_one, inverse_one = layer_norm(tok_f32, norm_gain[0], norm_bias[0])
    act_one = low(ln_one)
    from_y, from_x = over_y(act_one), over_x(act_one)
    enc_all = lax.all_gather(enc_low, PLANE, axis=0, tiled=True)
    act_mine, act_theirs = gather_rest(act_one, from_y, from_x)
    down_grad_low = trade_places(grad_out[0])
    grad_all = lax.all_gather(down_grad_low, PLANE, axis=0, tiled=False)
    full_self_out, full_cross_q, full_cross_out = (
        square[:, i * features : (i + 1) * features] for i in range(3)
    )

    head_bias = lax.dynamic_slice_in_dim(self_bias, own * PAIR, PAIR, 1)
    qkv_bias = jnp.concatenate([head_bias[0], jnp.zeros_like(head_bias[0]), head_bias[1]])
    qkv_factor = jnp.concatenate([jnp.full((PAIR,), q_scale), jnp.ones((2 * PAIR,))])

    def project(acts):
        return low((plain_dot(acts, qkv_own) + qkv_bias) * qkv_factor.astype(jnp.float32))

    qkv_heads = jnp.concatenate([project(act_mine), project(act_theirs)], axis=0)
    kv_bias = jnp.concatenate([jnp.zeros((features,), jnp.float32), cross_bias[1]])
    kv_columns = low(
        plain_dot(enc_all, kv_own) + lax.dynamic_slice_in_dim(kv_bias, own * column, column, 0)
    )
    kv_cross = lax.all_gather(after(kv_columns, grad_all), PLANE, axis=0, tiled=False)
    down_own = lax.dynamic_slice_in_dim(w_down, me_y * slab, slab, 0)
    att_heads = self_forward(doc_starts, own_index, qkv_heads)
    att_heads, down_own, up_own = tie((att_heads, down_own, up_own))
    att_self = lax.all_to_all(att_heads, PLANE, 0, 1, tiled=True)
    order = (0, 1, 4, 5, 2, 3, 6, 7)
    grad_mine = jnp.concatenate([at(grad_all, own ^ k, 0) for k in order[:4]], axis=0)
    grad_theirs = jnp.concatenate([at(grad_all, own ^ k, 0) for k in order[4:]], axis=0)

    hidden_one = tok_f32 + plain_dot(att_self, full_self_out) + self_bias[2]
    ln_two, normed_two, inverse_two = layer_norm(hidden_one, norm_gain[1], norm_bias[1])
    act_two = low(ln_two)
    q_cross = low((plain_dot(act_two, full_cross_q) + cross_bias[0]) * q_scale)
    att_cross = cross_forward(q_cross, kv_cross, span_low, span_high)
    hidden_two = hidden_one + plain_dot(att_cross, full_cross_out) + cross_bias[2]

    ln_three, normed_three, inverse_three = layer_norm(hidden_two, norm_gain[2], norm_bias[2])
    three_mine, three_theirs = gather_plane(low(ln_three))
    bias_own = lax.dynamic_slice_in_dim(up_bias, own * slab, slab, 0).reshape(1, -1)
    gelu_theirs, pre_theirs, part_theirs, sum_theirs = mlp_forward_back(
        three_theirs, grad_theirs, up_own, down_own, bias_own
    )
    gelu_mine, pre_mine, part_mine, sum_mine = mlp_forward_back(
        three_mine, grad_mine, up_own, down_own, bias_own
    )

    part_mine, three_mine, three_theirs, grad_mine, grad_theirs, act_mine, act_theirs = tie(
        (part_mine, three_mine, three_theirs, grad_mine, grad_theirs, act_mine, act_theirs)
    )
    act_grad, (up_grad, down_grad, out_sent) = scatter_plane(
        part_mine,
        part_theirs,
        (
            lambda: outer_pair(three_mine, pre_mine, three_theirs, pre_theirs),
            lambda: outer_pair(grad_mine, gelu_mine, grad_theirs, gelu_theirs),
            lambda: low(plain_dot(gelu_theirs, down_own)),
        ),
    )
    up_grad = lax.psum_scatter(up_grad, "cz", scatter_dimension=0, tiled=True)
    down_grad = lax.psum_scatter(down_grad, "cz", scatter_dimension=0, tiled=True)
    out_mine = low(plain_dot(gelu_mine, down_own))

    upstream = wide(down_grad_low)
    grad_down_bias = jnp.sum(upstream, axis=0)
    norm_in_three, gain_grad_three, shift_grad_three = norm_back(
        act_grad, normed_three, inverse_three, norm_gain[2]
    )
    grad_two = upstream + norm_in_three
    cross_grad_low = low(grad_two)
    cross_out_bias_grad = jnp.sum(wide(cross_grad_low), axis=0)
    cross_att_grad = low(times_transpose(cross_grad_low, full_cross_out))
    cross_v_bias_grad = jnp.sum(wide(cross_att_grad), axis=0)

    up_bias_grad = (sum_mine + sum_theirs)[0]

    me_x, me_core = me_f // 2, me_f % 2
    cross_q_low, cross_kv_part = cross_backward(
        q_cross, kv_cross, cross_att_grad, span_low, span_high
    )
    cross_q_bias_grad = jnp.sum(wide(cross_q_low), axis=0)
    norm_in_two, gain_grad_two, shift_grad_two = norm_back(
        times_transpose(cross_q_low, full_cross_q), normed_two, inverse_two, norm_gain[1]
    )
    grad_one = grad_two + norm_in_two
    self_grad_low = low(grad_one)
    self_att_grad = low(times_transpose(self_grad_low, full_self_out))
    self_v_bias_grad = jnp.sum(wide(self_att_grad), axis=0)
    kv_part = cross_kv_part.reshape(2, 2, 2, 2, enc_all.shape[0], PAIR)
    kv_other = over_core(at(kv_part, 1 - me_core, 1))
    self_att_grad, up_grad, kv_other = tie((self_att_grad, up_grad, kv_other))
    att_grad_heads = lax.all_to_all(self_att_grad, PLANE, 1, 0, tiled=True)
    kv_part = plus(at(kv_part, me_core, 1), kv_other)
    kv_other = over_x(at(kv_part, 1 - me_x, 0))

    send, keep = square_grads(
        me_core.astype(jnp.int32)[None],
        (
            (att_self, after(self_grad_low, self_att_grad)),
            (act_two, cross_q_low),
            (att_cross, cross_grad_low),
        ),
        n_y,
        n_z,
    )
    self_out_bias_grad = jnp.sum(wide(self_grad_low), axis=0)
    three = plus(keep, row_major(over_core(send)))
    out_sum = plus(out_mine, over_core(after(out_sent, self_att_grad)))
    att_grad_heads, kv_other, three, out_sum = tie((att_grad_heads, kv_other, three, out_sum))
    kv_part = plus(at(kv_part, me_x, 0), kv_other)
    kv_other = over_y(at(kv_part, 1 - me_y, 0))
    left, right = three[:, :, : n_z // 2], three[:, :, n_z // 2 :]
    left_other = over_x(at(left, 1 - me_x, 0))
    right_other = over_y(at(right, 1 - me_y, 1))
    out_own, out_y, out_x, out_diag = (out_sum[i * rows : (i + 1) * rows] for i in range(4))
    half_rows = rows // 2
    out_top, out_bottom = over_x(out_diag[:half_rows]), over_y(out_diag[half_rows:])

    proj_grad = self_backward(doc_starts, own_index, qkv_heads, att_grad_heads)
    half = proj_grad.shape[0] // 2

    def lane_blocks(value):
        return [
            value[:, i : i + PAIR].reshape(n_z, 1, shard, PAIR)
            for i in range(0, value.shape[1], PAIR)
        ]

    def project_back():
        weight = outer_rows(act_mine, proj_grad[:half]) + outer_rows(act_theirs, proj_grad[half:])
        sums = jnp.sum(wide(proj_grad), axis=0)[None]
        shift = jnp.sum(wide(qkv_own) * sums, axis=1)
        gain = jnp.sum(wide(qkv_own) * weight, axis=1) - norm_bias[0] * shift
        return row_major(low(weight)), sums[0], gain / norm_gain[0], shift

    act_grad, ((qkv_grad, proj_sums, gain_grad_one, shift_grad_one),) = scatter_plane(
        low(times_transpose(proj_grad[:half], qkv_own)),
        low(times_transpose(proj_grad[half:], qkv_own)),
        (project_back, None, None),
    )
    down_cols = later(down_grad, act_grad).reshape(n_y, width, slab)
    other = over_y(at(down_cols, 1 - me_y, 0))
    mine = at(down_cols, me_y, 0)

    left = later(plus(at(left, me_x, 0), left_other), act_grad)
    right = later(plus(at(right, me_y, 1), right_other), act_grad)
    left, left_send = at(left, me_y, 0), at(left, 1 - me_y, 0)
    right, right_send = at(right, me_x, 0), at(right, 1 - me_x, 0)
    out_y = jnp.concatenate([plus(out_y[:half_rows], out_top), out_y[half_rows:]], axis=0)
    out_x = jnp.concatenate([out_x[:half_rows], plus(out_x[half_rows:], out_bottom)], axis=0)
    out_y, out_x = later(out_y, act_grad), later(out_x, act_grad)
    mlp_out = wide(out_own) + wide(over_y(out_y)) + wide(over_x(out_x))
    layer_out = trade_places(low(hidden_two + mlp_out + down_bias))
    self_q_bias_grad = proj_sums[:PAIR]
    cross_kv_grad = plus(at(kv_part, me_y, 0), kv_other)
    cross_kv_grad = jnp.concatenate([cross_kv_grad[0], cross_kv_grad[1]], axis=1)
    grad_encoded = wide(
        trade_places(
            scatter_bits(
                after(low(times_transpose(cross_kv_grad, kv_own)), act_grad).reshape(
                    2, 2, 2, src_own, features
                )
            )
        )
    )
    cross_kv_grad = low(outer_rows(enc_all, cross_kv_grad))
    rest = jnp.concatenate(lane_blocks(cross_kv_grad) + lane_blocks(qkv_grad), axis=1)
    rest = lax.psum_scatter(row_major(rest), "cz", scatter_dimension=0, tiled=False)
    three = jnp.concatenate(
        [
            later(plus(left, over_y(left_send)), rest),
            later(plus(right, over_x(right_send)), rest),
        ],
        axis=0,
    )
    three = wide(lax.psum_scatter(row_major(three), "cz", scatter_dimension=0, tiled=False))
    kv_blocks = trade_places(rest[:2])
    grad_w_cross_kv = wide(jnp.concatenate([kv_blocks[0], kv_blocks[1]], axis=1))
    qkv_grad = rest[2:]

    norm_in_one, _, _ = norm_back(act_grad, normed_one, inverse_one, norm_gain[0])
    grad_tokens = low(grad_one + norm_in_one)
    grad_w_up = wide(trade_places(later(up_grad, proj_grad)))
    grad_tokens = wide(trade_places(grad_tokens))

    down_halves = jnp.stack([jnp.where(me_y == 0, mine, other), jnp.where(me_y == 0, other, mine)])
    grad_w_down = wide(jnp.transpose(down_halves, (0, 2, 1)).reshape(n_y * slab, width))

    qkv_blocks = []
    inverse_of_three = pow(3, -1, n_ctx)
    for slot in range(3):
        pairs = []
        for dest in range(n_ctx):
            source = (3 * dest + slot) % n_ctx
            for z in range(n_z):
                pairs.append(
                    ((z * n_y + source % n_y) * n_f + source // n_y, dest * n_f + z)
                )
        part = (3 * ((inverse_of_three * (own - slot)) % n_ctx) + slot) // n_ctx
        qkv_blocks.append(lax.ppermute(at(qkv_grad, part, 0), ALL, pairs))
    grad_w_qkv = wide(jnp.concatenate(qkv_blocks, axis=1))

    def placed(part):
        whole = jnp.zeros((n_ctx * part.shape[0],), jnp.float32)
        return lax.dynamic_update_slice_in_dim(whole, part, own * part.shape[0], 0).reshape(
            -1, features
        )

    level = jnp.stack(
        [
            gain_grad_one,
            gain_grad_two,
            gain_grad_three,
            shift_grad_one,
            shift_grad_two,
            shift_grad_three,
            self_v_bias_grad,
            self_out_bias_grad,
            cross_q_bias_grad,
            cross_v_bias_grad,
            cross_out_bias_grad,
            grad_down_bias,
        ]
    )
    level = sum_everywhere(
        jnp.concatenate([level, placed(self_q_bias_grad), placed(up_bias_grad)], axis=0), act_grad
    )
    grad_up_bias = level[13:].reshape(hidden)

    return (
        layer_out[None],
        grad_tokens[None],
        grad_encoded[None],
        level[0:3],
        level[3:6],
        grad_w_qkv,
        jnp.concatenate([level[12:13], level[6:8]], axis=0),
        three[0],
        three[1],
        grad_w_cross_kv,
        level[8:11],
        three[2],
        grad_w_up,
        grad_up_bias,
        grad_w_down,
        level[11],
    )


def planned_solution(mesh):
    n_ctx, n_f = mesh.shape["ctx"], mesh.shape["fsdp"]
    split = Mesh(mesh.devices.reshape(n_ctx // 2, 2, n_f // 2, 2), ALL)
    token = P(FSDP, CTX, None)
    row = P(FSDP, None)
    owned = P(FSDP, CTX)
    return jax.shard_map(
        planned_device,
        mesh=split,
        in_specs=(token, token, token, row, row, P(), P(), row, P(), row, row, row, P(), row)
        + (row, P(), row, P()),
        out_specs=(token, token, token, P(), P(), owned, P(), owned, owned, owned, P(), owned)
        + (owned, P(), owned, P()),
        check_vma=False,
    )


def solution(mesh):
    if mesh.shape["ctx"] * 2 == HEADS and mesh.shape["fsdp"] * 2 == mesh.shape["ctx"]:
        return planned_solution(mesh)
    return general_solution(mesh)
```
